256 devices in a mesh: pts: 16 (over z, core), bas: 16 (over x, y).
Axes of the slice: x: 4, y: 4, z: 8, core: 2. Of those that a mesh axis runs over, the one named last changes fastest.
Arguments:
- orbitals: float32 [61440, 8192], P('bas', 'pts'), may hold values from -1 to 1
- owner_perm: int32 [16], replicated, may hold values from 0 to 15, each once
- pair_reach: int32 [16], replicated, may hold values from 0 to 2
Outputs:
- metric: float32 [16, 4, 512, 512], P('pts', None, 'bas')
The draws below stay inside these ranges and needn't reach their ends.
Inputs may be any that keep to these rules, and one draw needn't show every extreme that they name: The metric rows of block b belong to owner owner_perm[b % 16], as its row group b // 16. Block b is paired with the existing blocks among b + 1 to b + pair_reach[b].
All inputs are finite; a program needn't handle non-finite values.
Results may differ from the reference program's by a relative error of at most 0.000092.
Values sent between devices are 32-bit elements; how exact they have to be, the bound alone decides.
No kernel may reach another device: no remote copies, remote signals or barrier semaphores. Data moves between devices by JAX's collectives and lax.ppermute only.
A program may use at most 128 MiB of HBM per device.

```python
import jax
import jax.numpy as jnp
from jax import lax

NBASIS = 61440
PB = 512
BLK_DEV = 1
REACH = 2
NBLK = 16
NPOINTS = 8192
N_PTS = 16


def with_ends(drawn, own_key, least, top_value):
    spot = [jax.random.randint(jax.random.fold_in(own_key, axis), (), 0, length) for axis, length in enumerate(drawn.shape)]
    longest = drawn.shape.index(max(drawn.shape))
    beside = spot[:longest] + [(spot[longest] + 1) % drawn.shape[longest]] + spot[longest + 1:]
    return drawn.at[tuple(spot)].set(least).at[tuple(beside)].set(top_value)


def steps_of(rng, dims, cuts, low, top_value):
    def one(dim, parts):
        draws = jax.random.uniform(jax.random.fold_in(jax.random.fold_in(rng, 6), dim), (parts,), jnp.float32, low / len(cuts), top_value / len(cuts))
        return jnp.repeat(jnp.exp(draws), dims[dim] // parts).reshape((-1,) + (1,) * (len(dims) - dim - 1))

    loudness = one(*cuts[0])
    for cut in cuts[1:]:
        loudness = loudness * one(*cut)
    return loudness


def gaussian(rng, dims, deviation, bound, cuts=(), kind=jnp.bfloat16):
    gain = steps_of(rng, dims, cuts, -0.22, 0.18) if cuts else 1.0
    values = jax.random.normal(rng, dims, jnp.float32) * deviation * gain
    return jnp.minimum(jnp.maximum(values, -bound), bound).astype(kind)


def setup_inputs(seed: int = 0) -> dict:
    key_list = jax.random.split(jax.random.key(seed), 4)
    orbitals = gaussian(key_list[0], (NBASIS, NPOINTS), (NBASIS ** -0.25), 1.0, ((0, 16), (1, 16)), jnp.float32)
    owner_perm = jax.random.permutation(key_list[1], N_PTS).astype(jnp.int32)
    pair_reach = with_ends(jax.random.randint(key_list[2], (NBLK,), 0, REACH + 1), jax.random.fold_in(key_list[2], 1), 0, REACH).astype(jnp.int32)
    return dict(orbitals=orbitals, owner_perm=owner_perm, pair_reach=pair_reach)


def pair_tile(orbitals, first_block, second_block):
    left_cols = lax.dynamic_slice_in_dim(orbitals, first_block * PB, PB, 1)
    right_cols = lax.dynamic_slice_in_dim(orbitals, second_block * PB, PB, 1)
    product = lax.dot_general(left_cols, right_cols, (((0,), (0,)), ((), ())), precision=lax.Precision.HIGHEST, preferred_element_type=jnp.float32)
    return product * product


def reference(orbitals, owner_perm, pair_reach):
    starts = jnp.arange(NBLK, dtype=jnp.int32)
    offsets = jnp.arange(REACH, dtype=jnp.int32)
    firsts = jnp.repeat(starts, REACH)
    step_offsets = jnp.tile(offsets, NBLK)
    seconds = firsts + step_offsets + 1
    living = (step_offsets < pair_reach[firsts]) & (seconds < NBLK)
    clipped = jnp.minimum(seconds, NBLK - 1).astype(jnp.int32)

    def make_tile(pair_item):
        first_block, second_block, is_alive = pair_item
        squared = pair_tile(orbitals, first_block, second_block)
        return jnp.where(is_alive, squared, jnp.zeros_like(squared))

    pair_tiles = lax.map(make_tile, (firsts, clipped, living)).reshape(NBLK, REACH, PB, PB)
    back_rows = starts[:, None] - offsets[None, :] - 1
    back_valid = back_rows >= 0
    mirrored = pair_tiles[jnp.maximum(back_rows, 0), jnp.broadcast_to(offsets[None, :], back_rows.shape)]
    mirrored = jnp.swapaxes(mirrored, 2, 3)
    mirrored = jnp.where(back_valid[:, :, None, None], mirrored, jnp.zeros_like(mirrored))
    stacked_rows = jnp.concatenate([pair_tiles, mirrored], axis=1)
    position = jnp.zeros((N_PTS,), jnp.int32).at[owner_perm].set(jnp.arange(N_PTS, dtype=jnp.int32))
    row_index = jnp.arange(NBLK, dtype=jnp.int32)
    owners = row_index // BLK_DEV
    groups = row_index % BLK_DEV
    row_blocks = groups * N_PTS + position[owners]
    return stacked_rows[row_blocks]
```

```python
import functools

import jax
import jax.numpy as jnp
from jax import lax
from jax.experimental import pallas as pl
from jax.experimental.pallas import tpu as pltpu
from jax.sharding import PartitionSpec as P

PB = 512
SHARE = 32
LANES = 128
SUB = 8
CHUNKS = PB // LANES
GROUP = LANES // SUB
PTS = 16
VMEM = 40 * 1024 * 1024
F32 = jnp.float32
BF16 = jnp.bfloat16
NT = (((1,), (1,)), ((), ()))
NN = (((1,), (0,)), ((), ()))


def dot(a, b, dims):
    return lax.dot_general(a, b, dims, preferred_element_type=F32)


def natural_of(index, chunk0):
    chunk = chunk0 + index // LANES
    within = index % LANES
    return SHARE * (within // SUB) + SUB * chunk + within % SUB


def split3(x):
    hi = x.astype(BF16)
    rest = x - hi.astype(F32)
    mid = rest.astype(BF16)
    lo = (rest - mid.astype(F32)).astype(BF16)
    return hi, mid, lo


def split2(x):
    hi = x.astype(BF16)
    return hi, (x - hi.astype(F32)).astype(BF16)


def row_block(depth):
    for size in (768, 640, 512, 384, 256, 128):
        if depth % size == 0:
            return size
    return depth


def chunk_kernel(chunk0, count, x_ref, *rest):
    out_refs, pick_ref = rest[:count], rest[count]

    @pl.when(pl.program_id(0) == 0)
    def _():
        rows = lax.broadcasted_iota(jnp.int32, pick_ref.shape, 0)
        cols = lax.broadcasted_iota(jnp.int32, pick_ref.shape, 1)
        pick_ref[...] = (rows == natural_of(cols, chunk0)).astype(F32).astype(BF16)

    hi, mid, lo = split3(x_ref[...])
    pick = pick_ref[...]
    moved = dot(hi, pick, NN) + dot(mid, pick, NN) + dot(lo, pick, NN)
    for n in range(count):
        out_refs[n][...] = moved[:, n * LANES:(n + 1) * LANES]


def chunks_of(x, chunk0, count):
    depth = x.shape[0]
    rows = row_block(depth)
    return pl.pallas_call(
        functools.partial(chunk_kernel, chunk0, count),
        grid=(depth // rows,),
        in_specs=[pl.BlockSpec((rows, PB), lambda k: (k, 0))],
        out_specs=[pl.BlockSpec((rows, LANES), lambda k: (k, 0))] * count,
        out_shape=[jax.ShapeDtypeStruct((depth, LANES), F32)] * count,
        scratch_shapes=[pltpu.VMEM((PB, count * LANES), BF16)],
        compiler_params=pltpu.CompilerParams(vmem_limit_bytes=VMEM),
        cost_estimate=pl.CostEstimate(
            flops=6 * depth * PB * LANES * count, bytes_accessed=4 * depth * (PB + LANES * count), transcendentals=0
        ),
        name="chunks",
    )(x)


def turn_kernel(x_ref, hi_ref, lo_ref, pick_ref):
    @pl.when(pl.program_id(0) == 0)
    def _():
        rows = lax.broadcasted_iota(jnp.int32, pick_ref.shape, 0)
        cols = lax.broadcasted_iota(jnp.int32, pick_ref.shape, 1)
        pick_ref[...] = (cols == natural_of(rows, 0)).astype(F32).astype(BF16)

    hi, lo = split2(x_ref[...])
    hi_ref[...] = dot(pick_ref[...], hi, NT).astype(BF16)
    lo_ref[...] = dot(pick_ref[...], lo, NT).astype(BF16)


def turned(x):
    depth = x.shape[0]
    rows = row_block(depth)
    return pl.pallas_call(
        turn_kernel,
        grid=(depth // rows,),
        in_specs=[pl.BlockSpec((rows, PB), lambda k: (k, 0))],
        out_specs=[pl.BlockSpec((PB, rows), lambda k: (0, k))] * 2,
        out_shape=[jax.ShapeDtypeStruct((PB, depth), BF16)] * 2,
        scratch_shapes=[pltpu.VMEM((PB, PB), BF16)],
        compiler_params=pltpu.CompilerParams(vmem_limit_bytes=VMEM),
        cost_estimate=pl.CostEstimate(flops=4 * depth * PB * PB, bytes_accessed=8 * depth * PB, transcendentals=0),
        name="turned",
    )(x)


def put(out_ref, unit, block):
    out_ref[:, unit] = block.reshape(GROUP, SUB, LANES)


def local_kernel(mhi_ref, mlo_ref, ohi_ref, olo_ref, out_ref, acc_ref):
    step = pl.program_id(0)

    @pl.when(step == 0)
    def _():
        acc_ref[...] = jnp.zeros_like(acc_ref)

    mhi, ohi = mhi_ref[...], ohi_ref[...]
    acc_ref[...] += dot(mhi, ohi, NT) + dot(mhi, olo_ref[...], NT) + dot(mlo_ref[...], ohi, NT)

    @pl.when(step == pl.num_programs(0) - 1)
    def _():
        for e in range(CHUNKS):
            for c in range(CHUNKS):
                put(out_ref, CHUNKS * e + c, acc_ref[e * LANES:(e + 1) * LANES, c * LANES:(c + 1) * LANES])


def local_units(mhi, mlo, ohi, olo):
    depth = mhi.shape[1]
    rows = row_block(depth)
    units = CHUNKS * CHUNKS
    return pl.pallas_call(
        local_kernel,
        grid=(depth // rows,),
        in_specs=[pl.BlockSpec((PB, rows), lambda k: (0, k))] * 4,
        out_specs=pl.BlockSpec((GROUP, units, SUB, LANES), lambda k: (0, 0, 0, 0)),
        out_shape=jax.ShapeDtypeStruct((GROUP, units, SUB, LANES), F32),
        scratch_shapes=[pltpu.VMEM((PB, PB), F32)],
        compiler_params=pltpu.CompilerParams(vmem_limit_bytes=VMEM),
        cost_estimate=pl.CostEstimate(flops=6 * depth * PB * PB, bytes_accessed=8 * depth * PB, transcendentals=0),
        name="local_units",
    )(mhi, mlo, ohi, olo)


def step_units(c):
    units = [("am", e, c, 0) for e in range(CHUNKS)]
    units += [("ar", c, e, 2) for e in range(CHUNKS)]
    units += [("b", e, c, 1) for e in range(c, CHUNKS)]
    units += [("b", c, e, 2) for e in range(c + 1, CHUNKS)]
    return units


def step_kernel(c, o_base, mhi_ref, mlo_ref, ohi_ref, olo_ref, r_ref, out_ref, wide_ref, slim_ref):
    step = pl.program_id(0)

    @pl.when(step == 0)
    def _():
        wide_ref[...] = jnp.zeros_like(wide_ref)
        slim_ref[...] = jnp.zeros_like(slim_ref)

    rhi, rlo = split2(r_ref[...])
    both = jnp.concatenate([rhi, rlo], axis=1)
    skip = c * LANES - o_base
    wide_ref[:PB] += dot(mhi_ref[...], both, NN)
    slim_ref[:PB] += dot(mlo_ref[...], rhi, NN)
    wide_ref[PB:] += dot(ohi_ref[skip:], both, NN)
    slim_ref[PB:] += dot(olo_ref[skip:], rhi, NN)

    @pl.when(step == pl.num_programs(0) - 1)
    def _():
        def block(n):
            rows = slice(n * LANES, (n + 1) * LANES)
            return wide_ref[rows, :LANES] + (wide_ref[rows, LANES:] + slim_ref[rows])

        unit = 0
        for e in range(CHUNKS):
            a = block(e)
            put(out_ref, e, a)
            put(out_ref, CHUNKS + e, a.T)
        for e in range(c, CHUNKS):
            b = block(CHUNKS + e - c)
            put(out_ref, 2 * CHUNKS + e - c, b)
            if e > c:
                put(out_ref, 3 * CHUNKS + e - 2 * c - 1, b.T)


def arrived_units(c, mhi, mlo, ohi, olo, r):
    depth = r.shape[0]
    rows = row_block(depth)
    units = len(step_units(c))
    o_rows = {0: PB, 1: PB, 2: PB // 2, 3: LANES}[c]
    o_base = PB - o_rows
    rows_out = PB + (CHUNKS - c) * LANES
    m_spec = pl.BlockSpec((PB, rows), lambda k: (0, k))
    o_spec = pl.BlockSpec((o_rows, rows), lambda k: (PB // o_rows - 1, k))
    return pl.pallas_call(
        functools.partial(step_kernel, c, o_base),
        grid=(depth // rows,),
        in_specs=[m_spec, m_spec, o_spec, o_spec, pl.BlockSpec((rows, LANES), lambda k: (k, 0))],
        out_specs=pl.BlockSpec((GROUP, units, SUB, LANES), lambda k: (0, 0, 0, 0)),
        out_shape=jax.ShapeDtypeStruct((GROUP, units, SUB, LANES), F32),
        scratch_shapes=[pltpu.VMEM((rows_out, 2 * LANES), F32), pltpu.VMEM((rows_out, LANES), F32)],
        compiler_params=pltpu.CompilerParams(vmem_limit_bytes=VMEM),
        cost_estimate=pl.CostEstimate(
            flops=6 * depth * rows_out * LANES, bytes_accessed=4 * depth * (PB + o_rows + LANES), transcendentals=0
        ),
        name="arrived_units",
    )(mhi, mlo, ohi, olo, r)


def final_kernel(order, odd_ref, units_ref, out_ref):
    rows = lax.broadcasted_iota(jnp.int32, (PB, PB), 0)
    cols = lax.broadcasted_iota(jnp.int32, (PB, PB), 1)
    back = (cols == natural_of(rows, 0)).astype(F32).astype(BF16)
    for g, name in enumerate(("c", "am", "b", "ar")):
        lines = [
            jnp.concatenate([units_ref[order[(name, e, c)]] for c in range(CHUNKS)], axis=1) for e in range(CHUNKS)
        ]
        hi, mid, lo = split3(jnp.concatenate(lines, axis=0))
        placed = dot(hi, back, NN) + dot(mid, back, NN) + dot(lo, back, NN)
        out_ref[(g + 2 * odd_ref[0]) % 4] = placed


def final_tiles(order, odd, units):
    return pl.pallas_call(
        functools.partial(final_kernel, order),
        in_specs=[pl.BlockSpec(memory_space=pltpu.SMEM), pl.BlockSpec(memory_space=pltpu.VMEM)],
        out_specs=pl.BlockSpec(memory_space=pltpu.VMEM),
        out_shape=jax.ShapeDtypeStruct((4, SHARE, PB), F32),
        compiler_params=pltpu.CompilerParams(vmem_limit_bytes=VMEM),
        name="final_tiles",
    )(odd, units)


def body(orbitals, owner_perm, pair_reach):
    me = lax.axis_index("pts")
    chips = PTS // 2
    swap = [(p, p ^ 1) for p in range(PTS)]
    onward = [(2 * z, 2 * z - 2) for z in range(1, chips)] + [(2 * z + 1, 2 * z + 3) for z in range(chips - 1)]

    sent = chunks_of(orbitals, 0, 1)
    arrived = [lax.ppermute(sent[0], "pts", onward)]
    other = lax.ppermute(orbitals, "pts", swap)
    sent += chunks_of(orbitals, 1, CHUNKS - 1)
    arrived += [lax.ppermute(x, "pts", onward) for x in sent[1:]]

    def live(b, r):
        return (r < pair_reach[jnp.clip(b, 0, PTS - 1)]) & (b >= 0) & (b + r + 1 < PTS)

    core = me % 2
    live_c = live(me - core, 0)
    live_a = live(me - 2 * core, 1)
    live_b = live(me + 1 - 3 * core, 0)

    def summed(units, flags):
        parts = lax.all_to_all(units, "bas", 0, 0)
        gram = jnp.sum(parts, axis=0)
        return jnp.where(flags[:, None, None], gram * gram, 0.0)

    mhi, mlo = turned(orbitals)
    ohi, olo = turned(other)
    kinds = [("c", e, c, 0) for e in range(CHUNKS) for c in range(CHUNKS)]
    tiles = [summed(local_units(mhi, mlo, ohi, olo), jnp.broadcast_to(live_c, (CHUNKS * CHUNKS,)))]
    for c in range(CHUNKS):
        own = step_units(c)
        flags = jnp.stack([live_b if u[0] == "b" else live_a for u in own])
        tiles.append(summed(arrived_units(c, mhi, mlo, ohi, olo, arrived[c]), flags))
        kinds += own

    per = len(kinds) // PTS
    spread = lax.all_to_all(jnp.concatenate(tiles, axis=0).reshape(PTS, per, SUB, LANES), "pts", 0, 0)
    block = jnp.sum(jnp.where(owner_perm[:, None] == jnp.arange(PTS)[None, :], jnp.arange(PTS)[:, None], 0), axis=0)
    kind = jnp.array([u[3] for u in kinds], jnp.int32).reshape(PTS, per)[me][None, :]
    held = block[:, None]
    source = jnp.where(kind == 0, held, jnp.where(kind == 1, held ^ 1, held - 2 + 4 * (held % 2)))
    there = (source >= 0) & (source < PTS)
    index = jnp.clip(source, 0, PTS - 1) * per + jnp.arange(per)[None, :]
    chosen = spread.reshape(PTS * per, SUB, LANES)[index]
    chosen = jnp.where(there[:, :, None, None], chosen, 0.0)
    mine = lax.all_to_all(chosen, "pts", 0, 0).reshape(PTS * per, SUB, LANES)
    order = {u[:3]: n for n, u in enumerate(kinds)}
    odd = (block[me] % 2).astype(jnp.int32)[None]
    return final_tiles(order, odd, mine)[None]


def solution(mesh):
    return jax.shard_map(
        body,
        mesh=mesh,
        in_specs=(P("bas", "pts"), P(), P()),
        out_specs=P("pts", None, "bas", None),
        check_vma=False,
    )
```

```python
import functools

import jax
import jax.numpy as jnp
from jax import lax
from jax.experimental import pallas as pl
from jax.experimental.pallas import tpu as pltpu
from jax.sharding import PartitionSpec as P

PB = 512
SHARE = 32
LANES = 128
SUB = 8
CHUNKS = PB // LANES
GROUP = LANES // SUB
PTS = 16
VMEM = 14 * 1024 * 1024
F32 = jnp.float32
BF16 = jnp.bfloat16
NT = (((1,), (1,)), ((), ()))
NN = (((1,), (0,)), ((), ()))


def whole(x):
    return pltpu.with_memory_space_constraint(x, pltpu.VMEM)


def in_hbm(x):
    return pltpu.with_memory_space_constraint(x, pltpu.HBM)


IN_VMEM = pl.BlockSpec(memory_space=pltpu.VMEM)
IN_SMEM = pl.BlockSpec(memory_space=pltpu.SMEM)
FLAG = {"c": 0, "am": 1, "ar": 1, "b": 2}
EARLY = 4


def dot(a, b, dims):
    return lax.dot_general(a, b, dims, preferred_element_type=F32)


def natural_of(index, chunk0):
    chunk = chunk0 + index // LANES
    within = index % LANES
    return SHARE * (within // SUB) + SUB * chunk + within % SUB


def split3(x):
    hi = x.astype(BF16)
    rest = x - hi.astype(F32)
    mid = rest.astype(BF16)
    lo = (rest - mid.astype(F32)).astype(BF16)
    return hi, mid, lo


def split2(x):
    hi = x.astype(BF16)
    return hi, (x - hi.astype(F32)).astype(BF16)


def row_block(depth, most=768):
    for size in (768, 640, 512, 384, 256, 128):
        if size <= most and depth % size == 0:
            return size
    return depth


def chunk_kernel(chunk0, count, x_ref, *rest):
    out_refs, pick_ref = rest[:count], rest[count]

    @pl.when(pl.program_id(0) == 0)
    def _():
        rows = lax.broadcasted_iota(jnp.int32, pick_ref.shape, 0)
        cols = lax.broadcasted_iota(jnp.int32, pick_ref.shape, 1)
        pick_ref[...] = (rows == natural_of(cols, chunk0)).astype(F32).astype(BF16)

    hi, mid, lo = split3(x_ref[...])
    pick = pick_ref[...]
    moved = dot(hi, pick, NN) + dot(mid, pick, NN) + dot(lo, pick, NN)
    for n in range(count):
        out_refs[n][...] = moved[:, n * LANES:(n + 1) * LANES]


def chunks_of(x, chunk0, count):
    depth = x.shape[0]
    rows = row_block(depth, 384)
    return pl.pallas_call(
        functools.partial(chunk_kernel, chunk0, count),
        grid=(depth // rows,),
        in_specs=[pl.BlockSpec((rows, PB), lambda k: (k, 0))],
        out_specs=[pl.BlockSpec((rows, LANES), lambda k: (k, 0))] * count,
        out_shape=[pltpu.HBM((depth, LANES), F32)] * count,
        scratch_shapes=[pltpu.VMEM((PB, count * LANES), BF16)],
        compiler_params=pltpu.CompilerParams(vmem_limit_bytes=VMEM),
        cost_estimate=pl.CostEstimate(
            flops=6 * depth * PB * LANES * count, bytes_accessed=4 * depth * (PB + LANES * count), transcendentals=0
        ),
        name="chunks",
    )(x)


def prep_kernel(x_ref, *refs):
    out_refs, hi_ref, lo_ref, pick_ref, back_ref = refs[:-4], *refs[-4:]

    @pl.when(pl.program_id(0) == 0)
    def _():
        rows = lax.broadcasted_iota(jnp.int32, (PB, PB), 0)
        cols = lax.broadcasted_iota(jnp.int32, (PB, PB), 1)
        pick_ref[...] = (rows == natural_of(cols, 0)).astype(F32).astype(BF16)
        back_ref[...] = (cols == natural_of(rows, 0)).astype(F32).astype(BF16)

    hi, mid, lo = split3(x_ref[...])
    pick = pick_ref[:, LANES:]
    moved = dot(hi, pick, NN) + dot(mid, pick, NN) + dot(lo, pick, NN)
    for n, out_ref in enumerate(out_refs):
        out_ref[...] = moved[:, n * LANES:(n + 1) * LANES]
    hi_ref[...] = dot(back_ref[...], hi, NT).astype(BF16)
    lo_ref[...] = dot(back_ref[...], mid, NT).astype(BF16)


def prepared(x):
    depth = x.shape[0]
    rows = row_block(depth, 384)
    count = CHUNKS - 1
    got = pl.pallas_call(
        prep_kernel,
        grid=(depth // rows,),
        in_specs=[pl.BlockSpec((rows, PB), lambda k: (k, 0))],
        out_specs=[pl.BlockSpec((rows, LANES), lambda k: (k, 0))] * count
        + [pl.BlockSpec((PB, rows), lambda k: (0, k))] * 2,
        out_shape=[pltpu.HBM((depth, LANES), F32)] * count
        + [pltpu.HBM((PB, depth), BF16)] * 2,
        scratch_shapes=[pltpu.VMEM((PB, PB), BF16)] * 2,
        compiler_params=pltpu.CompilerParams(vmem_limit_bytes=VMEM),
        cost_estimate=pl.CostEstimate(flops=9 * depth * PB * PB, bytes_accessed=14 * depth * PB, transcendentals=0),
        name="prepared",
    )(x)
    return got[:count], got[count], got[count + 1]


def turn_kernel(x_ref, hi_ref, lo_ref, pick_ref):
    @pl.when(pl.program_id(0) == 0)
    def _():
        rows = lax.broadcasted_iota(jnp.int32, pick_ref.shape, 0)
        cols = lax.broadcasted_iota(jnp.int32, pick_ref.shape, 1)
        pick_ref[...] = (cols == natural_of(rows, 0)).astype(F32).astype(BF16)

    hi, lo = split2(x_ref[...])
    hi_ref[...] = dot(pick_ref[...], hi, NT).astype(BF16)
    lo_ref[...] = dot(pick_ref[...], lo, NT).astype(BF16)


def turned(x):
    depth = x.shape[0]
    rows = row_block(depth, 384)
    return pl.pallas_call(
        turn_kernel,
        grid=(depth // rows,),
        in_specs=[pl.BlockSpec((rows, PB), lambda k: (k, 0))],
        out_specs=[pl.BlockSpec((PB, rows), lambda k: (0, k))] * 2,
        out_shape=[pltpu.HBM((PB, depth), BF16)] * 2,
        scratch_shapes=[pltpu.VMEM((PB, PB), BF16)],
        compiler_params=pltpu.CompilerParams(vmem_limit_bytes=VMEM),
        cost_estimate=pl.CostEstimate(flops=4 * depth * PB * PB, bytes_accessed=8 * depth * PB, transcendentals=0),
        name="turned",
    )(x)


def put(out_ref, unit, block):
    out_ref[:, unit] = block.reshape(GROUP, SUB, LANES)


IN_VMEM = pl.BlockSpec(memory_space=pltpu.VMEM)
IN_SMEM = pl.BlockSpec(memory_space=pltpu.SMEM)
FLAG = {"c": 0, "am": 1, "ar": 1, "b": 2}
EARLY = 4


def local_kernel(mhi_ref, mlo_ref, ohi_ref, olo_ref, out_ref, acc_ref):
    step = pl.program_id(0)

    @pl.when(step == 0)
    def _():
        acc_ref[...] = jnp.zeros_like(acc_ref)

    mhi, ohi = mhi_ref[...], ohi_ref[...]
    acc_ref[...] += dot(mhi, ohi, NT) + dot(mhi, olo_ref[...], NT) + dot(mlo_ref[...], ohi, NT)

    @pl.when(step == pl.num_programs(0) - 1)
    def _():
        for e in range(CHUNKS):
            for c in range(CHUNKS):
                put(out_ref, CHUNKS * e + c, acc_ref[e * LANES:(e + 1) * LANES, c * LANES:(c + 1) * LANES])


def local_units(mhi, mlo, ohi, olo):
    depth = mhi.shape[1]
    rows = row_block(depth)
    units = CHUNKS * CHUNKS
    return pl.pallas_call(
        local_kernel,
        grid=(depth // rows,),
        in_specs=[pl.BlockSpec((PB, rows), lambda k: (0, k))] * 4,
        out_specs=pl.BlockSpec((GROUP, units, SUB, LANES), lambda k: (0, 0, 0, 0)),
        out_shape=pltpu.HBM((GROUP, units, SUB, LANES), F32),
        scratch_shapes=[pltpu.VMEM((PB, PB), F32)],
        compiler_params=pltpu.CompilerParams(vmem_limit_bytes=VMEM),
        cost_estimate=pl.CostEstimate(flops=6 * depth * PB * PB, bytes_accessed=8 * depth * PB, transcendentals=0),
        name="local_units",
    )(in_hbm(mhi), in_hbm(mlo), in_hbm(ohi), in_hbm(olo))


def step_units(c):
    units = [("am", e, c, 0) for e in range(CHUNKS)]
    units += [("ar", c, e, 2) for e in range(CHUNKS)]
    units += [("b", e, c, 1) for e in range(c, CHUNKS)]
    units += [("b", c, e, 2) for e in range(c + 1, CHUNKS)]
    return units


def step_kernel(c, o_base, mhi_ref, mlo_ref, ohi_ref, olo_ref, r_ref, out_ref, wide_ref, slim_ref):
    step = pl.program_id(0)

    @pl.when(step == 0)
    def _():
        wide_ref[...] = jnp.zeros_like(wide_ref)
        slim_ref[...] = jnp.zeros_like(slim_ref)

    rhi, rlo = split2(r_ref[...])
    both = jnp.concatenate([rhi, rlo], axis=1)
    skip = c * LANES - o_base
    wide_ref[:PB] += dot(mhi_ref[...], both, NN)
    slim_ref[:PB] += dot(mlo_ref[...], rhi, NN)
    wide_ref[PB:] += dot(ohi_ref[skip:], both, NN)
    slim_ref[PB:] += dot(olo_ref[skip:], rhi, NN)

    @pl.when(step == pl.num_programs(0) - 1)
    def _():
        def block(n):
            rows = slice(n * LANES, (n + 1) * LANES)
            return wide_ref[rows, :LANES] + (wide_ref[rows, LANES:] + slim_ref[rows])

        unit = 0
        for e in range(CHUNKS):
            a = block(e)
            put(out_ref, e, a)
            put(out_ref, CHUNKS + e, a.T)
        for e in range(c, CHUNKS):
            b = block(CHUNKS + e - c)
            put(out_ref, 2 * CHUNKS + e - c, b)
            if e > c:
                put(out_ref, 3 * CHUNKS + e - 2 * c - 1, b.T)


def arrived_units(c, mhi, mlo, ohi, olo, r):
    depth = r.shape[0]
    rows = row_block(depth)
    units = len(step_units(c))
    o_rows = {0: PB, 1: PB, 2: PB // 2, 3: LANES}[c]
    o_base = PB - o_rows
    rows_out = PB + (CHUNKS - c) * LANES
    m_spec = pl.BlockSpec((PB, rows), lambda k: (0, k))
    o_spec = pl.BlockSpec((o_rows, rows), lambda k: (PB // o_rows - 1, k))
    return pl.pallas_call(
        functools.partial(step_kernel, c, o_base),
        grid=(depth // rows,),
        in_specs=[m_spec, m_spec, o_spec, o_spec, pl.BlockSpec((rows, LANES), lambda k: (k, 0))],
        out_specs=pl.BlockSpec((GROUP, units, SUB, LANES), lambda k: (0, 0, 0, 0)),
        out_shape=pltpu.HBM((GROUP, units, SUB, LANES), F32),
        scratch_shapes=[pltpu.VMEM((rows_out, 2 * LANES), F32), pltpu.VMEM((rows_out, LANES), F32)],
        compiler_params=pltpu.CompilerParams(vmem_limit_bytes=VMEM),
        cost_estimate=pl.CostEstimate(
            flops=6 * depth * rows_out * LANES, bytes_accessed=4 * depth * (PB + o_rows + LANES), transcendentals=0
        ),
        name="arrived_units",
    )(in_hbm(mhi), in_hbm(mlo), in_hbm(ohi), in_hbm(olo), in_hbm(r))


def squares(parts_ref, unit, flag):
    gram = parts_ref[0, unit]
    for n in range(1, GROUP):
        gram = gram + parts_ref[n, unit]
    return jnp.where(flag != 0, gram * gram, 0.0)


def early_kernel(names, flags_ref, *refs):
    part_refs, out_ref = refs[:-1], refs[-1]
    n = 0
    for part_ref, units in zip(part_refs, names):
        for u, name in enumerate(units):
            out_ref[n] = squares(part_ref, u, flags_ref[FLAG[name]])
            n += 1
    for pad in range(n, out_ref.shape[0]):
        out_ref[pad] = jnp.zeros((SUB, LANES), F32)


def early_tiles(names, flags, parts, count):
    return pl.pallas_call(
        functools.partial(early_kernel, names),
        in_specs=[IN_SMEM] + [IN_VMEM] * len(parts),
        out_specs=IN_VMEM,
        out_shape=pltpu.HBM((count, SUB, LANES), F32),
        compiler_params=pltpu.CompilerParams(vmem_limit_bytes=VMEM),
        name="early_tiles",
    )(flags, *[whole(x) for x in parts])


def send_kernel(slots, flags_ref, pick_ref, source_ref, parts_ref, spread_ref, out_ref, held_ref):
    size = held_ref.shape[1]
    per = out_ref.shape[1] - size
    for kind, units in enumerate(slots):
        for n, (u, name) in enumerate(units):
            held_ref[kind, n] = squares(parts_ref, u, flags_ref[FLAG[name]])
        for n in range(len(units), size):
            held_ref[kind, n] = jnp.zeros((SUB, LANES), F32)

    @pl.loop(0, PTS)
    def _(k):
        out_ref[k, :size] = held_ref[pick_ref[k]]
        for n in range(per):
            at = source_ref[k * per + n]
            out_ref[k, size + n] = jnp.where(at >= 0, spread_ref[jnp.maximum(at, 0)], 0.0)


def sendings(slots, flags, pick, source, parts, spread):
    size = max(len(units) for units in slots)
    per = spread.shape[0] // PTS
    return pl.pallas_call(
        functools.partial(send_kernel, slots),
        in_specs=[IN_SMEM] * 3 + [IN_VMEM] * 2,
        out_specs=IN_VMEM,
        out_shape=jax.ShapeDtypeStruct((PTS, size + per, SUB, LANES), F32),
        scratch_shapes=[pltpu.VMEM((len(slots), size, SUB, LANES), F32)],
        compiler_params=pltpu.CompilerParams(vmem_limit_bytes=VMEM),
        name="sendings",
    )(flags, pick, source, whole(parts), whole(spread))


def final_kernel(early_at, late_at, where_ref, got_ref, out_ref):
    rows = lax.broadcasted_iota(jnp.int32, (PB, PB), 0)
    cols = lax.broadcasted_iota(jnp.int32, (PB, PB), 1)
    back = (cols == natural_of(rows, 0)).astype(F32).astype(BF16)

    def unit(name, e, c):
        if (name, e, c) in early_at:
            return got_ref[early_at[(name, e, c)]]
        kind, slot = late_at[(name, e, c)]
        got = got_ref[where_ref[1 + kind], slot]
        return jnp.where(where_ref[4] != 0, got, 0.0) if kind == 2 else got

    for g, name in enumerate(("c", "am", "b", "ar")):
        lines = [jnp.concatenate([unit(name, e, c) for c in range(CHUNKS)], axis=1) for e in range(CHUNKS)]
        hi, mid, lo = split3(jnp.concatenate(lines, axis=0))
        placed = dot(hi, back, NN) + dot(mid, back, NN) + dot(lo, back, NN)
        out_ref[lax.rem(g + 2 * where_ref[0], 4)] = placed


def final_tiles(early_at, late_at, where, got):
    return pl.pallas_call(
        functools.partial(final_kernel, early_at, late_at),
        in_specs=[IN_SMEM, IN_VMEM],
        out_specs=IN_VMEM,
        out_shape=jax.ShapeDtypeStruct((4, SHARE, PB), F32),
        compiler_params=pltpu.CompilerParams(vmem_limit_bytes=VMEM),
        name="final_tiles",
    )(where, whole(got))


def after(x, *others):
    return lax.optimization_barrier((x,) + others)[0]


def body(orbitals, owner_perm, pair_reach):
    me = lax.axis_index("pts")
    chips = PTS // 2
    swap = [(p, p ^ 1) for p in range(PTS)]
    onward = [(2 * z, 2 * z - 2) for z in range(1, chips)] + [(2 * z + 1, 2 * z + 3) for z in range(chips - 1)]

    def live(b, r):
        return (r < pair_reach[jnp.clip(b, 0, PTS - 1)]) & (b >= 0) & (b + r + 1 < PTS)

    core = me % 2
    flags = jnp.stack([live(me - core, 0), live(me - 2 * core, 1), live(me + 1 - 3 * core, 0)]).astype(jnp.int32)
    ids = jnp.arange(PTS, dtype=jnp.int32)
    block = jnp.sum(jnp.where(owner_perm[:, None] == ids[None, :], ids[:, None], 0), axis=0)
    partner = block - 2 + 4 * (block % 2)
    there = (partner >= 0) & (partner < PTS)
    partner = jnp.clip(partner, 0, PTS - 1)
    mine = ids == me
    own = lambda x: jnp.sum(jnp.where(mine, x, 0))
    where = jnp.stack([own(block % 2), own(block), own(block ^ 1), own(partner), own(there.astype(jnp.int32))])
    pick = jnp.where(block == me, 0, jnp.where(block == (me ^ 1), 1, 2))

    sent = chunks_of(in_hbm(orbitals), 0, 1)
    other = lax.ppermute(after(orbitals, sent[0]), "pts", swap)
    rest, mhi, mlo = prepared(in_hbm(after(orbitals, sent[0])))
    arrived = []
    for c, x in enumerate([*sent, *rest]):
        arrived.append(lax.ppermute(x if c < 2 else after(x, arrived[c - 2]), "pts", onward))

    ohi, olo = turned(in_hbm(after(other, mhi)))
    to_sum = lambda x: lax.all_to_all(x, "bas", 0, 0)
    kinds = [[("c", e, c, 0) for e in range(CHUNKS) for c in range(CHUNKS)]] + [step_units(c) for c in range(CHUNKS)]
    names = [[u[0] for u in k] for k in kinds]
    flat = [u for k in kinds[:EARLY] for u in k]
    per = -(-len(flat) // PTS)
    kind = jnp.array([u[3] for u in flat] + [0] * (per * PTS - len(flat)), jnp.int32).reshape(PTS, per)
    kind = jnp.sum(jnp.where(mine[:, None], kind, 0), axis=0)[None, :]
    source = jnp.where(kind == 0, block[:, None], jnp.where(kind == 1, block[:, None] ^ 1, partner[:, None]))
    source = source * per + jnp.arange(per)[None, :]
    source = jnp.where((kind == 2) & ~there[:, None], -1, source).reshape(-1)

    units = [local_units(mhi, mlo, ohi, olo)]
    parts = [to_sum(units[0])]

    def multiply(c, *first):
        units.append(arrived_units(c, mhi, mlo, ohi, olo, after(arrived[c], units[-1], *first)))
        parts.append(to_sum(units[-1]))

    multiply(0, flags, where, pick, source)
    multiply(1, parts[0])
    multiply(2, parts[1])
    held = [after(x, units[3]) for x in parts[:3]]
    multiply(3, *held)
    early = early_tiles(names[:EARLY], flags, held + parts[3:EARLY], per * PTS)
    spread = lax.all_to_all(early.reshape(PTS, per, SUB, LANES), "pts", 0, 0).reshape(PTS * per, SUB, LANES)
    slots = [[], [], []]
    late_at = {}
    for u, (name, e, c, owner) in enumerate(kinds[EARLY]):
        late_at[(name, e, c)] = (owner, len(slots[owner]))
        slots[owner].append((u, name))
    size = max(len(x) for x in slots)
    early_at = {u[:3]: (n // per, size + n % per) for n, u in enumerate(flat)}
    got = lax.all_to_all(sendings(slots, flags, pick, source, parts[EARLY], spread), "pts", 0, 0)
    return final_tiles(early_at, late_at, where, got)[None]


def solution(mesh):
    return jax.shard_map(
        body,
        mesh=mesh,
        in_specs=(P("bas", "pts"), P(), P()),
        out_specs=P("pts", None, "bas", None),
        check_vma=False,
    )
```

```python
import functools

import jax
import jax.numpy as jnp
from jax import lax
from jax.experimental import pallas as pl
from jax.experimental.pallas import tpu as pltpu
from jax.sharding import PartitionSpec as P

PB = 512
SHARE = 32
LANES = 128
SUB = 8
CHUNKS = PB // LANES
GROUP = LANES // SUB
PTS = 16
VMEM = 14 * 1024 * 1024
WIDE = 48 * 1024 * 1024
F32 = jnp.float32
BF16 = jnp.bfloat16
NT = (((1,), (1,)), ((), ()))
NN = (((1,), (0,)), ((), ()))


def whole(x):
    return pltpu.with_memory_space_constraint(x, pltpu.VMEM)


def in_hbm(x):
    return pltpu.with_memory_space_constraint(x, pltpu.HBM)


IN_VMEM = pl.BlockSpec(memory_space=pltpu.VMEM)
IN_SMEM = pl.BlockSpec(memory_space=pltpu.SMEM)
FLAG = {"c": 0, "am": 1, "ar": 1, "b": 2}
EARLY = 4


def dot(a, b, dims):
    return lax.dot_general(a, b, dims, preferred_element_type=F32)


def natural_of(index, chunk0):
    chunk = chunk0 + index // LANES
    within = index % LANES
    return SHARE * (within // SUB) + SUB * chunk + within % SUB


def split3(x):
    hi = x.astype(BF16)
    rest = x - hi.astype(F32)
    mid = rest.astype(BF16)
    lo = (rest - mid.astype(F32)).astype(BF16)
    return hi, mid, lo


def split2(x):
    hi = x.astype(BF16)
    return hi, (x - hi.astype(F32)).astype(BF16)


def row_block(depth, most=768):
    for size in (768, 640, 512, 384, 256, 128):
        if size <= most and depth % size == 0:
            return size
    return depth


ANY = pl.BlockSpec(memory_space=pl.ANY)


def piece(k, rows):
    return pl.ds(pl.multiple_of(k * rows, rows), rows)


class Flow:
    def __init__(self, src, dst, sems, count):
        self.src, self.dst, self.sems, self.count = src, dst, sems, count

    def copy(self, k):
        return pltpu.make_async_copy(self.src(k), self.dst(k), self.sems.at[k])

    def start(self):
        for k in range(self.count):
            self.copy(k).start()

    def wait(self):
        for k in range(self.count):
            self.copy(k).wait()


def by_rows(src, dst, sems, rows, count):
    return Flow(lambda k: src.at[piece(k, rows)], lambda k: dst.at[piece(k, rows)], sems, count)


def by_lanes(src, dst, sems, rows, count):
    return Flow(lambda k: src.at[:, piece(k, rows)], lambda k: dst.at[:, piece(k, rows)], sems, count)


def start_all(flows):
    for k in range(flows[0].count):
        for flow in flows:
            flow.copy(k).start()


def picks(shape, chunk0):
    rows = lax.broadcasted_iota(jnp.int32, shape, 0)
    cols = lax.broadcasted_iota(jnp.int32, shape, 1)
    return (rows == natural_of(cols, chunk0)).astype(F32).astype(BF16)


def backs():
    rows = lax.broadcasted_iota(jnp.int32, (PB, PB), 0)
    cols = lax.broadcasted_iota(jnp.int32, (PB, PB), 1)
    return (cols == natural_of(rows, 0)).astype(F32).astype(BF16)


def first_kernel(count, rows, x_hbm, out_hbm, x_ref, out_ref, pick_ref, in_sems, out_sems):
    coming = by_rows(x_hbm, x_ref, in_sems, rows, count)
    going = by_rows(out_ref, out_hbm, out_sems, rows, count)
    coming.start()
    pick_ref[...] = picks(pick_ref.shape, 0)

    @pl.loop(0, count)
    def _(k):
        coming.copy(k).wait()
        hi, mid, lo = split3(x_ref[piece(k, rows)])
        pick = pick_ref[...]
        out_ref[piece(k, rows)] = dot(hi, pick, NN) + dot(mid, pick, NN) + dot(lo, pick, NN)
        going.copy(k).start()

    going.wait()


def first_chunk(x):
    depth = x.shape[0]
    rows = row_block(depth, 384)
    count = depth // rows
    return pl.pallas_call(
        functools.partial(first_kernel, count, rows),
        in_specs=[ANY],
        out_specs=ANY,
        out_shape=pltpu.HBM((depth, LANES), F32),
        scratch_shapes=[
            pltpu.VMEM((depth, PB), F32),
            pltpu.VMEM((depth, LANES), F32),
            pltpu.VMEM((PB, LANES), BF16),
            pltpu.SemaphoreType.DMA((count,)),
            pltpu.SemaphoreType.DMA((count,)),
        ],
        compiler_params=pltpu.CompilerParams(vmem_limit_bytes=WIDE),
        cost_estimate=pl.CostEstimate(flops=6 * depth * PB * LANES, bytes_accessed=4 * depth * (PB + LANES), transcendentals=0),
        name="first_chunk",
    )(in_hbm(x))


def prep_kernel(count, rows, x_hbm, *refs):
    out_hbm, turned_hbm = refs[:CHUNKS - 1], refs[CHUNKS - 1:CHUNKS + 1]
    x_ref, out_ref, hi_ref, lo_ref, pick_ref, back_ref, in_sems, out_sems = refs[CHUNKS + 1:]
    coming = by_rows(x_hbm, x_ref, in_sems, rows, count)
    going = [by_rows(out_ref.at[n], out_hbm[n], out_sems.at[n], rows, count) for n in range(CHUNKS - 1)]
    going += [
        by_lanes(ref, turned_hbm[n], out_sems.at[CHUNKS - 1 + n], rows, count) for n, ref in enumerate((hi_ref, lo_ref))
    ]
    coming.start()
    pick_ref[...] = picks(pick_ref.shape, 1)
    back_ref[...] = backs()

    @pl.loop(0, count)
    def _(k):
        coming.copy(k).wait()
        hi, mid, lo = split3(x_ref[piece(k, rows)])
        pick = pick_ref[...]
        moved = dot(hi, pick, NN) + dot(mid, pick, NN) + dot(lo, pick, NN)
        for n in range(CHUNKS - 1):
            out_ref[n, piece(k, rows)] = moved[:, n * LANES:(n + 1) * LANES]
        hi_ref[:, piece(k, rows)] = dot(back_ref[...], hi, NT).astype(BF16)
        lo_ref[:, piece(k, rows)] = dot(back_ref[...], mid, NT).astype(BF16)
        for flow in going:
            flow.copy(k).start()

    for flow in going:
        flow.wait()


def prepared(x):
    depth = x.shape[0]
    rows = row_block(depth, 384)
    count = depth // rows
    got = pl.pallas_call(
        functools.partial(prep_kernel, count, rows),
        in_specs=[ANY],
        out_specs=[ANY] * (CHUNKS + 1),
        out_shape=[pltpu.HBM((depth, LANES), F32)] * (CHUNKS - 1) + [pltpu.HBM((PB, depth), BF16)] * 2,
        scratch_shapes=[
            pltpu.VMEM((depth, PB), F32),
            pltpu.VMEM((CHUNKS - 1, depth, LANES), F32),
            pltpu.VMEM((PB, depth), BF16),
            pltpu.VMEM((PB, depth), BF16),
            pltpu.VMEM((PB, PB - LANES), BF16),
            pltpu.VMEM((PB, PB), BF16),
            pltpu.SemaphoreType.DMA((count,)),
            pltpu.SemaphoreType.DMA((CHUNKS + 1, count)),
        ],
        compiler_params=pltpu.CompilerParams(vmem_limit_bytes=WIDE),
        cost_estimate=pl.CostEstimate(flops=9 * depth * PB * PB, bytes_accessed=14 * depth * PB, transcendentals=0),
        name="prepared",
    )(in_hbm(x))
    return got[:CHUNKS - 1], got[CHUNKS - 1], got[CHUNKS]


def local_kernel(
    count, rows, o_hbm, mhi_hbm, mlo_hbm, ohi_hbm, olo_hbm, out_ref,
    o_ref, mhi_ref, mlo_ref, ohi_ref, olo_ref, back_ref, acc_ref, in_sems, out_sems,
):
    coming = [
        by_rows(o_hbm, o_ref, in_sems.at[0], rows, count),
        by_lanes(mhi_hbm, mhi_ref, in_sems.at[1], rows, count),
        by_lanes(mlo_hbm, mlo_ref, in_sems.at[2], rows, count),
    ]
    going = [
        by_lanes(ohi_ref, ohi_hbm, out_sems.at[0], rows, count),
        by_lanes(olo_ref, olo_hbm, out_sems.at[1], rows, count),
    ]
    start_all(coming)
    back_ref[...] = backs()
    acc_ref[...] = jnp.zeros_like(acc_ref)

    @pl.loop(0, count)
    def _(k):
        at = piece(k, rows)
        coming[0].copy(k).wait()
        hi, lo = split2(o_ref[at])
        ohi = dot(back_ref[...], hi, NT).astype(BF16)
        olo = dot(back_ref[...], lo, NT).astype(BF16)
        ohi_ref[:, at] = ohi
        olo_ref[:, at] = olo
        for flow in going:
            flow.copy(k).start()
        for flow in coming[1:]:
            flow.copy(k).wait()
        mhi = mhi_ref[:, at]
        acc_ref[...] += dot(mhi, ohi, NT) + dot(mhi, olo, NT) + dot(mlo_ref[:, at], ohi, NT)

    for e in range(CHUNKS):
        for c in range(CHUNKS):
            put(out_ref, CHUNKS * e + c, acc_ref[e * LANES:(e + 1) * LANES, c * LANES:(c + 1) * LANES])
    for flow in going:
        flow.wait()


def local_units(other, mhi, mlo):
    depth = other.shape[0]
    rows = row_block(depth)
    count = depth // rows
    units = CHUNKS * CHUNKS
    wide = pltpu.VMEM((PB, depth), BF16)
    return pl.pallas_call(
        functools.partial(local_kernel, count, rows),
        in_specs=[ANY] * 3,
        out_specs=[ANY, ANY, pl.BlockSpec((GROUP, units, SUB, LANES))],
        out_shape=[pltpu.HBM((PB, depth), BF16)] * 2 + [pltpu.HBM((GROUP, units, SUB, LANES), F32)],
        scratch_shapes=[
            pltpu.VMEM((depth, PB), F32), wide, wide, wide, wide,
            pltpu.VMEM((PB, PB), BF16),
            pltpu.VMEM((PB, PB), F32),
            pltpu.SemaphoreType.DMA((3, count)),
            pltpu.SemaphoreType.DMA((2, count)),
        ],
        compiler_params=pltpu.CompilerParams(vmem_limit_bytes=WIDE),
        cost_estimate=pl.CostEstimate(flops=10 * depth * PB * PB, bytes_accessed=12 * depth * PB, transcendentals=0),
        name="local_units",
    )(in_hbm(other), in_hbm(mhi), in_hbm(mlo))


def put(out_ref, unit, block):
    out_ref[:, unit] = block.reshape(GROUP, SUB, LANES)


IN_VMEM = pl.BlockSpec(memory_space=pltpu.VMEM)
IN_SMEM = pl.BlockSpec(memory_space=pltpu.SMEM)
FLAG = {"c": 0, "am": 1, "ar": 1, "b": 2}
EARLY = 4


def step_units(c):
    units = [("am", e, c, 0) for e in range(CHUNKS)]
    units += [("ar", c, e, 2) for e in range(CHUNKS)]
    units += [("b", e, c, 1) for e in range(c, CHUNKS)]
    units += [("b", c, e, 2) for e in range(c + 1, CHUNKS)]
    return units


def step_kernel(
    c, count, rows, mhi_hbm, mlo_hbm, ohi_hbm, olo_hbm, r_hbm, out_ref,
    hi_ref, lo_ref, r_ref, wide_ref, slim_ref, sems,
):
    left = (CHUNKS - c) * LANES

    def lanes(src, dst, sem, first, base, n):
        return Flow(
            lambda k: src.at[pl.ds(first, n), piece(k, rows)], lambda k: dst.at[pl.ds(base, n), piece(k, rows)], sem, count
        )

    coming = [
        by_rows(r_hbm, r_ref, sems.at[0], rows, count),
        lanes(mhi_hbm, hi_ref, sems.at[1], 0, 0, PB),
        lanes(ohi_hbm, hi_ref, sems.at[2], PB - left, PB, left),
        lanes(mlo_hbm, lo_ref, sems.at[3], 0, 0, PB),
        lanes(olo_hbm, lo_ref, sems.at[4], PB - left, PB, left),
    ]
    start_all(coming)
    wide_ref[...] = jnp.zeros_like(wide_ref)
    slim_ref[...] = jnp.zeros_like(slim_ref)

    @pl.loop(0, count)
    def _(k):
        at = piece(k, rows)
        coming[0].copy(k).wait()
        rhi, rlo = split2(r_ref[at])
        coming[1].copy(k).wait()
        coming[2].copy(k).wait()
        wide_ref[...] += dot(hi_ref[:, at], jnp.concatenate([rhi, rlo], axis=1), NN)
        coming[3].copy(k).wait()
        coming[4].copy(k).wait()
        slim_ref[...] += dot(lo_ref[:, at], rhi, NN)

    def block(n):
        rows = slice(n * LANES, (n + 1) * LANES)
        return wide_ref[rows, :LANES] + (wide_ref[rows, LANES:] + slim_ref[rows])

    for e in range(CHUNKS):
        a = block(e)
        put(out_ref, e, a)
        put(out_ref, CHUNKS + e, a.T)
    for e in range(c, CHUNKS):
        b = block(CHUNKS + e - c)
        put(out_ref, 2 * CHUNKS + e - c, b)
        if e > c:
            put(out_ref, 3 * CHUNKS + e - 2 * c - 1, b.T)


def arrived_units(c, mhi, mlo, ohi, olo, r):
    depth = r.shape[0]
    rows = row_block(depth)
    count = depth // rows
    units = len(step_units(c))
    lines = PB + (CHUNKS - c) * LANES
    return pl.pallas_call(
        functools.partial(step_kernel, c, count, rows),
        in_specs=[ANY] * 5,
        out_specs=pl.BlockSpec((GROUP, units, SUB, LANES)),
        out_shape=pltpu.HBM((GROUP, units, SUB, LANES), F32),
        scratch_shapes=[
            pltpu.VMEM((lines, depth), BF16),
            pltpu.VMEM((lines, depth), BF16),
            pltpu.VMEM((depth, LANES), F32),
            pltpu.VMEM((lines, 2 * LANES), F32),
            pltpu.VMEM((lines, LANES), F32),
            pltpu.SemaphoreType.DMA((5, count)),
        ],
        compiler_params=pltpu.CompilerParams(vmem_limit_bytes=WIDE),
        cost_estimate=pl.CostEstimate(
            flops=6 * depth * lines * LANES, bytes_accessed=4 * depth * (lines + LANES), transcendentals=0
        ),
        name="arrived_units",
    )(in_hbm(mhi), in_hbm(mlo), in_hbm(ohi), in_hbm(olo), in_hbm(r))


def squares(parts_ref, unit, flag):
    gram = parts_ref[0, unit]
    for n in range(1, GROUP):
        gram = gram + parts_ref[n, unit]
    return jnp.where(flag != 0, gram * gram, 0.0)


def early_kernel(names, flags_ref, *refs):
    part_refs, out_ref = refs[:-1], refs[-1]
    n = 0
    for part_ref, units in zip(part_refs, names):
        for u, name in enumerate(units):
            out_ref[n] = squares(part_ref, u, flags_ref[FLAG[name]])
            n += 1
    for pad in range(n, out_ref.shape[0]):
        out_ref[pad] = jnp.zeros((SUB, LANES), F32)


def early_tiles(names, flags, parts, count):
    return pl.pallas_call(
        functools.partial(early_kernel, names),
        in_specs=[IN_SMEM] + [IN_VMEM] * len(parts),
        out_specs=IN_VMEM,
        out_shape=pltpu.HBM((count, SUB, LANES), F32),
        compiler_params=pltpu.CompilerParams(vmem_limit_bytes=VMEM),
        name="early_tiles",
    )(flags, *[whole(x) for x in parts])


def send_kernel(slots, flags_ref, pick_ref, source_ref, parts_ref, spread_ref, out_ref, held_ref):
    size = held_ref.shape[1]
    per = out_ref.shape[1] - size
    for kind, units in enumerate(slots):
        for n, (u, name) in enumerate(units):
            held_ref[kind, n] = squares(parts_ref, u, flags_ref[FLAG[name]])
        for n in range(len(units), size):
            held_ref[kind, n] = jnp.zeros((SUB, LANES), F32)

    @pl.loop(0, PTS)
    def _(k):
        out_ref[k, :size] = held_ref[pick_ref[k]]
        for n in range(per):
            at = source_ref[k * per + n]
            out_ref[k, size + n] = jnp.where(at >= 0, spread_ref[jnp.maximum(at, 0)], 0.0)


def sendings(slots, flags, pick, source, parts, spread):
    size = max(len(units) for units in slots)
    per = spread.shape[0] // PTS
    return pl.pallas_call(
        functools.partial(send_kernel, slots),
        in_specs=[IN_SMEM] * 3 + [IN_VMEM] * 2,
        out_specs=IN_VMEM,
        out_shape=jax.ShapeDtypeStruct((PTS, size + per, SUB, LANES), F32),
        scratch_shapes=[pltpu.VMEM((len(slots), size, SUB, LANES), F32)],
        compiler_params=pltpu.CompilerParams(vmem_limit_bytes=VMEM),
        name="sendings",
    )(flags, pick, source, whole(parts), whole(spread))


def final_kernel(early_at, late_at, where_ref, got_ref, out_ref):
    rows = lax.broadcasted_iota(jnp.int32, (PB, PB), 0)
    cols = lax.broadcasted_iota(jnp.int32, (PB, PB), 1)
    back = (cols == natural_of(rows, 0)).astype(F32).astype(BF16)

    def unit(name, e, c):
        if (name, e, c) in early_at:
            return got_ref[early_at[(name, e, c)]]
        kind, slot = late_at[(name, e, c)]
        got = got_ref[where_ref[1 + kind], slot]
        return jnp.where(where_ref[4] != 0, got, 0.0) if kind == 2 else got

    for g, name in enumerate(("c", "am", "b", "ar")):
        lines = [jnp.concatenate([unit(name, e, c) for c in range(CHUNKS)], axis=1) for e in range(CHUNKS)]
        hi, mid, lo = split3(jnp.concatenate(lines, axis=0))
        placed = dot(hi, back, NN) + dot(mid, back, NN) + dot(lo, back, NN)
        out_ref[lax.rem(g + 2 * where_ref[0], 4)] = placed


def final_tiles(early_at, late_at, where, got):
    return pl.pallas_call(
        functools.partial(final_kernel, early_at, late_at),
        in_specs=[IN_SMEM, IN_VMEM],
        out_specs=IN_VMEM,
        out_shape=jax.ShapeDtypeStruct((4, SHARE, PB), F32),
        compiler_params=pltpu.CompilerParams(vmem_limit_bytes=VMEM),
        name="final_tiles",
    )(where, whole(got))


def after(x, *others):
    return lax.optimization_barrier((x,) + others)[0]


def body(orbitals, owner_perm, pair_reach):
    me = lax.axis_index("pts")
    chips = PTS // 2
    swap = [(p, p ^ 1) for p in range(PTS)]
    onward = [(2 * z, 2 * z - 2) for z in range(1, chips)] + [(2 * z + 1, 2 * z + 3) for z in range(chips - 1)]

    ids = jnp.arange(PTS, dtype=jnp.int32)
    three = jnp.arange(3, dtype=jnp.int32)[:, None]
    first_of = me + (three == 2) - (me % 2) * (three + 1)
    apart = (three == 1).astype(jnp.int32)
    live = (ids == first_of) & (apart < pair_reach[None, :]) & (ids + apart + 1 < PTS)
    flags = jnp.sum(live.astype(jnp.int32), axis=1)
    block = jnp.sum(jnp.where(owner_perm[:, None] == ids[None, :], ids[:, None], 0), axis=0)
    partner = block - 2 + 4 * (block % 2)
    there = (partner >= 0) & (partner < PTS)
    partner = jnp.clip(partner, 0, PTS - 1)
    mine = ids == me
    five = jnp.arange(5, dtype=jnp.int32)[:, None]
    facts = jnp.where(five == 0, block % 2, jnp.where(five == 1, block, jnp.where(five == 2, block ^ 1, partner)))
    facts = jnp.where(five == 4, there.astype(jnp.int32), facts)
    where = jnp.sum(jnp.where(mine, facts, 0), axis=1)
    pick = jnp.where(block == me, 0, jnp.where(block == (me ^ 1), 1, 2))

    first = first_chunk(orbitals)
    other = lax.ppermute(after(orbitals, first), "pts", swap)
    rest, mhi, mlo = prepared(after(orbitals, first))
    arrived = []
    for c, x in enumerate([first, *rest]):
        arrived.append(lax.ppermute(x if c < 2 else after(x, arrived[c - 2]), "pts", onward))

    ohi, olo, local = local_units(after(other, mhi), mhi, mlo)
    to_sum = lambda x: lax.all_to_all(x, "bas", 0, 0)
    kinds = [[("c", e, c, 0) for e in range(CHUNKS) for c in range(CHUNKS)]] + [step_units(c) for c in range(CHUNKS)]
    names = [[u[0] for u in k] for k in kinds]
    flat = [u for k in kinds[:EARLY] for u in k]
    per = -(-len(flat) // PTS)
    kind = jnp.array([u[3] for u in flat] + [0] * (per * PTS - len(flat)), jnp.int32).reshape(PTS, per)
    kind = jnp.sum(jnp.where(mine[:, None], kind, 0), axis=0)[None, :]
    source = jnp.where(kind == 0, block[:, None], jnp.where(kind == 1, block[:, None] ^ 1, partner[:, None]))
    source = source * per + jnp.arange(per)[None, :]
    source = jnp.where((kind == 2) & ~there[:, None], -1, source).reshape(-1)

    units = [local]
    parts = [to_sum(units[0])]

    def multiply(c, *first):
        units.append(arrived_units(c, mhi, mlo, ohi, olo, after(arrived[c], units[-1], *first)))
        parts.append(to_sum(units[-1]))

    multiply(0, flags, where, pick, source)
    multiply(1, parts[0])
    multiply(2, parts[1])
    held = [after(x, units[3]) for x in parts[:3]]
    multiply(3, *held)
    early = early_tiles(names[:EARLY], flags, held + parts[3:EARLY], per * PTS)
    spread = lax.all_to_all(early.reshape(PTS, per, SUB, LANES), "pts", 0, 0).reshape(PTS * per, SUB, LANES)
    slots = [[], [], []]
    late_at = {}
    for u, (name, e, c, owner) in enumerate(kinds[EARLY]):
        late_at[(name, e, c)] = (owner, len(slots[owner]))
        slots[owner].append((u, name))
    size = max(len(x) for x in slots)
    early_at = {u[:3]: (n // per, size + n % per) for n, u in enumerate(flat)}
    got = lax.all_to_all(sendings(slots, flags, pick, source, parts[EARLY], spread), "pts", 0, 0)
    return final_tiles(early_at, late_at, where, got)[None]


def solution(mesh):
    return jax.shard_map(
        body,
        mesh=mesh,
        in_specs=(P("bas", "pts"), P(), P()),
        out_specs=P("pts", None, "bas", None),
        check_vma=False,
    )
```

```python
import functools

import jax
import jax.numpy as jnp
from jax import lax
from jax.experimental import pallas as pl
from jax.experimental.pallas import tpu as pltpu
from jax.sharding import PartitionSpec as P

PB = 512
SHARE = 32
LANES = 128
SUB = 8
CHUNKS = PB // LANES
GROUP = LANES // SUB
PTS = 16
VMEM = 14 * 1024 * 1024
WIDE = 48 * 1024 * 1024
F32 = jnp.float32
BF16 = jnp.bfloat16
NT = (((1,), (1,)), ((), ()))
NN = (((1,), (0,)), ((), ()))


def whole(x):
    return pltpu.with_memory_space_constraint(x, pltpu.VMEM)


def in_hbm(x):
    return pltpu.with_memory_space_constraint(x, pltpu.HBM)


IN_VMEM = pl.BlockSpec(memory_space=pltpu.VMEM)
IN_SMEM = pl.BlockSpec(memory_space=pltpu.SMEM)
FLAG = {"c": 0, "am": 1, "ar": 1, "b": 2}
EARLY = 4


def dot(a, b, dims):
    return lax.dot_general(a, b, dims, preferred_element_type=F32)


def split2(x):
    hi = x.astype(BF16)
    return hi, (x - hi.astype(F32)).astype(BF16)


def row_block(depth, most=768):
    for size in (768, 640, 512, 384, 256, 128):
        if size <= most and depth % size == 0:
            return size
    return depth


ANY = pl.BlockSpec(memory_space=pl.ANY)


def piece(k, rows):
    return pl.ds(pl.multiple_of(k * rows, rows), rows)


class Flow:
    def __init__(self, src, dst, sems, count):
        self.src, self.dst, self.sems, self.count = src, dst, sems, count

    def copy(self, k):
        return pltpu.make_async_copy(self.src(k), self.dst(k), self.sems.at[k])

    def start(self):
        for k in range(self.count):
            self.copy(k).start()

    def wait(self):
        for k in range(self.count):
            self.copy(k).wait()


def by_rows(src, dst, sems, rows, count):
    return Flow(lambda k: src.at[piece(k, rows)], lambda k: dst.at[piece(k, rows)], sems, count)


def by_lanes(src, dst, sems, rows, count):
    return Flow(lambda k: src.at[:, piece(k, rows)], lambda k: dst.at[:, piece(k, rows)], sems, count)


def start_all(flows):
    for k in range(flows[0].count):
        for flow in flows:
            flow.copy(k).start()


def turned(x):
    t = x.T
    return jnp.swapaxes(t.reshape(GROUP, CHUNKS, SUB, t.shape[1]), 0, 1).reshape(t.shape)


def turned_back(t):
    x = jnp.swapaxes(t.reshape(CHUNKS, GROUP, SUB, t.shape[1]), 0, 1).reshape(t.shape)
    return x.T


def first_kernel(count, rows, x_hbm, out_hbm, x_ref, out_ref, in_sems, out_sems):
    coming = by_rows(x_hbm, x_ref, in_sems, rows, count)
    going = by_rows(out_ref, out_hbm, out_sems, rows, count)
    coming.start()

    @pl.loop(0, count)
    def _(k):
        coming.copy(k).wait()
        out_ref[piece(k, rows)] = turned(x_ref[piece(k, rows)])[:LANES].T
        going.copy(k).start()

    going.wait()


def first_chunk(x):
    depth = x.shape[0]
    rows = row_block(depth)
    count = depth // rows
    return pl.pallas_call(
        functools.partial(first_kernel, count, rows),
        in_specs=[ANY],
        out_specs=ANY,
        out_shape=pltpu.HBM((depth, LANES), F32),
        scratch_shapes=[
            pltpu.VMEM((depth, PB), F32),
            pltpu.VMEM((depth, LANES), F32),
            pltpu.SemaphoreType.DMA((count,)),
            pltpu.SemaphoreType.DMA((count,)),
        ],
        compiler_params=pltpu.CompilerParams(vmem_limit_bytes=WIDE),
        cost_estimate=pl.CostEstimate(flops=6 * depth * PB * LANES, bytes_accessed=4 * depth * (PB + LANES), transcendentals=0),
        name="first_chunk",
    )(in_hbm(x))


def prep_kernel(count, rows, x_hbm, *refs):
    out_hbm, turned_hbm = refs[:CHUNKS - 1], refs[CHUNKS - 1:CHUNKS + 1]
    x_ref, out_ref, hi_ref, lo_ref, in_sems, out_sems = refs[CHUNKS + 1:]
    coming = by_rows(x_hbm, x_ref, in_sems, rows, count)
    going = [by_rows(out_ref.at[n], out_hbm[n], out_sems.at[n], rows, count) for n in range(CHUNKS - 1)]
    going += [
        by_lanes(ref, turned_hbm[n], out_sems.at[CHUNKS - 1 + n], rows, count) for n, ref in enumerate((hi_ref, lo_ref))
    ]
    coming.start()

    @pl.loop(0, count)
    def _(k):
        coming.copy(k).wait()
        at = piece(k, rows)
        t = turned(x_ref[at])
        hi_ref[:, at], lo_ref[:, at] = split2(t)
        for n in range(CHUNKS - 1):
            out_ref[n, at] = t[(n + 1) * LANES:(n + 2) * LANES].T
        for flow in going:
            flow.copy(k).start()

    for flow in going:
        flow.wait()


def prepared(x):
    depth = x.shape[0]
    rows = row_block(depth, 384)
    count = depth // rows
    got = pl.pallas_call(
        functools.partial(prep_kernel, count, rows),
        in_specs=[ANY],
        out_specs=[ANY] * (CHUNKS + 1),
        out_shape=[pltpu.HBM((depth, LANES), F32)] * (CHUNKS - 1) + [pltpu.HBM((PB, depth), BF16)] * 2,
        scratch_shapes=[
            pltpu.VMEM((depth, PB), F32),
            pltpu.VMEM((CHUNKS - 1, depth, LANES), F32),
            pltpu.VMEM((PB, depth), BF16),
            pltpu.VMEM((PB, depth), BF16),
            pltpu.SemaphoreType.DMA((count,)),
            pltpu.SemaphoreType.DMA((CHUNKS + 1, count)),
        ],
        compiler_params=pltpu.CompilerParams(vmem_limit_bytes=WIDE),
        cost_estimate=pl.CostEstimate(flops=9 * depth * PB * PB, bytes_accessed=14 * depth * PB, transcendentals=0),
        name="prepared",
    )(in_hbm(x))
    return got[:CHUNKS - 1], got[CHUNKS - 1], got[CHUNKS]


def local_kernel(
    count, rows, o_hbm, mhi_hbm, mlo_hbm, ohi_hbm, olo_hbm, out_ref,
    o_ref, mhi_ref, mlo_ref, ohi_ref, olo_ref, acc_ref, in_sems, out_sems,
):
    coming = [
        by_rows(o_hbm, o_ref, in_sems.at[0], rows, count),
        by_lanes(mhi_hbm, mhi_ref, in_sems.at[1], rows, count),
        by_lanes(mlo_hbm, mlo_ref, in_sems.at[2], rows, count),
    ]
    going = [
        by_lanes(ohi_ref, ohi_hbm, out_sems.at[0], rows, count),
        by_lanes(olo_ref, olo_hbm, out_sems.at[1], rows, count),
    ]
    start_all(coming)
    acc_ref[...] = jnp.zeros_like(acc_ref)

    @pl.loop(0, count)
    def _(k):
        at = piece(k, rows)
        for flow in coming:
            flow.copy(k).wait()
        ohi, olo = split2(turned(o_ref[at]))
        ohi_ref[:, at] = ohi
        olo_ref[:, at] = olo
        mhi = mhi_ref[:, at]
        acc_ref[...] += dot(mhi, ohi, NT) + dot(mhi, olo, NT) + dot(mlo_ref[:, at], ohi, NT)
        for flow in going:
            flow.copy(k).start()

    for e in range(CHUNKS):
        for c in range(CHUNKS):
            put(out_ref, CHUNKS * e + c, acc_ref[e * LANES:(e + 1) * LANES, c * LANES:(c + 1) * LANES])
    for flow in going:
        flow.wait()


def local_units(other, mhi, mlo):
    depth = other.shape[0]
    rows = row_block(depth)
    count = depth // rows
    units = CHUNKS * CHUNKS
    wide = pltpu.VMEM((PB, depth), BF16)
    return pl.pallas_call(
        functools.partial(local_kernel, count, rows),
        in_specs=[ANY] * 3,
        out_specs=[ANY, ANY, pl.BlockSpec((GROUP, units, SUB, LANES))],
        out_shape=[pltpu.HBM((PB, depth), BF16)] * 2 + [pltpu.HBM((GROUP, units, SUB, LANES), F32)],
        scratch_shapes=[
            pltpu.VMEM((depth, PB), F32), wide, wide, wide, wide,
            pltpu.VMEM((PB, PB), F32),
            pltpu.SemaphoreType.DMA((3, count)),
            pltpu.SemaphoreType.DMA((2, count)),
        ],
        compiler_params=pltpu.CompilerParams(vmem_limit_bytes=WIDE),
        cost_estimate=pl.CostEstimate(flops=10 * depth * PB * PB, bytes_accessed=12 * depth * PB, transcendentals=0),
        name="local_units",
    )(in_hbm(other), in_hbm(mhi), in_hbm(mlo))


def put(out_ref, unit, block):
    out_ref[:, unit] = block.reshape(GROUP, SUB, LANES)


IN_VMEM = pl.BlockSpec(memory_space=pltpu.VMEM)
IN_SMEM = pl.BlockSpec(memory_space=pltpu.SMEM)
FLAG = {"c": 0, "am": 1, "ar": 1, "b": 2}
EARLY = 4


def step_units(c):
    units = [("am", e, c, 0) for e in range(CHUNKS)]
    units += [("ar", c, e, 2) for e in range(CHUNKS)]
    units += [("b", e, c, 1) for e in range(c, CHUNKS)]
    units += [("b", c, e, 2) for e in range(c + 1, CHUNKS)]
    return units


def step_kernel(
    c, count, rows, mhi_hbm, mlo_hbm, ohi_hbm, olo_hbm, r_hbm, out_ref,
    hi_ref, lo_ref, r_ref, wide_ref, slim_ref, sems,
):
    left = (CHUNKS - c) * LANES

    def lanes(src, dst, sem, first, base, n):
        return Flow(
            lambda k: src.at[pl.ds(first, n), piece(k, rows)], lambda k: dst.at[pl.ds(base, n), piece(k, rows)], sem, count
        )

    coming = [
        by_rows(r_hbm, r_ref, sems.at[0], rows, count),
        lanes(mhi_hbm, hi_ref, sems.at[1], 0, 0, PB),
        lanes(ohi_hbm, hi_ref, sems.at[2], PB - left, PB, left),
        lanes(mlo_hbm, lo_ref, sems.at[3], 0, 0, PB),
        lanes(olo_hbm, lo_ref, sems.at[4], PB - left, PB, left),
    ]
    start_all(coming)
    wide_ref[...] = jnp.zeros_like(wide_ref)
    slim_ref[...] = jnp.zeros_like(slim_ref)

    @pl.loop(0, count)
    def _(k):
        at = piece(k, rows)
        for flow in coming:
            flow.copy(k).wait()
        rhi, rlo = split2(r_ref[at])
        wide_ref[...] += dot(hi_ref[:, at], jnp.concatenate([rhi, rlo], axis=1), NN)
        slim_ref[...] += dot(lo_ref[:, at], rhi, NN)

    def block(n):
        rows = slice(n * LANES, (n + 1) * LANES)
        return wide_ref[rows, :LANES] + (wide_ref[rows, LANES:] + slim_ref[rows])

    for e in range(CHUNKS):
        a = block(e)
        put(out_ref, e, a)
        put(out_ref, CHUNKS + e, a.T)
    for e in range(c, CHUNKS):
        b = block(CHUNKS + e - c)
        put(out_ref, 2 * CHUNKS + e - c, b)
        if e > c:
            put(out_ref, 3 * CHUNKS + e - 2 * c - 1, b.T)


def arrived_units(c, mhi, mlo, ohi, olo, r):
    depth = r.shape[0]
    rows = row_block(depth)
    count = depth // rows
    units = len(step_units(c))
    lines = PB + (CHUNKS - c) * LANES
    return pl.pallas_call(
        functools.partial(step_kernel, c, count, rows),
        in_specs=[ANY] * 5,
        out_specs=pl.BlockSpec((GROUP, units, SUB, LANES)),
        out_shape=pltpu.HBM((GROUP, units, SUB, LANES), F32),
        scratch_shapes=[
            pltpu.VMEM((lines, depth), BF16),
            pltpu.VMEM((lines, depth), BF16),
            pltpu.VMEM((depth, LANES), F32),
            pltpu.VMEM((lines, 2 * LANES), F32),
            pltpu.VMEM((lines, LANES), F32),
            pltpu.SemaphoreType.DMA((5, count)),
        ],
        compiler_params=pltpu.CompilerParams(vmem_limit_bytes=WIDE),
        cost_estimate=pl.CostEstimate(
            flops=6 * depth * lines * LANES, bytes_accessed=4 * depth * (lines + LANES), transcendentals=0
        ),
        name="arrived_units",
    )(in_hbm(mhi), in_hbm(mlo), in_hbm(ohi), in_hbm(olo), in_hbm(r))


def squares(parts_ref, unit, flag):
    gram = parts_ref[0, unit]
    for n in range(1, GROUP):
        gram = gram + parts_ref[n, unit]
    return jnp.where(flag != 0, gram * gram, 0.0)


def early_kernel(names, flags_ref, *refs):
    part_refs, out_ref = refs[:-1], refs[-1]
    n = 0
    for part_ref, units in zip(part_refs, names):
        for u, name in enumerate(units):
            out_ref[n] = squares(part_ref, u, flags_ref[FLAG[name]])
            n += 1
    for pad in range(n, out_ref.shape[0]):
        out_ref[pad] = jnp.zeros((SUB, LANES), F32)


def early_tiles(names, flags, parts, count):
    return pl.pallas_call(
        functools.partial(early_kernel, names),
        in_specs=[IN_SMEM] + [IN_VMEM] * len(parts),
        out_specs=IN_VMEM,
        out_shape=pltpu.HBM((count, SUB, LANES), F32),
        compiler_params=pltpu.CompilerParams(vmem_limit_bytes=VMEM),
        name="early_tiles",
    )(flags, *[whole(x) for x in parts])


def send_kernel(slots, flags_ref, pick_ref, source_ref, parts_ref, spread_ref, out_ref, held_ref):
    size = held_ref.shape[1]
    per = out_ref.shape[1] - size
    for kind, units in enumerate(slots):
        for n, (u, name) in enumerate(units):
            held_ref[kind, n] = squares(parts_ref, u, flags_ref[FLAG[name]])
        for n in range(len(units), size):
            held_ref[kind, n] = jnp.zeros((SUB, LANES), F32)

    @pl.loop(0, PTS)
    def _(k):
        out_ref[k, :size] = held_ref[pick_ref[k]]
        for n in range(per):
            at = source_ref[k * per + n]
            out_ref[k, size + n] = jnp.where(at >= 0, spread_ref[jnp.maximum(at, 0)], 0.0)


def sendings(slots, flags, pick, source, parts, spread):
    size = max(len(units) for units in slots)
    per = spread.shape[0] // PTS
    return pl.pallas_call(
        functools.partial(send_kernel, slots),
        in_specs=[IN_SMEM] * 3 + [IN_VMEM] * 2,
        out_specs=IN_VMEM,
        out_shape=jax.ShapeDtypeStruct((PTS, size + per, SUB, LANES), F32),
        scratch_shapes=[pltpu.VMEM((len(slots), size, SUB, LANES), F32)],
        compiler_params=pltpu.CompilerParams(vmem_limit_bytes=VMEM),
        name="sendings",
    )(flags, pick, source, whole(parts), whole(spread))


def final_kernel(early_at, late_at, where_ref, got_ref, out_ref):
    def unit(name, e, c):
        if (name, e, c) in early_at:
            return got_ref[early_at[(name, e, c)]]
        kind, slot = late_at[(name, e, c)]
        got = got_ref[where_ref[1 + kind], slot]
        return jnp.where(where_ref[4] != 0, got, 0.0) if kind == 2 else got

    groups = ("c", "am", "b", "ar")
    sides = [jnp.concatenate([unit(g, e, c) for g in groups for e in range(CHUNKS)], axis=0).T for c in range(CHUNKS)]
    placed = turned_back(jnp.concatenate(sides, axis=0))
    for g in range(len(groups)):
        out_ref[lax.rem(g + 2 * where_ref[0], 4)] = placed[g * SHARE:(g + 1) * SHARE]


def final_tiles(early_at, late_at, where, got):
    return pl.pallas_call(
        functools.partial(final_kernel, early_at, late_at),
        in_specs=[IN_SMEM, IN_VMEM],
        out_specs=IN_VMEM,
        out_shape=jax.ShapeDtypeStruct((4, SHARE, PB), F32),
        compiler_params=pltpu.CompilerParams(vmem_limit_bytes=VMEM),
        name="final_tiles",
    )(where, whole(got))


def after(x, *others):
    return lax.optimization_barrier((x,) + others)[0]


def body(orbitals, owner_perm, pair_reach):
    me = lax.axis_index("pts")
    chips = PTS // 2
    swap = [(p, p ^ 1) for p in range(PTS)]
    onward = [(2 * z, 2 * z - 2) for z in range(1, chips)] + [(2 * z + 1, 2 * z + 3) for z in range(chips - 1)]

    ids = jnp.arange(PTS, dtype=jnp.int32)
    three = jnp.arange(3, dtype=jnp.int32)[:, None]
    first_of = me + (three == 2) - (me % 2) * (three + 1)
    apart = (three == 1).astype(jnp.int32)
    live = (ids == first_of) & (apart < pair_reach[None, :]) & (ids + apart + 1 < PTS)
    flags = jnp.sum(live.astype(jnp.int32), axis=1)
    block = jnp.sum(jnp.where(owner_perm[:, None] == ids[None, :], ids[:, None], 0), axis=0)
    partner = block - 2 + 4 * (block % 2)
    there = (partner >= 0) & (partner < PTS)
    partner = jnp.clip(partner, 0, PTS - 1)
    mine = ids == me
    five = jnp.arange(5, dtype=jnp.int32)[:, None]
    facts = jnp.where(five == 0, block % 2, jnp.where(five == 1, block, jnp.where(five == 2, block ^ 1, partner)))
    facts = jnp.where(five == 4, there.astype(jnp.int32), facts)
    where = jnp.sum(jnp.where(mine, facts, 0), axis=1)
    pick = jnp.where(block == me, 0, jnp.where(block == (me ^ 1), 1, 2))

    first = first_chunk(orbitals)
    other = lax.ppermute(after(orbitals, first), "pts", swap)
    rest, mhi, mlo = prepared(after(orbitals, first))
    arrived = []
    for c, x in enumerate([first, *rest]):
        arrived.append(lax.ppermute(x if c < 2 else after(x, arrived[c - 2]), "pts", onward))

    ohi, olo, local = local_units(after(other, mhi), mhi, mlo)
    to_sum = lambda x: lax.all_to_all(x, "bas", 0, 0)
    kinds = [[("c", e, c, 0) for e in range(CHUNKS) for c in range(CHUNKS)]] + [step_units(c) for c in range(CHUNKS)]
    names = [[u[0] for u in k] for k in kinds]
    flat = [u for k in kinds[:EARLY] for u in k]
    per = -(-len(flat) // PTS)
    kind = jnp.array([u[3] for u in flat] + [0] * (per * PTS - len(flat)), jnp.int32).reshape(PTS, per)
    kind = jnp.sum(jnp.where(mine[:, None], kind, 0), axis=0)[None, :]
    source = jnp.where(kind == 0, block[:, None], jnp.where(kind == 1, block[:, None] ^ 1, partner[:, None]))
    source = source * per + jnp.arange(per)[None, :]
    source = jnp.where((kind == 2) & ~there[:, None], -1, source).reshape(-1)

    units = [local]
    parts = [to_sum(units[0])]

    def multiply(c, *first):
        units.append(arrived_units(c, mhi, mlo, ohi, olo, after(arrived[c], units[-1], *first)))
        parts.append(to_sum(units[-1]))

    multiply(0, flags, where, pick, source)
    multiply(1, parts[0])
    multiply(2, parts[1])
    held = [after(x, units[3]) for x in parts[:3]]
    multiply(3, *held)
    early = early_tiles(names[:EARLY], flags, held + parts[3:EARLY], per * PTS)
    spread = lax.all_to_all(early.reshape(PTS, per, SUB, LANES), "pts", 0, 0).reshape(PTS * per, SUB, LANES)
    slots = [[], [], []]
    late_at = {}
    for u, (name, e, c, owner) in enumerate(kinds[EARLY]):
        late_at[(name, e, c)] = (owner, len(slots[owner]))
        slots[owner].append((u, name))
    size = max(len(x) for x in slots)
    early_at = {u[:3]: (n // per, size + n % per) for n, u in enumerate(flat)}
    got = lax.all_to_all(sendings(slots, flags, pick, source, parts[EARLY], spread), "pts", 0, 0)
    return final_tiles(early_at, late_at, where, got)[None]


def solution(mesh):
    return jax.shard_map(
        body,
        mesh=mesh,
        in_specs=(P("bas", "pts"), P(), P()),
        out_specs=P("pts", None, "bas", None),
        check_vma=False,
    )
```

```python
import functools

import jax
import jax.numpy as jnp
from jax import lax
from jax.experimental import pallas as pl
from jax.experimental.pallas import tpu as pltpu
from jax.sharding import PartitionSpec as P

PB = 512
SHARE = 32
LANES = 128
SUB = 8
CHUNKS = PB // LANES
GROUP = LANES // SUB
PTS = 16
VMEM = 14 * 1024 * 1024
WIDE = 48 * 1024 * 1024
F32 = jnp.float32
BF16 = jnp.bfloat16
NT = (((1,), (1,)), ((), ()))
NN = (((1,), (0,)), ((), ()))


def whole(x):
    return pltpu.with_memory_space_constraint(x, pltpu.VMEM)


def in_hbm(x):
    return pltpu.with_memory_space_constraint(x, pltpu.HBM)


IN_VMEM = pl.BlockSpec(memory_space=pltpu.VMEM)
IN_SMEM = pl.BlockSpec(memory_space=pltpu.SMEM)
FLAG = {"c": 0, "am": 1, "ar": 1, "b": 2}
EARLY = 3


def dot(a, b, dims):
    return lax.dot_general(a, b, dims, preferred_element_type=F32)


def split2(x):
    hi = x.astype(BF16)
    return hi, (x - hi.astype(F32)).astype(BF16)


def row_block(depth, most=768):
    for size in (768, 640, 512, 384, 256, 128):
        if size <= most and depth % size == 0:
            return size
    return depth


ANY = pl.BlockSpec(memory_space=pl.ANY)


def piece(k, rows):
    return pl.ds(pl.multiple_of(k * rows, rows), rows)


class Flow:
    def __init__(self, src, dst, sems, count):
        self.src, self.dst, self.sems, self.count = src, dst, sems, count

    def copy(self, k):
        return pltpu.make_async_copy(self.src(k), self.dst(k), self.sems.at[k])

    def start(self):
        for k in range(self.count):
            self.copy(k).start()

    def wait(self):
        for k in range(self.count):
            self.copy(k).wait()


def by_rows(src, dst, sems, rows, count):
    return Flow(lambda k: src.at[piece(k, rows)], lambda k: dst.at[piece(k, rows)], sems, count)


def by_lanes(src, dst, sems, rows, count):
    return Flow(lambda k: src.at[:, piece(k, rows)], lambda k: dst.at[:, piece(k, rows)], sems, count)


def start_all(flows):
    for k in range(flows[0].count):
        for flow in flows:
            flow.copy(k).start()


def turned(x):
    t = x.T
    return jnp.swapaxes(t.reshape(GROUP, CHUNKS, SUB, t.shape[1]), 0, 1).reshape(t.shape)


def turned_back(t):
    x = jnp.swapaxes(t.reshape(CHUNKS, GROUP, SUB, t.shape[1]), 0, 1).reshape(t.shape)
    return x.T


def first_kernel(count, rows, x_hbm, out_hbm, x_ref, out_ref, in_sems, out_sems):
    coming = by_rows(x_hbm, x_ref, in_sems, rows, count)
    going = by_rows(out_ref, out_hbm, out_sems, rows, count)
    coming.start()

    @pl.loop(0, count)
    def _(k):
        coming.copy(k).wait()
        out_ref[piece(k, rows)] = turned(x_ref[piece(k, rows)])[:LANES].T
        going.copy(k).start()

    going.wait()


def first_chunk(x):
    depth = x.shape[0]
    rows = row_block(depth)
    count = depth // rows
    return pl.pallas_call(
        functools.partial(first_kernel, count, rows),
        in_specs=[ANY],
        out_specs=ANY,
        out_shape=pltpu.HBM((depth, LANES), F32),
        scratch_shapes=[
            pltpu.VMEM((depth, PB), F32),
            pltpu.VMEM((depth, LANES), F32),
            pltpu.SemaphoreType.DMA((count,)),
            pltpu.SemaphoreType.DMA((count,)),
        ],
        compiler_params=pltpu.CompilerParams(vmem_limit_bytes=WIDE),
        cost_estimate=pl.CostEstimate(flops=6 * depth * PB * LANES, bytes_accessed=4 * depth * (PB + LANES), transcendentals=0),
        name="first_chunk",
    )(in_hbm(x))


def prep_kernel(count, rows, x_hbm, *refs):
    out_hbm, turned_hbm = refs[:CHUNKS - 1], refs[CHUNKS - 1:CHUNKS + 1]
    x_ref, out_ref, hi_ref, lo_ref, in_sems, out_sems = refs[CHUNKS + 1:]
    coming = by_rows(x_hbm, x_ref, in_sems, rows, count)
    going = [by_rows(out_ref.at[n], out_hbm[n], out_sems.at[n], rows, count) for n in range(CHUNKS - 1)]
    going += [
        by_lanes(ref, turned_hbm[n], out_sems.at[CHUNKS - 1 + n], rows, count) for n, ref in enumerate((hi_ref, lo_ref))
    ]
    coming.start()

    @pl.loop(0, count)
    def _(k):
        coming.copy(k).wait()
        at = piece(k, rows)
        t = turned(x_ref[at])
        hi_ref[:, at], lo_ref[:, at] = split2(t)
        for n in range(CHUNKS - 1):
            out_ref[n, at] = t[(n + 1) * LANES:(n + 2) * LANES].T
        for flow in going:
            flow.copy(k).start()

    for flow in going:
        flow.wait()


def prepared(x):
    depth = x.shape[0]
    rows = row_block(depth, 384)
    count = depth // rows
    got = pl.pallas_call(
        functools.partial(prep_kernel, count, rows),
        in_specs=[ANY],
        out_specs=[ANY] * (CHUNKS + 1),
        out_shape=[pltpu.HBM((depth, LANES), F32)] * (CHUNKS - 1) + [pltpu.HBM((PB, depth), BF16)] * 2,
        scratch_shapes=[
            pltpu.VMEM((depth, PB), F32),
            pltpu.VMEM((CHUNKS - 1, depth, LANES), F32),
            pltpu.VMEM((PB, depth), BF16),
            pltpu.VMEM((PB, depth), BF16),
            pltpu.SemaphoreType.DMA((count,)),
            pltpu.SemaphoreType.DMA((CHUNKS + 1, count)),
        ],
        compiler_params=pltpu.CompilerParams(vmem_limit_bytes=WIDE),
        cost_estimate=pl.CostEstimate(flops=9 * depth * PB * PB, bytes_accessed=14 * depth * PB, transcendentals=0),
        name="prepared",
    )(in_hbm(x))
    return got[:CHUNKS - 1], got[CHUNKS - 1], got[CHUNKS]


def local_kernel(
    count, rows, o_hbm, mhi_hbm, mlo_hbm, ohi_hbm, olo_hbm, out_ref,
    o_ref, mhi_ref, mlo_ref, ohi_ref, olo_ref, acc_ref, in_sems, out_sems,
):
    coming = [
        by_rows(o_hbm, o_ref, in_sems.at[0], rows, count),
        by_lanes(mhi_hbm, mhi_ref, in_sems.at[1], rows, count),
        by_lanes(mlo_hbm, mlo_ref, in_sems.at[2], rows, count),
    ]
    going = [
        by_lanes(ohi_ref, ohi_hbm, out_sems.at[0], rows, count),
        by_lanes(olo_ref, olo_hbm, out_sems.at[1], rows, count),
    ]
    start_all(coming)
    acc_ref[...] = jnp.zeros_like(acc_ref)

    @pl.loop(0, count)
    def _(k):
        at = piece(k, rows)
        for flow in coming:
            flow.copy(k).wait()
        ohi, olo = split2(turned(o_ref[at]))
        ohi_ref[:, at] = ohi
        olo_ref[:, at] = olo
        mhi = mhi_ref[:, at]
        acc_ref[...] += dot(mhi, ohi, NT) + dot(mhi, olo, NT) + dot(mlo_ref[:, at], ohi, NT)
        for flow in going:
            flow.copy(k).start()

    for e in range(CHUNKS):
        for c in range(CHUNKS):
            put(out_ref, CHUNKS * e + c, acc_ref[e * LANES:(e + 1) * LANES, c * LANES:(c + 1) * LANES])
    for flow in going:
        flow.wait()


def local_units(other, mhi, mlo):
    depth = other.shape[0]
    rows = row_block(depth)
    count = depth // rows
    units = CHUNKS * CHUNKS
    wide = pltpu.VMEM((PB, depth), BF16)
    return pl.pallas_call(
        functools.partial(local_kernel, count, rows),
        in_specs=[ANY] * 3,
        out_specs=[ANY, ANY, pl.BlockSpec((GROUP, units, SUB, LANES))],
        out_shape=[pltpu.HBM((PB, depth), BF16)] * 2 + [pltpu.HBM((GROUP, units, SUB, LANES), F32)],
        scratch_shapes=[
            pltpu.VMEM((depth, PB), F32), wide, wide, wide, wide,
            pltpu.VMEM((PB, PB), F32),
            pltpu.SemaphoreType.DMA((3, count)),
            pltpu.SemaphoreType.DMA((2, count)),
        ],
        compiler_params=pltpu.CompilerParams(vmem_limit_bytes=WIDE),
        cost_estimate=pl.CostEstimate(flops=10 * depth * PB * PB, bytes_accessed=12 * depth * PB, transcendentals=0),
        name="local_units",
    )(in_hbm(other), in_hbm(mhi), in_hbm(mlo))


def put(out_ref, unit, block):
    out_ref[:, unit] = block.reshape(GROUP, SUB, LANES)


IN_VMEM = pl.BlockSpec(memory_space=pltpu.VMEM)
IN_SMEM = pl.BlockSpec(memory_space=pltpu.SMEM)
FLAG = {"c": 0, "am": 1, "ar": 1, "b": 2}
EARLY = 3


def step_units(c):
    units = [("am", e, c, 0) for e in range(CHUNKS)]
    units += [("ar", c, e, 2) for e in range(CHUNKS)]
    units += [("b", e, c, 1) for e in range(c, CHUNKS)]
    units += [("b", c, e, 2) for e in range(c + 1, CHUNKS)]
    return units


def step_kernel(
    c, count, rows, mhi_hbm, mlo_hbm, ohi_hbm, olo_hbm, r_hbm, out_ref,
    hi_ref, lo_ref, r_ref, wide_ref, slim_ref, sems,
):
    left = (CHUNKS - c) * LANES

    def lanes(src, dst, sem, first, base, n):
        return Flow(
            lambda k: src.at[pl.ds(first, n), piece(k, rows)], lambda k: dst.at[pl.ds(base, n), piece(k, rows)], sem, count
        )

    coming = [
        by_rows(r_hbm, r_ref, sems.at[0], rows, count),
        lanes(mhi_hbm, hi_ref, sems.at[1], 0, 0, PB),
        lanes(ohi_hbm, hi_ref, sems.at[2], PB - left, PB, left),
        lanes(mlo_hbm, lo_ref, sems.at[3], 0, 0, PB),
        lanes(olo_hbm, lo_ref, sems.at[4], PB - left, PB, left),
    ]
    start_all(coming)
    wide_ref[...] = jnp.zeros_like(wide_ref)
    slim_ref[...] = jnp.zeros_like(slim_ref)

    @pl.loop(0, count)
    def _(k):
        at = piece(k, rows)
        for flow in coming:
            flow.copy(k).wait()
        rhi, rlo = split2(r_ref[at])
        wide_ref[...] += dot(hi_ref[:, at], jnp.concatenate([rhi, rlo], axis=1), NN)
        slim_ref[...] += dot(lo_ref[:, at], rhi, NN)

    def block(n):
        rows = slice(n * LANES, (n + 1) * LANES)
        return wide_ref[rows, :LANES] + (wide_ref[rows, LANES:] + slim_ref[rows])

    for e in range(CHUNKS):
        a = block(e)
        put(out_ref, e, a)
        put(out_ref, CHUNKS + e, a.T)
    for e in range(c, CHUNKS):
        b = block(CHUNKS + e - c)
        put(out_ref, 2 * CHUNKS + e - c, b)
        if e > c:
            put(out_ref, 3 * CHUNKS + e - 2 * c - 1, b.T)


def arrived_units(c, mhi, mlo, ohi, olo, r):
    depth = r.shape[0]
    rows = row_block(depth)
    count = depth // rows
    units = len(step_units(c))
    lines = PB + (CHUNKS - c) * LANES
    return pl.pallas_call(
        functools.partial(step_kernel, c, count, rows),
        in_specs=[ANY] * 5,
        out_specs=pl.BlockSpec((GROUP, units, SUB, LANES)),
        out_shape=pltpu.HBM((GROUP, units, SUB, LANES), F32),
        scratch_shapes=[
            pltpu.VMEM((lines, depth), BF16),
            pltpu.VMEM((lines, depth), BF16),
            pltpu.VMEM((depth, LANES), F32),
            pltpu.VMEM((lines, 2 * LANES), F32),
            pltpu.VMEM((lines, LANES), F32),
            pltpu.SemaphoreType.DMA((5, count)),
        ],
        compiler_params=pltpu.CompilerParams(vmem_limit_bytes=WIDE),
        cost_estimate=pl.CostEstimate(
            flops=6 * depth * lines * LANES, bytes_accessed=4 * depth * (lines + LANES), transcendentals=0
        ),
        name="arrived_units",
    )(in_hbm(mhi), in_hbm(mlo), in_hbm(ohi), in_hbm(olo), in_hbm(r))


def squares(parts_ref, unit, flag):
    gram = parts_ref[0, unit]
    for n in range(1, GROUP):
        gram = gram + parts_ref[n, unit]
    return jnp.where(flag != 0, gram * gram, 0.0)


def early_kernel(names, flags_ref, *refs):
    part_refs, out_ref = refs[:-1], refs[-1]
    n = 0
    for part_ref, units in zip(part_refs, names):
        for u, name in enumerate(units):
            out_ref[n] = squares(part_ref, u, flags_ref[FLAG[name]])
            n += 1


def early_tiles(names, flags, parts):
    count = sum(len(units) for units in names)
    return pl.pallas_call(
        functools.partial(early_kernel, names),
        in_specs=[IN_SMEM] + [IN_VMEM] * len(parts),
        out_specs=IN_VMEM,
        out_shape=pltpu.HBM((count, SUB, LANES), F32),
        compiler_params=pltpu.CompilerParams(vmem_limit_bytes=VMEM),
        name="early_tiles",
    )(flags, *[whole(x) for x in parts])


def send_kernel(slots, flags_ref, pick_ref, *refs):
    part_refs, out_ref, held_ref = refs[:-2], refs[-2], refs[-1]
    size = held_ref.shape[1]
    for kind, units in enumerate(slots):
        for n, (part, u, name) in enumerate(units):
            held_ref[kind, n] = squares(part_refs[part], u, flags_ref[FLAG[name]])
        for n in range(len(units), size):
            held_ref[kind, n] = jnp.zeros((SUB, LANES), F32)

    @pl.loop(0, PTS)
    def _(k):
        out_ref[k] = held_ref[pick_ref[k]]


def sendings(slots, flags, pick, parts):
    size = max(len(units) for units in slots)
    return pl.pallas_call(
        functools.partial(send_kernel, slots),
        in_specs=[IN_SMEM] * 2 + [IN_VMEM] * len(parts),
        out_specs=IN_VMEM,
        out_shape=jax.ShapeDtypeStruct((PTS, size, SUB, LANES), F32),
        scratch_shapes=[pltpu.VMEM((len(slots), size, SUB, LANES), F32)],
        compiler_params=pltpu.CompilerParams(vmem_limit_bytes=VMEM),
        name="sendings",
    )(flags, pick, *[whole(x) for x in parts])


def final_kernel(early_at, late_at, where_ref, early_hbm, late_ref, out_ref, early_ref, sems):
    copies = [
        pltpu.make_async_copy(early_hbm.at[where_ref[1 + kind]], early_ref.at[kind], sems.at[kind]) for kind in range(3)
    ]
    for copy in copies:
        copy.start()
    for copy in copies:
        copy.wait()

    def unit(name, e, c):
        here = early_at.get((name, e, c))
        if here is not None:
            kind, got = here[0], early_ref[here]
        else:
            kind, slot = late_at[(name, e, c)]
            got = late_ref[where_ref[1 + kind], slot]
        return jnp.where(where_ref[4] != 0, got, 0.0) if kind == 2 else got

    groups = ("c", "am", "b", "ar")
    sides = [jnp.concatenate([unit(g, e, c) for g in groups for e in range(CHUNKS)], axis=0).T for c in range(CHUNKS)]
    placed = turned_back(jnp.concatenate(sides, axis=0))
    for g in range(len(groups)):
        out_ref[lax.rem(g + 2 * where_ref[0], 4)] = placed[g * SHARE:(g + 1) * SHARE]


def final_tiles(early_at, late_at, where, early, late):
    return pl.pallas_call(
        functools.partial(final_kernel, early_at, late_at),
        in_specs=[IN_SMEM, ANY, IN_VMEM],
        out_specs=IN_VMEM,
        out_shape=jax.ShapeDtypeStruct((4, SHARE, PB), F32),
        scratch_shapes=[pltpu.VMEM((3,) + early.shape[1:], F32), pltpu.SemaphoreType.DMA((3,))],
        compiler_params=pltpu.CompilerParams(vmem_limit_bytes=VMEM),
        name="final_tiles",
    )(where, in_hbm(early), whole(late))


def after(x, *others):
    return lax.optimization_barrier((x,) + others)[0]


def body(orbitals, owner_perm, pair_reach):
    me = lax.axis_index("pts")
    chips = PTS // 2
    swap = [(p, p ^ 1) for p in range(PTS)]
    onward = [(2 * z, 2 * z - 2) for z in range(1, chips)] + [(2 * z + 1, 2 * z + 3) for z in range(chips - 1)]

    ids = jnp.arange(PTS, dtype=jnp.int32)
    three = jnp.arange(3, dtype=jnp.int32)[:, None]
    first_of = me + (three == 2) - (me % 2) * (three + 1)
    apart = (three == 1).astype(jnp.int32)
    live = (ids == first_of) & (apart < pair_reach[None, :]) & (ids + apart + 1 < PTS)
    flags = jnp.sum(live.astype(jnp.int32), axis=1)
    block = jnp.sum(jnp.where(owner_perm[:, None] == ids[None, :], ids[:, None], 0), axis=0)
    partner = block - 2 + 4 * (block % 2)
    there = (partner >= 0) & (partner < PTS)
    partner = jnp.clip(partner, 0, PTS - 1)
    mine = ids == me
    five = jnp.arange(5, dtype=jnp.int32)[:, None]
    facts = jnp.where(five == 0, block % 2, jnp.where(five == 1, block, jnp.where(five == 2, block ^ 1, partner)))
    facts = jnp.where(five == 4, there.astype(jnp.int32), facts)
    where = jnp.sum(jnp.where(mine, facts, 0), axis=1)
    pick = jnp.where(block == me, 0, jnp.where(block == (me ^ 1), 1, 2))

    first = first_chunk(orbitals)
    other = lax.ppermute(after(orbitals, first), "pts", swap)
    rest, mhi, mlo = prepared(after(orbitals, first))
    arrived = []
    for c, x in enumerate([first, *rest]):
        arrived.append(lax.ppermute(x if c < 2 else after(x, arrived[0]), "pts", onward))

    ohi, olo, local = local_units(after(other, mhi), mhi, mlo)
    to_sum = lambda x: lax.all_to_all(x, "bas", 0, 0)
    kinds = [[("c", e, c, 0) for e in range(CHUNKS) for c in range(CHUNKS)]] + [step_units(c) for c in range(CHUNKS)]
    names = [[u[0] for u in k] for k in kinds]
    units = [local]
    parts = [to_sum(units[0])]

    def multiply(c, *first):
        units.append(arrived_units(c, mhi, mlo, ohi, olo, after(arrived[c], units[-1], *first)))
        parts.append(to_sum(units[-1]))

    multiply(0, flags, where, pick)
    multiply(1, parts[0])
    multiply(2, parts[1])
    held = [after(x, units[3], arrived[3]) for x in parts[:EARLY]]
    early = early_tiles(names[:EARLY], flags, held)
    multiply(3, *held)
    flat = [u for k in kinds[:EARLY] for u in k]
    early_at = {u[:3]: (u[3], n) for n, u in enumerate(flat)}
    early = lax.all_gather(early, "pts")
    slots = [[], [], []]
    late_at = {}
    for part, k in enumerate(kinds[EARLY:]):
        for u, (name, e, c, owner) in enumerate(k):
            late_at[(name, e, c)] = (owner, len(slots[owner]))
            slots[owner].append((part, u, name))
    late = lax.all_to_all(sendings(slots, flags, pick, parts[EARLY:]), "pts", 0, 0)
    return final_tiles(early_at, late_at, where, early, late)[None]


def solution(mesh):
    return jax.shard_map(
        body,
        mesh=mesh,
        in_specs=(P("bas", "pts"), P(), P()),
        out_specs=P("pts", None, "bas", None),
        check_vma=False,
    )
```

```python
import functools

import jax
import jax.numpy as jnp
from jax import lax
from jax.experimental import pallas as pl
from jax.experimental.pallas import tpu as pltpu
from jax.sharding import PartitionSpec as P

PB = 512
SHARE = 32
LANES = 128
SUB = 8
CHUNKS = PB // LANES
GROUP = LANES // SUB
PTS = 16
VMEM = 14 * 1024 * 1024
WIDE = 32 * 1024 * 1024
F32 = jnp.float32
BF16 = jnp.bfloat16
NT = (((1,), (1,)), ((), ()))
NN = (((1,), (0,)), ((), ()))


def whole(x):
    return pltpu.with_memory_space_constraint(x, pltpu.VMEM)


def in_hbm(x):
    return pltpu.with_memory_space_constraint(x, pltpu.HBM)


IN_VMEM = pl.BlockSpec(memory_space=pltpu.VMEM)
IN_SMEM = pl.BlockSpec(memory_space=pltpu.SMEM)
FLAG = {"c": 0, "am": 1, "ar": 1, "b": 2}
EARLY = 4


def dot(a, b, dims):
    return lax.dot_general(a, b, dims, preferred_element_type=F32)


def split2(x):
    hi = x.astype(BF16)
    return hi, (x - hi.astype(F32)).astype(BF16)


def row_block(depth, most=768):
    for size in (768, 640, 512, 384, 256, 128):
        if size <= most and depth % size == 0:
            return size
    return depth


ANY = pl.BlockSpec(memory_space=pl.ANY)


def piece(k, rows):
    return pl.ds(pl.multiple_of(k * rows, rows), rows)


class Flow:
    def __init__(self, src, dst, sems, count):
        self.src, self.dst, self.sems, self.count = src, dst, sems, count

    def copy(self, k):
        return pltpu.make_async_copy(self.src(k), self.dst(k), self.sems.at[k])

    def start(self):
        for k in range(self.count):
            self.copy(k).start()

    def wait(self):
        for k in range(self.count):
            self.copy(k).wait()


def by_rows(src, dst, sems, rows, count):
    return Flow(lambda k: src.at[piece(k, rows)], lambda k: dst.at[piece(k, rows)], sems, count)


def by_lanes(src, dst, sems, rows, count):
    return Flow(lambda k: src.at[:, piece(k, rows)], lambda k: dst.at[:, piece(k, rows)], sems, count)


def start_all(flows):
    for k in range(flows[0].count):
        for flow in flows:
            flow.copy(k).start()


def turned(x):
    t = x.T
    return jnp.swapaxes(t.reshape(GROUP, CHUNKS, SUB, t.shape[1]), 0, 1).reshape(t.shape)


def turned_back(t):
    x = jnp.swapaxes(t.reshape(CHUNKS, GROUP, SUB, t.shape[1]), 0, 1).reshape(t.shape)
    return x.T


def chunks_kernel(chunk0, number, with_turned, count, rows, x_hbm, *refs):
    out_hbm, refs = refs[:number], refs[number:]
    if with_turned:
        hi_ref, lo_ref, refs = refs[0], refs[1], refs[2:]
    x_ref, out_ref, in_sems, out_sems = refs
    coming = by_rows(x_hbm, x_ref, in_sems, rows, count)
    going = [by_rows(out_ref.at[n], out_hbm[n], out_sems.at[n], rows, count) for n in range(number)]
    coming.start()

    @pl.loop(0, count)
    def _(k):
        coming.copy(k).wait()
        at = piece(k, rows)
        t = turned(x_ref[at])
        for n in range(number):
            out_ref[n, at] = t[(chunk0 + n) * LANES:(chunk0 + n + 1) * LANES].T
        if with_turned:
            hi_ref[:, at], lo_ref[:, at] = split2(t)
        for flow in going:
            flow.copy(k).start()

    for flow in going:
        flow.wait()


def chunks(x, chunk0, number, with_turned=False):
    depth = x.shape[0]
    rows = row_block(depth)
    count = depth // rows
    out_specs, out_shape = [ANY] * number, [pltpu.HBM((depth, LANES), F32)] * number
    if with_turned:
        out_specs += [IN_VMEM] * 2
        out_shape += [pltpu.VMEM((PB, depth), BF16)] * 2
    return pl.pallas_call(
        functools.partial(chunks_kernel, chunk0, number, with_turned, count, rows),
        in_specs=[ANY],
        out_specs=out_specs,
        out_shape=out_shape,
        scratch_shapes=[
            pltpu.VMEM((depth, PB), F32),
            pltpu.VMEM((number, depth, LANES), F32),
            pltpu.SemaphoreType.DMA((count,)),
            pltpu.SemaphoreType.DMA((number, count)),
        ],
        compiler_params=pltpu.CompilerParams(vmem_limit_bytes=WIDE),
        cost_estimate=pl.CostEstimate(flops=9 * depth * PB * PB, bytes_accessed=4 * depth * (PB + LANES * number), transcendentals=0),
        name="chunks",
    )(in_hbm(x))


def local_kernel(
    count, rows, o_hbm, mhi_hbm, mlo_hbm, ohi_hbm, olo_hbm, out_ref,
    o_ref, mhi_ref, mlo_ref, ohi_ref, olo_ref, acc_ref, in_sems, out_sems,
):
    coming = [
        by_rows(o_hbm, o_ref, in_sems.at[0], rows, count),
        by_lanes(mhi_hbm, mhi_ref, in_sems.at[1], rows, count),
        by_lanes(mlo_hbm, mlo_ref, in_sems.at[2], rows, count),
    ]
    going = [
        by_lanes(ohi_ref, ohi_hbm, out_sems.at[0], rows, count),
        by_lanes(olo_ref, olo_hbm, out_sems.at[1], rows, count),
    ]
    start_all(coming)
    acc_ref[...] = jnp.zeros_like(acc_ref)

    @pl.loop(0, count)
    def _(k):
        at = piece(k, rows)
        for flow in coming:
            flow.copy(k).wait()
        ohi, olo = split2(turned(o_ref[at]))
        ohi_ref[:, at] = ohi
        olo_ref[:, at] = olo
        mhi = mhi_ref[:, at]
        acc_ref[...] += dot(mhi, ohi, NT) + dot(mhi, olo, NT) + dot(mlo_ref[:, at], ohi, NT)
        for flow in going:
            flow.copy(k).start()

    for e in range(CHUNKS):
        for c in range(CHUNKS):
            put(out_ref, CHUNKS * e + c, acc_ref[e * LANES:(e + 1) * LANES, c * LANES:(c + 1) * LANES])
    for flow in going:
        flow.wait()


def local_units(other, mhi, mlo):
    depth = other.shape[0]
    rows = row_block(depth)
    count = depth // rows
    units = CHUNKS * CHUNKS
    wide = pltpu.VMEM((PB, depth), BF16)
    return pl.pallas_call(
        functools.partial(local_kernel, count, rows),
        in_specs=[ANY] * 3,
        out_specs=[ANY, ANY, pl.BlockSpec((GROUP, units, SUB, LANES))],
        out_shape=[pltpu.HBM((PB, depth), BF16)] * 2 + [pltpu.HBM((GROUP, units, SUB, LANES), F32)],
        scratch_shapes=[
            pltpu.VMEM((depth, PB), F32), wide, wide, wide, wide,
            pltpu.VMEM((PB, PB), F32),
            pltpu.SemaphoreType.DMA((3, count)),
            pltpu.SemaphoreType.DMA((2, count)),
        ],
        compiler_params=pltpu.CompilerParams(vmem_limit_bytes=WIDE),
        cost_estimate=pl.CostEstimate(flops=10 * depth * PB * PB, bytes_accessed=12 * depth * PB, transcendentals=0),
        name="local_units",
    )(in_hbm(other), in_hbm(mhi), in_hbm(mlo))


def put(out_ref, unit, block):
    out_ref[:, unit] = block.reshape(GROUP, SUB, LANES)


IN_VMEM = pl.BlockSpec(memory_space=pltpu.VMEM)
IN_SMEM = pl.BlockSpec(memory_space=pltpu.SMEM)
FLAG = {"c": 0, "am": 1, "ar": 1, "b": 2}
EARLY = 4


def step_units(c):
    units = [("am", e, c, 0) for e in range(CHUNKS)]
    units += [("ar", c, e, 2) for e in range(CHUNKS)]
    units += [("b", e, c, 1) for e in range(c, CHUNKS)]
    units += [("b", c, e, 2) for e in range(c + 1, CHUNKS)]
    return units


def step_kernel(
    c, count, rows, mhi_hbm, mlo_hbm, ohi_hbm, olo_hbm, r_hbm, out_ref,
    hi_ref, lo_ref, r_ref, wide_ref, slim_ref, sems,
):
    left = (CHUNKS - c) * LANES

    def lanes(src, dst, sem, first, base, n):
        return Flow(
            lambda k: src.at[pl.ds(first, n), piece(k, rows)], lambda k: dst.at[pl.ds(base, n), piece(k, rows)], sem, count
        )

    coming = [
        by_rows(r_hbm, r_ref, sems.at[0], rows, count),
        lanes(mhi_hbm, hi_ref, sems.at[1], 0, 0, PB),
        lanes(ohi_hbm, hi_ref, sems.at[2], PB - left, PB, left),
        lanes(mlo_hbm, lo_ref, sems.at[3], 0, 0, PB),
        lanes(olo_hbm, lo_ref, sems.at[4], PB - left, PB, left),
    ]
    start_all(coming)
    wide_ref[...] = jnp.zeros_like(wide_ref)
    slim_ref[...] = jnp.zeros_like(slim_ref)

    @pl.loop(0, count)
    def _(k):
        at = piece(k, rows)
        for flow in coming:
            flow.copy(k).wait()
        rhi, rlo = split2(r_ref[at])
        wide_ref[...] += dot(hi_ref[:, at], jnp.concatenate([rhi, rlo], axis=1), NN)
        slim_ref[...] += dot(lo_ref[:, at], rhi, NN)

    def block(n):
        rows = slice(n * LANES, (n + 1) * LANES)
        return wide_ref[rows, :LANES] + (wide_ref[rows, LANES:] + slim_ref[rows])

    for e in range(CHUNKS):
        a = block(e)
        put(out_ref, e, a)
        put(out_ref, CHUNKS + e, a.T)
    for e in range(c, CHUNKS):
        b = block(CHUNKS + e - c)
        put(out_ref, 2 * CHUNKS + e - c, b)
        if e > c:
            put(out_ref, 3 * CHUNKS + e - 2 * c - 1, b.T)


def arrived_units(c, mhi, mlo, ohi, olo, r):
    depth = r.shape[0]
    rows = row_block(depth)
    count = depth // rows
    units = len(step_units(c))
    lines = PB + (CHUNKS - c) * LANES
    return pl.pallas_call(
        functools.partial(step_kernel, c, count, rows),
        in_specs=[ANY] * 5,
        out_specs=pl.BlockSpec((GROUP, units, SUB, LANES)),
        out_shape=pltpu.HBM((GROUP, units, SUB, LANES), F32),
        scratch_shapes=[
            pltpu.VMEM((lines, depth), BF16),
            pltpu.VMEM((lines, depth), BF16),
            pltpu.VMEM((depth, LANES), F32),
            pltpu.VMEM((lines, 2 * LANES), F32),
            pltpu.VMEM((lines, LANES), F32),
            pltpu.SemaphoreType.DMA((5, count)),
        ],
        compiler_params=pltpu.CompilerParams(vmem_limit_bytes=WIDE),
        cost_estimate=pl.CostEstimate(
            flops=6 * depth * lines * LANES, bytes_accessed=4 * depth * (lines + LANES), transcendentals=0
        ),
        name="arrived_units",
    )(in_hbm(mhi), in_hbm(mlo), in_hbm(ohi), in_hbm(olo), in_hbm(r))


def squares(parts_ref, unit, flag):
    gram = parts_ref[0, unit]
    for n in range(1, GROUP):
        gram = gram + parts_ref[n, unit]
    return jnp.where(flag != 0, gram * gram, 0.0)


def early_kernel(names, kept, flags_ref, *refs):
    part_refs, out_ref = refs[:-1], refs[-1]
    n = 0
    if kept:
        n = part_refs[0].shape[0]
        out_ref[:n] = part_refs[0][...]
        part_refs = part_refs[1:]
    for part_ref, units in zip(part_refs, names):
        for u, name in enumerate(units):
            out_ref[n] = squares(part_ref, u, flags_ref[FLAG[name]])
            n += 1
    for pad in range(n, out_ref.shape[0]):
        out_ref[pad] = jnp.zeros((SUB, LANES), F32)


def early_tiles(names, flags, parts, count, kept=()):
    return pl.pallas_call(
        functools.partial(early_kernel, names, len(kept)),
        in_specs=[IN_SMEM] + [IN_VMEM] * (len(kept) + len(parts)),
        out_specs=IN_VMEM,
        out_shape=pltpu.HBM((count, SUB, LANES), F32),
        compiler_params=pltpu.CompilerParams(vmem_limit_bytes=VMEM),
        name="early_tiles",
    )(flags, *[whole(x) for x in (*kept, *parts)])


def send_kernel(slots, flags_ref, pick_ref, source_ref, parts_ref, spread_ref, out_ref, held_ref):
    size = held_ref.shape[1]
    per = out_ref.shape[1] - size
    for kind, units in enumerate(slots):
        for n, (u, name) in enumerate(units):
            held_ref[kind, n] = squares(parts_ref, u, flags_ref[FLAG[name]])
        for n in range(len(units), size):
            held_ref[kind, n] = jnp.zeros((SUB, LANES), F32)

    @pl.loop(0, PTS)
    def _(k):
        out_ref[k, :size] = held_ref[pick_ref[k]]
        for n in range(per):
            at = source_ref[k * per + n]
            out_ref[k, size + n] = jnp.where(at >= 0, spread_ref[jnp.maximum(at, 0)], 0.0)


def sendings(slots, flags, pick, source, parts, spread):
    size = max(len(units) for units in slots)
    per = spread.shape[0] // PTS
    return pl.pallas_call(
        functools.partial(send_kernel, slots),
        in_specs=[IN_SMEM] * 3 + [IN_VMEM] * 2,
        out_specs=IN_VMEM,
        out_shape=jax.ShapeDtypeStruct((PTS, size + per, SUB, LANES), F32),
        scratch_shapes=[pltpu.VMEM((len(slots), size, SUB, LANES), F32)],
        compiler_params=pltpu.CompilerParams(vmem_limit_bytes=VMEM),
        name="sendings",
    )(flags, pick, source, whole(parts), whole(spread))


def final_kernel(early_at, late_at, where_ref, got_ref, out_ref):
    def unit(name, e, c):
        if (name, e, c) in early_at:
            return got_ref[early_at[(name, e, c)]]
        kind, slot = late_at[(name, e, c)]
        got = got_ref[where_ref[1 + kind], slot]
        return jnp.where(where_ref[4] != 0, got, 0.0) if kind == 2 else got

    groups = ("c", "am", "b", "ar")
    sides = [jnp.concatenate([unit(g, e, c) for g in groups for e in range(CHUNKS)], axis=0).T for c in range(CHUNKS)]
    placed = turned_back(jnp.concatenate(sides, axis=0))
    for g in range(len(groups)):
        out_ref[lax.rem(g + 2 * where_ref[0], 4)] = placed[g * SHARE:(g + 1) * SHARE]


def final_tiles(early_at, late_at, where, got):
    return pl.pallas_call(
        functools.partial(final_kernel, early_at, late_at),
        in_specs=[IN_SMEM, IN_VMEM],
        out_specs=IN_VMEM,
        out_shape=jax.ShapeDtypeStruct((4, SHARE, PB), F32),
        compiler_params=pltpu.CompilerParams(vmem_limit_bytes=VMEM),
        name="final_tiles",
    )(where, whole(got))


def after(x, *others):
    return lax.optimization_barrier((x,) + others)[0]


def body(orbitals, owner_perm, pair_reach):
    me = lax.axis_index("pts")
    chips = PTS // 2
    swap = [(p, p ^ 1) for p in range(PTS)]
    onward = [(2 * z, 2 * z - 2) for z in range(1, chips)] + [(2 * z + 1, 2 * z + 3) for z in range(chips - 1)]

    ids = jnp.arange(PTS, dtype=jnp.int32)
    three = jnp.arange(3, dtype=jnp.int32)[:, None]
    first_of = me + (three == 2) - (me % 2) * (three + 1)
    apart = (three == 1).astype(jnp.int32)
    live = (ids == first_of) & (apart < pair_reach[None, :]) & (ids + apart + 1 < PTS)
    flags = jnp.sum(live.astype(jnp.int32), axis=1)
    block = jnp.sum(jnp.where(owner_perm[:, None] == ids[None, :], ids[:, None], 0), axis=0)
    partner = block - 2 + 4 * (block % 2)
    there = (partner >= 0) & (partner < PTS)
    partner = jnp.clip(partner, 0, PTS - 1)
    mine = ids == me
    five = jnp.arange(5, dtype=jnp.int32)[:, None]
    facts = jnp.where(five == 0, block % 2, jnp.where(five == 1, block, jnp.where(five == 2, block ^ 1, partner)))
    facts = jnp.where(five == 4, there.astype(jnp.int32), facts)
    where = jnp.sum(jnp.where(mine, facts, 0), axis=1)
    pick = jnp.where(block == me, 0, jnp.where(block == (me ^ 1), 1, 2))

    other = lax.ppermute(orbitals, "pts", swap)
    first, mhi, mlo = chunks(orbitals, 0, 1, True)
    (second,) = chunks(after(orbitals, first), 1, 1)
    ohi, olo, local = local_units(after(other, second), mhi, mlo)
    sent = [first, second, *chunks(after(orbitals, local), 2, 2)]
    arrived = []
    for c, x in enumerate(sent):
        arrived.append(lax.ppermute(x if c < 2 else after(x, arrived[0]), "pts", onward))

    to_sum = lambda x: lax.all_to_all(x, "bas", 0, 0)
    kinds = [[("c", e, c, 0) for e in range(CHUNKS) for c in range(CHUNKS)]] + [step_units(c) for c in range(CHUNKS)]
    names = [[u[0] for u in k] for k in kinds]
    flat = [u for k in kinds[:EARLY] for u in k]
    per = -(-len(flat) // PTS)
    kind = jnp.array([u[3] for u in flat] + [0] * (per * PTS - len(flat)), jnp.int32).reshape(PTS, per)
    kind = jnp.sum(jnp.where(mine[:, None], kind, 0), axis=0)[None, :]
    source = jnp.where(kind == 0, block[:, None], jnp.where(kind == 1, block[:, None] ^ 1, partner[:, None]))
    source = source * per + jnp.arange(per)[None, :]
    source = jnp.where((kind == 2) & ~there[:, None], -1, source).reshape(-1)

    units = [local]
    parts = [to_sum(units[0])]

    def multiply(c, *first):
        units.append(arrived_units(c, mhi, mlo, ohi, olo, after(arrived[c], units[-1], *first)))
        parts.append(to_sum(units[-1]))

    multiply(0, flags, where, pick, source)
    multiply(1, parts[0])
    multiply(2, parts[1])
    held = [after(x, units[3], arrived[3]) for x in parts[:3]]
    early = early_tiles(names[:3], flags, held, sum(len(x) for x in names[:3]))
    multiply(3, early)
    early = early_tiles(names[3:EARLY], flags, [after(x, units[4]) for x in parts[3:EARLY]], per * PTS, (early,))
    spread = lax.all_to_all(early.reshape(PTS, per, SUB, LANES), "pts", 0, 0).reshape(PTS * per, SUB, LANES)
    slots = [[], [], []]
    late_at = {}
    for u, (name, e, c, owner) in enumerate(kinds[EARLY]):
        late_at[(name, e, c)] = (owner, len(slots[owner]))
        slots[owner].append((u, name))
    size = max(len(x) for x in slots)
    early_at = {u[:3]: (n // per, size + n % per) for n, u in enumerate(flat)}
    got = lax.all_to_all(sendings(slots, flags, pick, source, parts[EARLY], spread), "pts", 0, 0)
    return final_tiles(early_at, late_at, where, got)[None]


def solution(mesh):
    return jax.shard_map(
        body,
        mesh=mesh,
        in_specs=(P("bas", "pts"), P(), P()),
        out_specs=P("pts", None, "bas", None),
        check_vma=False,
    )
```

```python
import functools

import jax
import jax.numpy as jnp
from jax import lax
from jax.experimental import pallas as pl
from jax.experimental.pallas import tpu as pltpu
from jax.sharding import PartitionSpec as P

PB = 512
SHARE = 32
LANES = 128
SUB = 8
CHUNKS = PB // LANES
GROUP = LANES // SUB
PTS = 16
VMEM = 14 * 1024 * 1024
WIDE = 32 * 1024 * 1024
F32 = jnp.float32
BF16 = jnp.bfloat16
NT = (((1,), (1,)), ((), ()))
NN = (((1,), (0,)), ((), ()))


def whole(x):
    return pltpu.with_memory_space_constraint(x, pltpu.VMEM)


def in_hbm(x):
    return pltpu.with_memory_space_constraint(x, pltpu.HBM)


IN_VMEM = pl.BlockSpec(memory_space=pltpu.VMEM)
IN_SMEM = pl.BlockSpec(memory_space=pltpu.SMEM)
FLAG = {"c": 0, "am": 1, "ar": 1, "b": 2}
EARLY = 4


def dot(a, b, dims):
    return lax.dot_general(a, b, dims, preferred_element_type=F32)


def split2(x):
    hi = x.astype(BF16)
    return hi, (x - hi.astype(F32)).astype(BF16)


def row_block(depth, most=768):
    for size in (768, 640, 512, 384, 256, 128):
        if size <= most and depth % size == 0:
            return size
    return depth


ANY = pl.BlockSpec(memory_space=pl.ANY)


def piece(k, rows):
    return pl.ds(pl.multiple_of(k * rows, rows), rows)


class Flow:
    def __init__(self, src, dst, sems, count):
        self.src, self.dst, self.sems, self.count = src, dst, sems, count

    def copy(self, k):
        return pltpu.make_async_copy(self.src(k), self.dst(k), self.sems.at[k])

    def start(self):
        for k in range(self.count):
            self.copy(k).start()

    def wait(self):
        for k in range(self.count):
            self.copy(k).wait()


def by_rows(src, dst, sems, rows, count):
    return Flow(lambda k: src.at[piece(k, rows)], lambda k: dst.at[piece(k, rows)], sems, count)


def by_lanes(src, dst, sems, rows, count):
    return Flow(lambda k: src.at[:, piece(k, rows)], lambda k: dst.at[:, piece(k, rows)], sems, count)


def start_all(flows):
    for k in range(flows[0].count):
        for flow in flows:
            flow.copy(k).start()


def turned(x):
    t = x.T
    return jnp.swapaxes(t.reshape(GROUP, CHUNKS, SUB, t.shape[1]), 0, 1).reshape(t.shape)


def turned_back(t):
    x = jnp.swapaxes(t.reshape(CHUNKS, GROUP, SUB, t.shape[1]), 0, 1).reshape(t.shape)
    return x.T


def chunks_kernel(chunk0, number, count, rows, x_hbm, *refs):
    outs = (len(refs) - 3) // 2
    out_hbm, (x_ref, *out_refs, in_sems, out_sems) = refs[:outs], refs[outs:]
    coming = by_rows(x_hbm, x_ref, in_sems, rows, count)
    going = [
        (by_rows if n < number else by_lanes)(ref, out_hbm[n], out_sems.at[n], rows, count)
        for n, ref in enumerate(out_refs)
    ]
    coming.start()

    @pl.loop(0, count)
    def _(k):
        coming.copy(k).wait()
        at = piece(k, rows)
        t = turned(x_ref[at])
        for n in range(number):
            out_refs[n][at] = t[(chunk0 + n) * LANES:(chunk0 + n + 1) * LANES].T
        if outs > number:
            out_refs[number][:, at], out_refs[number + 1][:, at] = split2(t)
        for flow in going:
            flow.copy(k).start()

    for flow in going:
        flow.wait()


def chunks(x, chunk0, number, with_turned=False):
    depth = x.shape[0]
    rows = row_block(depth)
    count = depth // rows
    kinds = [((depth, LANES), F32)] * number + [((PB, depth), BF16)] * (2 if with_turned else 0)
    return pl.pallas_call(
        functools.partial(chunks_kernel, chunk0, number, count, rows),
        in_specs=[ANY],
        out_specs=[ANY] * len(kinds),
        out_shape=[pltpu.HBM(*kind) for kind in kinds],
        scratch_shapes=[pltpu.VMEM((depth, PB), F32)]
        + [pltpu.VMEM(*kind) for kind in kinds]
        + [pltpu.SemaphoreType.DMA((count,)), pltpu.SemaphoreType.DMA((len(kinds), count))],
        compiler_params=pltpu.CompilerParams(vmem_limit_bytes=WIDE),
        cost_estimate=pl.CostEstimate(
            flops=9 * depth * PB * PB, bytes_accessed=4 * depth * (PB + LANES * number), transcendentals=0
        ),
        name="chunks",
    )(in_hbm(x))


def local_kernel(
    count, rows, o_hbm, mhi_hbm, mlo_hbm, ohi_hbm, olo_hbm, out_ref,
    o_ref, mhi_ref, mlo_ref, ohi_ref, olo_ref, acc_ref, in_sems, out_sems,
):
    coming = [
        by_rows(o_hbm, o_ref, in_sems.at[0], rows, count),
        by_lanes(mhi_hbm, mhi_ref, in_sems.at[1], rows, count),
        by_lanes(mlo_hbm, mlo_ref, in_sems.at[2], rows, count),
    ]
    going = [
        by_lanes(ohi_ref, ohi_hbm, out_sems.at[0], rows, count),
        by_lanes(olo_ref, olo_hbm, out_sems.at[1], rows, count),
    ]
    start_all(coming)
    acc_ref[...] = jnp.zeros_like(acc_ref)

    @pl.loop(0, count)
    def _(k):
        at = piece(k, rows)
        for flow in coming:
            flow.copy(k).wait()
        ohi, olo = split2(turned(o_ref[at]))
        ohi_ref[:, at] = ohi
        olo_ref[:, at] = olo
        mhi = mhi_ref[:, at]
        acc_ref[...] += dot(mhi, ohi, NT) + dot(mhi, olo, NT) + dot(mlo_ref[:, at], ohi, NT)
        for flow in going:
            flow.copy(k).start()

    for e in range(CHUNKS):
        for c in range(CHUNKS):
            put(out_ref, CHUNKS * e + c, acc_ref[e * LANES:(e + 1) * LANES, c * LANES:(c + 1) * LANES])
    for flow in going:
        flow.wait()


def local_units(other, mhi, mlo):
    depth = other.shape[0]
    rows = row_block(depth)
    count = depth // rows
    units = CHUNKS * CHUNKS
    wide = pltpu.VMEM((PB, depth), BF16)
    return pl.pallas_call(
        functools.partial(local_kernel, count, rows),
        in_specs=[ANY] * 3,
        out_specs=[ANY, ANY, pl.BlockSpec((GROUP, units, SUB, LANES))],
        out_shape=[pltpu.HBM((PB, depth), BF16)] * 2 + [pltpu.HBM((GROUP, units, SUB, LANES), F32)],
        scratch_shapes=[
            pltpu.VMEM((depth, PB), F32), wide, wide, wide, wide,
            pltpu.VMEM((PB, PB), F32),
            pltpu.SemaphoreType.DMA((3, count)),
            pltpu.SemaphoreType.DMA((2, count)),
        ],
        compiler_params=pltpu.CompilerParams(vmem_limit_bytes=WIDE),
        cost_estimate=pl.CostEstimate(flops=10 * depth * PB * PB, bytes_accessed=12 * depth * PB, transcendentals=0),
        name="local_units",
    )(in_hbm(other), in_hbm(mhi), in_hbm(mlo))


def put(out_ref, unit, block):
    out_ref[:, unit] = block.reshape(GROUP, SUB, LANES)


IN_VMEM = pl.BlockSpec(memory_space=pltpu.VMEM)
IN_SMEM = pl.BlockSpec(memory_space=pltpu.SMEM)
FLAG = {"c": 0, "am": 1, "ar": 1, "b": 2}
EARLY = 4


def step_units(c):
    units = [("am", e, c, 0) for e in range(CHUNKS)]
    units += [("ar", c, e, 2) for e in range(CHUNKS)]
    units += [("b", e, c, 1) for e in range(c, CHUNKS)]
    units += [("b", c, e, 2) for e in range(c + 1, CHUNKS)]
    return units


def step_kernel(
    c, count, rows, mhi_hbm, mlo_hbm, ohi_hbm, olo_hbm, r_hbm, out_ref,
    hi_ref, lo_ref, r_ref, wide_ref, slim_ref, sems,
):
    left = (CHUNKS - c) * LANES

    def lanes(src, dst, sem, first, base, n):
        return Flow(
            lambda k: src.at[pl.ds(first, n), piece(k, rows)], lambda k: dst.at[pl.ds(base, n), piece(k, rows)], sem, count
        )

    coming = [
        by_rows(r_hbm, r_ref, sems.at[0], rows, count),
        lanes(mhi_hbm, hi_ref, sems.at[1], 0, 0, PB),
        lanes(ohi_hbm, hi_ref, sems.at[2], PB - left, PB, left),
        lanes(mlo_hbm, lo_ref, sems.at[3], 0, 0, PB),
        lanes(olo_hbm, lo_ref, sems.at[4], PB - left, PB, left),
    ]
    start_all(coming)
    wide_ref[...] = jnp.zeros_like(wide_ref)
    slim_ref[...] = jnp.zeros_like(slim_ref)

    @pl.loop(0, count)
    def _(k):
        at = piece(k, rows)
        for flow in coming:
            flow.copy(k).wait()
        rhi, rlo = split2(r_ref[at])
        wide_ref[...] += dot(hi_ref[:, at], jnp.concatenate([rhi, rlo], axis=1), NN)
        slim_ref[...] += dot(lo_ref[:, at], rhi, NN)

    def block(n):
        rows = slice(n * LANES, (n + 1) * LANES)
        return wide_ref[rows, :LANES] + (wide_ref[rows, LANES:] + slim_ref[rows])

    for e in range(CHUNKS):
        a = block(e)
        put(out_ref, e, a)
        put(out_ref, CHUNKS + e, a.T)
    for e in range(c, CHUNKS):
        b = block(CHUNKS + e - c)
        put(out_ref, 2 * CHUNKS + e - c, b)
        if e > c:
            put(out_ref, 3 * CHUNKS + e - 2 * c - 1, b.T)


def arrived_units(c, mhi, mlo, ohi, olo, r):
    depth = r.shape[0]
    rows = row_block(depth)
    count = depth // rows
    units = len(step_units(c))
    lines = PB + (CHUNKS - c) * LANES
    return pl.pallas_call(
        functools.partial(step_kernel, c, count, rows),
        in_specs=[ANY] * 5,
        out_specs=pl.BlockSpec((GROUP, units, SUB, LANES)),
        out_shape=pltpu.HBM((GROUP, units, SUB, LANES), F32),
        scratch_shapes=[
            pltpu.VMEM((lines, depth), BF16),
            pltpu.VMEM((lines, depth), BF16),
            pltpu.VMEM((depth, LANES), F32),
            pltpu.VMEM((lines, 2 * LANES), F32),
            pltpu.VMEM((lines, LANES), F32),
            pltpu.SemaphoreType.DMA((5, count)),
        ],
        compiler_params=pltpu.CompilerParams(vmem_limit_bytes=WIDE),
        cost_estimate=pl.CostEstimate(
            flops=6 * depth * lines * LANES, bytes_accessed=4 * depth * (lines + LANES), transcendentals=0
        ),
        name="arrived_units",
    )(in_hbm(mhi), in_hbm(mlo), in_hbm(ohi), in_hbm(olo), in_hbm(r))


def squares(parts_ref, unit, flag):
    gram = parts_ref[0, unit]
    for n in range(1, GROUP):
        gram = gram + parts_ref[n, unit]
    return jnp.where(flag != 0, gram * gram, 0.0)


def early_kernel(names, kept, flags_ref, *refs):
    part_refs, out_ref = refs[:-1], refs[-1]
    n = 0
    if kept:
        n = part_refs[0].shape[0]
        out_ref[:n] = part_refs[0][...]
        part_refs = part_refs[1:]
    for part_ref, units in zip(part_refs, names):
        for u, name in enumerate(units):
            out_ref[n] = squares(part_ref, u, flags_ref[FLAG[name]])
            n += 1
    for pad in range(n, out_ref.shape[0]):
        out_ref[pad] = jnp.zeros((SUB, LANES), F32)


def early_tiles(names, flags, parts, count, kept=()):
    return pl.pallas_call(
        functools.partial(early_kernel, names, len(kept)),
        in_specs=[IN_SMEM] + [IN_VMEM] * (len(kept) + len(parts)),
        out_specs=IN_VMEM,
        out_shape=pltpu.HBM((count, SUB, LANES), F32),
        compiler_params=pltpu.CompilerParams(vmem_limit_bytes=VMEM),
        name="early_tiles",
    )(flags, *[whole(x) for x in (*kept, *parts)])


def send_kernel(slots, flags_ref, pick_ref, source_ref, parts_ref, spread_ref, out_ref, held_ref):
    size = held_ref.shape[1]
    per = out_ref.shape[1] - size
    for kind, units in enumerate(slots):
        for n, (u, name) in enumerate(units):
            held_ref[kind, n] = squares(parts_ref, u, flags_ref[FLAG[name]])
        for n in range(len(units), size):
            held_ref[kind, n] = jnp.zeros((SUB, LANES), F32)

    @pl.loop(0, PTS)
    def _(k):
        out_ref[k, :size] = held_ref[pick_ref[k]]
        for n in range(per):
            at = source_ref[k * per + n]
            out_ref[k, size + n] = jnp.where(at >= 0, spread_ref[jnp.maximum(at, 0)], 0.0)


def sendings(slots, flags, pick, source, parts, spread):
    size = max(len(units) for units in slots)
    per = spread.shape[0] // PTS
    return pl.pallas_call(
        functools.partial(send_kernel, slots),
        in_specs=[IN_SMEM] * 3 + [IN_VMEM] * 2,
        out_specs=IN_VMEM,
        out_shape=jax.ShapeDtypeStruct((PTS, size + per, SUB, LANES), F32),
        scratch_shapes=[pltpu.VMEM((len(slots), size, SUB, LANES), F32)],
        compiler_params=pltpu.CompilerParams(vmem_limit_bytes=VMEM),
        name="sendings",
    )(flags, pick, source, whole(parts), whole(spread))


def final_kernel(early_at, late_at, where_ref, got_ref, out_ref):
    def unit(name, e, c):
        if (name, e, c) in early_at:
            return got_ref[early_at[(name, e, c)]]
        kind, slot = late_at[(name, e, c)]
        got = got_ref[where_ref[1 + kind], slot]
        return jnp.where(where_ref[4] != 0, got, 0.0) if kind == 2 else got

    groups = ("c", "am", "b", "ar")
    sides = [jnp.concatenate([unit(g, e, c) for g in groups for e in range(CHUNKS)], axis=0).T for c in range(CHUNKS)]
    placed = turned_back(jnp.concatenate(sides, axis=0))
    for g in range(len(groups)):
        out_ref[lax.rem(g + 2 * where_ref[0], 4)] = placed[g * SHARE:(g + 1) * SHARE]


def final_tiles(early_at, late_at, where, got):
    return pl.pallas_call(
        functools.partial(final_kernel, early_at, late_at),
        in_specs=[IN_SMEM, IN_VMEM],
        out_specs=IN_VMEM,
        out_shape=jax.ShapeDtypeStruct((4, SHARE, PB), F32),
        compiler_params=pltpu.CompilerParams(vmem_limit_bytes=VMEM),
        name="final_tiles",
    )(where, whole(got))


def after(x, *others):
    return lax.optimization_barrier((x,) + others)[0]


def body(orbitals, owner_perm, pair_reach):
    me = lax.axis_index("pts")
    chips = PTS // 2
    swap = [(p, p ^ 1) for p in range(PTS)]
    onward = [(2 * z, (2 * z - 2) % PTS) for z in range(chips)] + [(2 * z + 1, (2 * z + 3) % PTS) for z in range(chips)]

    ids = jnp.arange(PTS, dtype=jnp.int32)
    three = jnp.arange(3, dtype=jnp.int32)[:, None]
    first_of = me + (three == 2) - (me % 2) * (three + 1)
    apart = (three == 1).astype(jnp.int32)
    live = (ids == first_of) & (apart < pair_reach[None, :]) & (ids + apart + 1 < PTS)
    flags = jnp.sum(live.astype(jnp.int32), axis=1)
    block = jnp.sum(jnp.where(owner_perm[:, None] == ids[None, :], ids[:, None], 0), axis=0)
    partner = block - 2 + 4 * (block % 2)
    there = (partner >= 0) & (partner < PTS)
    partner = jnp.clip(partner, 0, PTS - 1)
    mine = ids == me
    five = jnp.arange(5, dtype=jnp.int32)[:, None]
    facts = jnp.where(five == 0, block % 2, jnp.where(five == 1, block, jnp.where(five == 2, block ^ 1, partner)))
    facts = jnp.where(five == 4, there.astype(jnp.int32), facts)
    where = jnp.sum(jnp.where(mine, facts, 0), axis=1)
    pick = jnp.where(block == me, 0, jnp.where(block == (me ^ 1), 1, 2))

    other = lax.ppermute(orbitals, "pts", swap)
    first, second, mhi, mlo = chunks(orbitals, 0, 2, True)
    ohi, olo, local = local_units(other, mhi, mlo)
    sent = [first, after(second, other), *chunks(after(orbitals, local), 2, 2)]
    arrived = []
    for c, x in enumerate(sent):
        arrived.append(lax.ppermute(x if c < 2 else after(x, arrived[0]), "pts", onward))

    to_sum = lambda x: lax.all_to_all(x, "bas", 0, 0)
    kinds = [[("c", e, c, 0) for e in range(CHUNKS) for c in range(CHUNKS)]] + [step_units(c) for c in range(CHUNKS)]
    names = [[u[0] for u in k] for k in kinds]
    flat = [u for k in kinds[:EARLY] for u in k]
    per = -(-len(flat) // PTS)
    kind = jnp.array([u[3] for u in flat] + [0] * (per * PTS - len(flat)), jnp.int32).reshape(PTS, per)
    kind = jnp.sum(jnp.where(mine[:, None], kind, 0), axis=0)[None, :]
    source = jnp.where(kind == 0, block[:, None], jnp.where(kind == 1, block[:, None] ^ 1, partner[:, None]))
    source = source * per + jnp.arange(per)[None, :]
    source = jnp.where((kind == 2) & ~there[:, None], -1, source).reshape(-1)

    units = [local]
    parts = [to_sum(units[0])]

    def multiply(c, *first):
        units.append(arrived_units(c, mhi, mlo, ohi, olo, after(arrived[c], units[-1], *first)))
        parts.append(to_sum(units[-1]))

    multiply(0, flags, where, pick, source)
    multiply(1, parts[0])
    multiply(2, parts[1])
    held = [after(x, units[3], arrived[3]) for x in parts[:3]]
    early = early_tiles(names[:3], flags, held, sum(len(x) for x in names[:3]))
    multiply(3, early)
    early = early_tiles(names[3:EARLY], flags, [after(x, units[4]) for x in parts[3:EARLY]], per * PTS, (early,))
    spread = lax.all_to_all(early.reshape(PTS, per, SUB, LANES), "pts", 0, 0).reshape(PTS * per, SUB, LANES)
    slots = [[], [], []]
    late_at = {}
    for u, (name, e, c, owner) in enumerate(kinds[EARLY]):
        late_at[(name, e, c)] = (owner, len(slots[owner]))
        slots[owner].append((u, name))
    size = max(len(x) for x in slots)
    early_at = {u[:3]: (n // per, size + n % per) for n, u in enumerate(flat)}
    got = lax.all_to_all(sendings(slots, flags, pick, source, parts[EARLY], spread), "pts", 0, 0)
    return final_tiles(early_at, late_at, where, got)[None]


def solution(mesh):
    return jax.shard_map(
        body,
        mesh=mesh,
        in_specs=(P("bas", "pts"), P(), P()),
        out_specs=P("pts", None, "bas", None),
        check_vma=False,
    )
```

```python
import functools

import jax
import jax.numpy as jnp
from jax import lax
from jax.experimental import pallas as pl
from jax.experimental.pallas import tpu as pltpu
from jax.sharding import PartitionSpec as P

PB = 512
SHARE = 32
LANES = 128
SUB = 8
CHUNKS = PB // LANES
GROUP = LANES // SUB
PTS = 16
VMEM = 14 * 1024 * 1024
WIDE = 32 * 1024 * 1024
F32 = jnp.float32
BF16 = jnp.bfloat16
NT = (((1,), (1,)), ((), ()))
NN = (((1,), (0,)), ((), ()))


def whole(x):
    return pltpu.with_memory_space_constraint(x, pltpu.VMEM)


def in_hbm(x):
    return pltpu.with_memory_space_constraint(x, pltpu.HBM)


IN_VMEM = pl.BlockSpec(memory_space=pltpu.VMEM)
IN_SMEM = pl.BlockSpec(memory_space=pltpu.SMEM)
FLAG = {"c": 0, "am": 1, "ar": 1, "b": 2}
EARLY = 3


def dot(a, b, dims):
    return lax.dot_general(a, b, dims, preferred_element_type=F32)


def split2(x):
    hi = x.astype(BF16)
    return hi, (x - hi.astype(F32)).astype(BF16)


def row_block(depth, most=768):
    for size in (768, 640, 512, 384, 256, 128):
        if size <= most and depth % size == 0:
            return size
    return depth


ANY = pl.BlockSpec(memory_space=pl.ANY)


def piece(k, rows):
    return pl.ds(pl.multiple_of(k * rows, rows), rows)


class Flow:
    def __init__(self, src, dst, sems, count):
        self.src, self.dst, self.sems, self.count = src, dst, sems, count

    def copy(self, k):
        return pltpu.make_async_copy(self.src(k), self.dst(k), self.sems.at[k])

    def start(self):
        for k in range(self.count):
            self.copy(k).start()

    def wait(self):
        for k in range(self.count):
            self.copy(k).wait()


def by_rows(src, dst, sems, rows, count):
    return Flow(lambda k: src.at[piece(k, rows)], lambda k: dst.at[piece(k, rows)], sems, count)


def by_lanes(src, dst, sems, rows, count):
    return Flow(lambda k: src.at[:, piece(k, rows)], lambda k: dst.at[:, piece(k, rows)], sems, count)


def start_all(flows):
    for k in range(flows[0].count):
        for flow in flows:
            flow.copy(k).start()


def turned(x):
    t = x.T
    return jnp.swapaxes(t.reshape(GROUP, CHUNKS, SUB, t.shape[1]), 0, 1).reshape(t.shape)


def turned_back(t):
    x = jnp.swapaxes(t.reshape(CHUNKS, GROUP, SUB, t.shape[1]), 0, 1).reshape(t.shape)
    return x.T


def chunks_kernel(chunk0, number, count, rows, x_hbm, *refs):
    outs = (len(refs) - 3) // 2
    out_hbm, (x_ref, *out_refs, in_sems, out_sems) = refs[:outs], refs[outs:]
    coming = by_rows(x_hbm, x_ref, in_sems, rows, count)
    going = [
        (by_rows if n < number else by_lanes)(ref, out_hbm[n], out_sems.at[n], rows, count)
        for n, ref in enumerate(out_refs)
    ]
    coming.start()

    @pl.loop(0, count)
    def _(k):
        coming.copy(k).wait()
        at = piece(k, rows)
        t = turned(x_ref[at])
        for n in range(number):
            out_refs[n][at] = t[(chunk0 + n) * LANES:(chunk0 + n + 1) * LANES].T
        if outs > number:
            out_refs[number][:, at], out_refs[number + 1][:, at] = split2(t)
        for flow in going:
            flow.copy(k).start()

    for flow in going:
        flow.wait()


def chunks(x, chunk0, number, with_turned=False):
    depth = x.shape[0]
    rows = row_block(depth)
    count = depth // rows
    kinds = [((depth, LANES), F32)] * number + [((PB, depth), BF16)] * (2 if with_turned else 0)
    return pl.pallas_call(
        functools.partial(chunks_kernel, chunk0, number, count, rows),
        in_specs=[ANY],
        out_specs=[ANY] * len(kinds),
        out_shape=[pltpu.HBM(*kind) for kind in kinds],
        scratch_shapes=[pltpu.VMEM((depth, PB), F32)]
        + [pltpu.VMEM(*kind) for kind in kinds]
        + [pltpu.SemaphoreType.DMA((count,)), pltpu.SemaphoreType.DMA((len(kinds), count))],
        compiler_params=pltpu.CompilerParams(vmem_limit_bytes=WIDE),
        cost_estimate=pl.CostEstimate(
            flops=9 * depth * PB * PB, bytes_accessed=4 * depth * (PB + LANES * number), transcendentals=0
        ),
        name="chunks",
    )(in_hbm(x))


def local_kernel(
    count, rows, o_hbm, mhi_hbm, mlo_hbm, ohi_hbm, olo_hbm, out_ref,
    o_ref, mhi_ref, mlo_ref, ohi_ref, olo_ref, acc_ref, in_sems, out_sems,
):
    coming = [
        by_rows(o_hbm, o_ref, in_sems.at[0], rows, count),
        by_lanes(mhi_hbm, mhi_ref, in_sems.at[1], rows, count),
        by_lanes(mlo_hbm, mlo_ref, in_sems.at[2], rows, count),
    ]
    going = [
        by_lanes(ohi_ref, ohi_hbm, out_sems.at[0], rows, count),
        by_lanes(olo_ref, olo_hbm, out_sems.at[1], rows, count),
    ]
    start_all(coming)
    acc_ref[...] = jnp.zeros_like(acc_ref)

    @pl.loop(0, count)
    def _(k):
        at = piece(k, rows)
        for flow in coming:
            flow.copy(k).wait()
        ohi, olo = split2(turned(o_ref[at]))
        ohi_ref[:, at] = ohi
        olo_ref[:, at] = olo
        mhi = mhi_ref[:, at]
        acc_ref[...] += dot(mhi, ohi, NT) + dot(mhi, olo, NT) + dot(mlo_ref[:, at], ohi, NT)
        for flow in going:
            flow.copy(k).start()

    for e in range(CHUNKS):
        for c in range(CHUNKS):
            put(out_ref, CHUNKS * e + c, acc_ref[e * LANES:(e + 1) * LANES, c * LANES:(c + 1) * LANES])
    for flow in going:
        flow.wait()


def local_units(other, mhi, mlo):
    depth = other.shape[0]
    rows = row_block(depth)
    count = depth // rows
    units = CHUNKS * CHUNKS
    wide = pltpu.VMEM((PB, depth), BF16)
    return pl.pallas_call(
        functools.partial(local_kernel, count, rows),
        in_specs=[ANY] * 3,
        out_specs=[ANY, ANY, pl.BlockSpec((GROUP, units, SUB, LANES))],
        out_shape=[pltpu.HBM((PB, depth), BF16)] * 2 + [pltpu.HBM((GROUP, units, SUB, LANES), F32)],
        scratch_shapes=[
            pltpu.VMEM((depth, PB), F32), wide, wide, wide, wide,
            pltpu.VMEM((PB, PB), F32),
            pltpu.SemaphoreType.DMA((3, count)),
            pltpu.SemaphoreType.DMA((2, count)),
        ],
        compiler_params=pltpu.CompilerParams(vmem_limit_bytes=WIDE),
        cost_estimate=pl.CostEstimate(flops=10 * depth * PB * PB, bytes_accessed=12 * depth * PB, transcendentals=0),
        name="local_units",
    )(in_hbm(other), in_hbm(mhi), in_hbm(mlo))


def put(out_ref, unit, block):
    out_ref[:, unit] = block.reshape(GROUP, SUB, LANES)


IN_VMEM = pl.BlockSpec(memory_space=pltpu.VMEM)
IN_SMEM = pl.BlockSpec(memory_space=pltpu.SMEM)
FLAG = {"c": 0, "am": 1, "ar": 1, "b": 2}
EARLY = 3


def step_units(c):
    units = [("am", e, c, 0) for e in range(CHUNKS)]
    units += [("ar", c, e, 2) for e in range(CHUNKS)]
    units += [("b", e, c, 1) for e in range(c, CHUNKS)]
    units += [("b", c, e, 2) for e in range(c + 1, CHUNKS)]
    return units


def step_kernel(
    c, count, rows, mhi_hbm, mlo_hbm, ohi_hbm, olo_hbm, r_hbm, out_ref,
    hi_ref, lo_ref, r_ref, wide_ref, slim_ref, sems,
):
    left = (CHUNKS - c) * LANES

    def lanes(src, dst, sem, first, base, n):
        return Flow(
            lambda k: src.at[pl.ds(first, n), piece(k, rows)], lambda k: dst.at[pl.ds(base, n), piece(k, rows)], sem, count
        )

    coming = [
        by_rows(r_hbm, r_ref, sems.at[0], rows, count),
        lanes(mhi_hbm, hi_ref, sems.at[1], 0, 0, PB),
        lanes(ohi_hbm, hi_ref, sems.at[2], PB - left, PB, left),
        lanes(mlo_hbm, lo_ref, sems.at[3], 0, 0, PB),
        lanes(olo_hbm, lo_ref, sems.at[4], PB - left, PB, left),
    ]
    start_all(coming)
    wide_ref[...] = jnp.zeros_like(wide_ref)
    slim_ref[...] = jnp.zeros_like(slim_ref)

    @pl.loop(0, count)
    def _(k):
        at = piece(k, rows)
        for flow in coming:
            flow.copy(k).wait()
        rhi, rlo = split2(r_ref[at])
        wide_ref[...] += dot(hi_ref[:, at], jnp.concatenate([rhi, rlo], axis=1), NN)
        slim_ref[...] += dot(lo_ref[:, at], rhi, NN)

    def block(n):
        rows = slice(n * LANES, (n + 1) * LANES)
        return wide_ref[rows, :LANES] + (wide_ref[rows, LANES:] + slim_ref[rows])

    for e in range(CHUNKS):
        a = block(e)
        put(out_ref, e, a)
        put(out_ref, CHUNKS + e, a.T)
    for e in range(c, CHUNKS):
        b = block(CHUNKS + e - c)
        put(out_ref, 2 * CHUNKS + e - c, b)
        if e > c:
            put(out_ref, 3 * CHUNKS + e - 2 * c - 1, b.T)


def arrived_units(c, mhi, mlo, ohi, olo, r):
    depth = r.shape[0]
    rows = row_block(depth)
    count = depth // rows
    units = len(step_units(c))
    lines = PB + (CHUNKS - c) * LANES
    return pl.pallas_call(
        functools.partial(step_kernel, c, count, rows),
        in_specs=[ANY] * 5,
        out_specs=pl.BlockSpec((GROUP, units, SUB, LANES)),
        out_shape=pltpu.HBM((GROUP, units, SUB, LANES), F32),
        scratch_shapes=[
            pltpu.VMEM((lines, depth), BF16),
            pltpu.VMEM((lines, depth), BF16),
            pltpu.VMEM((depth, LANES), F32),
            pltpu.VMEM((lines, 2 * LANES), F32),
            pltpu.VMEM((lines, LANES), F32),
            pltpu.SemaphoreType.DMA((5, count)),
        ],
        compiler_params=pltpu.CompilerParams(vmem_limit_bytes=WIDE),
        cost_estimate=pl.CostEstimate(
            flops=6 * depth * lines * LANES, bytes_accessed=4 * depth * (lines + LANES), transcendentals=0
        ),
        name="arrived_units",
    )(in_hbm(mhi), in_hbm(mlo), in_hbm(ohi), in_hbm(olo), in_hbm(r))


def squares(parts_ref, unit, flag):
    gram = parts_ref[0, unit]
    for n in range(1, GROUP):
        gram = gram + parts_ref[n, unit]
    return jnp.where(flag != 0, gram * gram, 0.0)


def early_kernel(names, flags_ref, *refs):
    part_refs, out_ref = refs[:-1], refs[-1]
    n = 0
    for part_ref, units in zip(part_refs, names):
        for u, name in enumerate(units):
            out_ref[n] = squares(part_ref, u, flags_ref[FLAG[name]])
            n += 1
    for pad in range(n, out_ref.shape[0]):
        out_ref[pad] = jnp.zeros((SUB, LANES), F32)


def early_tiles(names, flags, parts, count):
    return pl.pallas_call(
        functools.partial(early_kernel, names),
        in_specs=[IN_SMEM] + [IN_VMEM] * len(parts),
        out_specs=IN_VMEM,
        out_shape=pltpu.HBM((count, SUB, LANES), F32),
        compiler_params=pltpu.CompilerParams(vmem_limit_bytes=VMEM),
        name="early_tiles",
    )(flags, *[whole(x) for x in parts])


def send_kernel(slots, flags_ref, pick_ref, source_ref, spread_ref, *refs):
    part_refs, out_ref, held_ref = refs[:-2], refs[-2], refs[-1]
    size = held_ref.shape[1]
    per = out_ref.shape[1] - size
    for kind, units in enumerate(slots):
        for n, (part, u, name) in enumerate(units):
            held_ref[kind, n] = squares(part_refs[part], u, flags_ref[FLAG[name]])
        for n in range(len(units), size):
            held_ref[kind, n] = jnp.zeros((SUB, LANES), F32)

    @pl.loop(0, PTS)
    def _(k):
        out_ref[k, :size] = held_ref[pick_ref[k]]
        for n in range(per):
            at = source_ref[k * per + n]
            out_ref[k, size + n] = jnp.where(at >= 0, spread_ref[jnp.maximum(at, 0)], 0.0)


def sendings(slots, flags, pick, source, spread, parts):
    size = max(len(units) for units in slots)
    per = spread.shape[0] // PTS
    return pl.pallas_call(
        functools.partial(send_kernel, slots),
        in_specs=[IN_SMEM] * 3 + [IN_VMEM] * (1 + len(parts)),
        out_specs=IN_VMEM,
        out_shape=jax.ShapeDtypeStruct((PTS, size + per, SUB, LANES), F32),
        scratch_shapes=[pltpu.VMEM((len(slots), size, SUB, LANES), F32)],
        compiler_params=pltpu.CompilerParams(vmem_limit_bytes=VMEM),
        name="sendings",
    )(flags, pick, source, whole(spread), *[whole(x) for x in parts])


def final_kernel(early_at, late_at, where_ref, got_ref, out_ref):
    def unit(name, e, c):
        if (name, e, c) in early_at:
            return got_ref[early_at[(name, e, c)]]
        kind, slot = late_at[(name, e, c)]
        got = got_ref[where_ref[1 + kind], slot]
        return jnp.where(where_ref[4] != 0, got, 0.0) if kind == 2 else got

    groups = ("c", "am", "b", "ar")
    sides = [jnp.concatenate([unit(g, e, c) for g in groups for e in range(CHUNKS)], axis=0).T for c in range(CHUNKS)]
    placed = turned_back(jnp.concatenate(sides, axis=0))
    for g in range(len(groups)):
        out_ref[lax.rem(g + 2 * where_ref[0], 4)] = placed[g * SHARE:(g + 1) * SHARE]


def final_tiles(early_at, late_at, where, got):
    return pl.pallas_call(
        functools.partial(final_kernel, early_at, late_at),
        in_specs=[IN_SMEM, IN_VMEM],
        out_specs=IN_VMEM,
        out_shape=jax.ShapeDtypeStruct((4, SHARE, PB), F32),
        compiler_params=pltpu.CompilerParams(vmem_limit_bytes=VMEM),
        name="final_tiles",
    )(where, whole(got))


def after(x, *others):
    return lax.optimization_barrier((x,) + others)[0]


def body(orbitals, owner_perm, pair_reach):
    me = lax.axis_index("pts")
    chips = PTS // 2
    swap = [(p, p ^ 1) for p in range(PTS)]
    onward = [(2 * z, (2 * z - 2) % PTS) for z in range(chips)] + [(2 * z + 1, (2 * z + 3) % PTS) for z in range(chips)]

    ids = jnp.arange(PTS, dtype=jnp.int32)
    three = jnp.arange(3, dtype=jnp.int32)[:, None]
    first_of = me + (three == 2) - (me % 2) * (three + 1)
    apart = (three == 1).astype(jnp.int32)
    live = (ids == first_of) & (apart < pair_reach[None, :]) & (ids + apart + 1 < PTS)
    flags = jnp.sum(live.astype(jnp.int32), axis=1)
    block = jnp.sum(jnp.where(owner_perm[:, None] == ids[None, :], ids[:, None], 0), axis=0)
    partner = block - 2 + 4 * (block % 2)
    there = (partner >= 0) & (partner < PTS)
    partner = jnp.clip(partner, 0, PTS - 1)
    mine = ids == me
    five = jnp.arange(5, dtype=jnp.int32)[:, None]
    facts = jnp.where(five == 0, block % 2, jnp.where(five == 1, block, jnp.where(five == 2, block ^ 1, partner)))
    facts = jnp.where(five == 4, there.astype(jnp.int32), facts)
    where = jnp.sum(jnp.where(mine, facts, 0), axis=1)
    pick = jnp.where(block == me, 0, jnp.where(block == (me ^ 1), 1, 2))

    other = lax.ppermute(orbitals, "pts", swap)
    first, second, mhi, mlo = chunks(orbitals, 0, 2, True)
    ohi, olo, local = local_units(other, mhi, mlo)
    sent = [first, after(second, other), *chunks(after(orbitals, local), 2, 2)]
    arrived = []
    for c, x in enumerate(sent):
        arrived.append(lax.ppermute(x if c < 2 else after(x, arrived[0]), "pts", onward))

    to_sum = lambda x: lax.all_to_all(x, "bas", 0, 0)
    kinds = [[("c", e, c, 0) for e in range(CHUNKS) for c in range(CHUNKS)]] + [step_units(c) for c in range(CHUNKS)]
    names = [[u[0] for u in k] for k in kinds]
    flat = [u for k in kinds[:EARLY] for u in k]
    per = -(-len(flat) // PTS)
    kind = jnp.array([u[3] for u in flat] + [0] * (per * PTS - len(flat)), jnp.int32).reshape(PTS, per)
    kind = jnp.sum(jnp.where(mine[:, None], kind, 0), axis=0)[None, :]
    source = jnp.where(kind == 0, block[:, None], jnp.where(kind == 1, block[:, None] ^ 1, partner[:, None]))
    source = source * per + jnp.arange(per)[None, :]
    source = jnp.where((kind == 2) & ~there[:, None], -1, source).reshape(-1)

    units = [local]
    parts = [to_sum(units[0])]

    def multiply(c, *first):
        units.append(arrived_units(c, mhi, mlo, ohi, olo, after(arrived[c], units[-1], *first)))

    multiply(0, flags, where, pick, source)
    parts.append(to_sum(units[1]))
    multiply(1, parts[0])
    parts.append(to_sum(units[2]))
    multiply(2, parts[1])
    early = early_tiles(names[:EARLY], flags, [after(x, units[3]) for x in parts], per * PTS)
    spread = lax.all_to_all(early.reshape(PTS, per, SUB, LANES), "pts", 0, 0).reshape(PTS * per, SUB, LANES)
    parts.append(to_sum(after(units[3], spread)))
    multiply(3, spread)
    parts.append(to_sum(after(units[4], parts[3])))
    slots = [[], [], []]
    late_at = {}
    for part, k in enumerate(kinds[EARLY:]):
        for u, (name, e, c, owner) in enumerate(k):
            late_at[(name, e, c)] = (owner, len(slots[owner]))
            slots[owner].append((part, u, name))
    size = max(len(x) for x in slots)
    early_at = {u[:3]: (n // per, size + n % per) for n, u in enumerate(flat)}
    got = lax.all_to_all(sendings(slots, flags, pick, source, spread, parts[EARLY:]), "pts", 0, 0)
    return final_tiles(early_at, late_at, where, got)[None]


def solution(mesh):
    return jax.shard_map(
        body,
        mesh=mesh,
        in_specs=(P("bas", "pts"), P(), P()),
        out_specs=P("pts", None, "bas", None),
        check_vma=False,
    )
```

```python
import functools

import jax
import jax.numpy as jnp
from jax import lax
from jax.experimental import pallas as pl
from jax.experimental.pallas import tpu as pltpu
from jax.sharding import PartitionSpec as P

PB = 512
SHARE = 32
LANES = 128
SUB = 8
CHUNKS = PB // LANES
GROUP = LANES // SUB
SIDE = 4
PTS = 16
VMEM = 14 * 1024 * 1024
WIDE = 32 * 1024 * 1024
F32 = jnp.float32
BF16 = jnp.bfloat16
NT = (((1,), (1,)), ((), ()))
NN = (((1,), (0,)), ((), ()))


def whole(x):
    return pltpu.with_memory_space_constraint(x, pltpu.VMEM)


def in_hbm(x):
    return pltpu.with_memory_space_constraint(x, pltpu.HBM)


IN_VMEM = pl.BlockSpec(memory_space=pltpu.VMEM)
IN_SMEM = pl.BlockSpec(memory_space=pltpu.SMEM)
FLAG = {"c": 0, "am": 1, "ar": 1, "b": 2}
EARLY = 4


def dot(a, b, dims):
    return lax.dot_general(a, b, dims, preferred_element_type=F32)


def split2(x):
    hi = x.astype(BF16)
    return hi, (x - hi.astype(F32)).astype(BF16)


def row_block(depth, most=768):
    for size in (768, 640, 512, 384, 256, 128):
        if size <= most and depth % size == 0:
            return size
    return depth


ANY = pl.BlockSpec(memory_space=pl.ANY)


def piece(k, rows):
    return pl.ds(pl.multiple_of(k * rows, rows), rows)


class Flow:
    def __init__(self, src, dst, sems, count):
        self.src, self.dst, self.sems, self.count = src, dst, sems, count

    def copy(self, k):
        return pltpu.make_async_copy(self.src(k), self.dst(k), self.sems.at[k])

    def start(self):
        for k in range(self.count):
            self.copy(k).start()

    def wait(self):
        for k in range(self.count):
            self.copy(k).wait()


def by_rows(src, dst, sems, rows, count):
    return Flow(lambda k: src.at[piece(k, rows)], lambda k: dst.at[piece(k, rows)], sems, count)


def by_lanes(src, dst, sems, rows, count):
    return Flow(lambda k: src.at[:, piece(k, rows)], lambda k: dst.at[:, piece(k, rows)], sems, count)


def start_all(flows):
    for k in range(flows[0].count):
        for flow in flows:
            flow.copy(k).start()


def turned(x):
    t = x.T
    return jnp.swapaxes(t.reshape(GROUP, CHUNKS, SUB, t.shape[1]), 0, 1).reshape(t.shape)


def turned_back(t):
    x = jnp.swapaxes(t.reshape(CHUNKS, GROUP, SUB, t.shape[1]), 0, 1).reshape(t.shape)
    return x.T


def chunks_kernel(chunk0, number, count, rows, x_hbm, *refs):
    outs = (len(refs) - 3) // 2
    out_hbm, (x_ref, *out_refs, in_sems, out_sems) = refs[:outs], refs[outs:]
    coming = by_rows(x_hbm, x_ref, in_sems, rows, count)
    going = [
        (by_rows if n < number else by_lanes)(ref, out_hbm[n], out_sems.at[n], rows, count)
        for n, ref in enumerate(out_refs)
    ]
    coming.start()

    @pl.loop(0, count)
    def _(k):
        coming.copy(k).wait()
        at = piece(k, rows)
        t = turned(x_ref[at])
        for n in range(number):
            out_refs[n][at] = t[(chunk0 + n) * LANES:(chunk0 + n + 1) * LANES].T
        if outs > number:
            out_refs[number][:, at], out_refs[number + 1][:, at] = split2(t)
        for flow in going:
            flow.copy(k).start()

    for flow in going:
        flow.wait()


def chunks(x, chunk0, number, with_turned=False):
    depth = x.shape[0]
    rows = row_block(depth)
    count = depth // rows
    kinds = [((depth, LANES), F32)] * number + [((PB, depth), BF16)] * (2 if with_turned else 0)
    return pl.pallas_call(
        functools.partial(chunks_kernel, chunk0, number, count, rows),
        in_specs=[ANY],
        out_specs=[ANY] * len(kinds),
        out_shape=[pltpu.HBM(*kind) for kind in kinds],
        scratch_shapes=[pltpu.VMEM((depth, PB), F32)]
        + [pltpu.VMEM(*kind) for kind in kinds]
        + [pltpu.SemaphoreType.DMA((count,)), pltpu.SemaphoreType.DMA((len(kinds), count))],
        compiler_params=pltpu.CompilerParams(vmem_limit_bytes=WIDE),
        cost_estimate=pl.CostEstimate(
            flops=9 * depth * PB * PB, bytes_accessed=4 * depth * (PB + LANES * number), transcendentals=0
        ),
        name="chunks",
    )(in_hbm(x))


def local_kernel(
    count, rows, o_hbm, mhi_hbm, mlo_hbm, ohi_hbm, olo_hbm, out_ref,
    o_ref, mhi_ref, mlo_ref, ohi_ref, olo_ref, acc_ref, in_sems, out_sems,
):
    coming = [
        by_rows(o_hbm, o_ref, in_sems.at[0], rows, count),
        by_lanes(mhi_hbm, mhi_ref, in_sems.at[1], rows, count),
        by_lanes(mlo_hbm, mlo_ref, in_sems.at[2], rows, count),
    ]
    going = [
        by_lanes(ohi_ref, ohi_hbm, out_sems.at[0], rows, count),
        by_lanes(olo_ref, olo_hbm, out_sems.at[1], rows, count),
    ]
    start_all(coming)
    acc_ref[...] = jnp.zeros_like(acc_ref)

    @pl.loop(0, count)
    def _(k):
        at = piece(k, rows)
        for flow in coming:
            flow.copy(k).wait()
        ohi, olo = split2(turned(o_ref[at]))
        ohi_ref[:, at] = ohi
        olo_ref[:, at] = olo
        mhi = mhi_ref[:, at]
        acc_ref[...] += dot(mhi, ohi, NT) + dot(mhi, olo, NT) + dot(mlo_ref[:, at], ohi, NT)
        for flow in going:
            flow.copy(k).start()

    for e in range(CHUNKS):
        for c in range(CHUNKS):
            put(out_ref, CHUNKS * e + c, acc_ref[e * LANES:(e + 1) * LANES, c * LANES:(c + 1) * LANES])
    for flow in going:
        flow.wait()


def local_units(other, mhi, mlo):
    depth = other.shape[0]
    rows = row_block(depth)
    count = depth // rows
    units = CHUNKS * CHUNKS
    wide = pltpu.VMEM((PB, depth), BF16)
    return pl.pallas_call(
        functools.partial(local_kernel, count, rows),
        in_specs=[ANY] * 3,
        out_specs=[ANY, ANY, pl.BlockSpec((GROUP, units, SUB, LANES))],
        out_shape=[pltpu.HBM((PB, depth), BF16)] * 2 + [pltpu.HBM((GROUP, units, SUB, LANES), F32)],
        scratch_shapes=[
            pltpu.VMEM((depth, PB), F32), wide, wide, wide, wide,
            pltpu.VMEM((PB, PB), F32),
            pltpu.SemaphoreType.DMA((3, count)),
            pltpu.SemaphoreType.DMA((2, count)),
        ],
        compiler_params=pltpu.CompilerParams(vmem_limit_bytes=WIDE),
        cost_estimate=pl.CostEstimate(flops=10 * depth * PB * PB, bytes_accessed=12 * depth * PB, transcendentals=0),
        name="local_units",
    )(in_hbm(other), in_hbm(mhi), in_hbm(mlo))


def put(out_ref, unit, block):
    out_ref[:, unit] = block.reshape(GROUP, SUB, LANES)


IN_VMEM = pl.BlockSpec(memory_space=pltpu.VMEM)
IN_SMEM = pl.BlockSpec(memory_space=pltpu.SMEM)
FLAG = {"c": 0, "am": 1, "ar": 1, "b": 2}
EARLY = 4


def step_units(c):
    units = [("am", e, c, 0) for e in range(CHUNKS)]
    units += [("ar", c, e, 2) for e in range(CHUNKS)]
    units += [("b", e, c, 1) for e in range(c, CHUNKS)]
    units += [("b", c, e, 2) for e in range(c + 1, CHUNKS)]
    return units


def step_kernel(
    c, count, rows, mhi_hbm, mlo_hbm, ohi_hbm, olo_hbm, r_hbm, out_ref,
    hi_ref, lo_ref, r_ref, wide_ref, slim_ref, sems,
):
    left = (CHUNKS - c) * LANES

    def lanes(src, dst, sem, first, base, n):
        return Flow(
            lambda k: src.at[pl.ds(first, n), piece(k, rows)], lambda k: dst.at[pl.ds(base, n), piece(k, rows)], sem, count
        )

    coming = [
        by_rows(r_hbm, r_ref, sems.at[0], rows, count),
        lanes(mhi_hbm, hi_ref, sems.at[1], 0, 0, PB),
        lanes(ohi_hbm, hi_ref, sems.at[2], PB - left, PB, left),
        lanes(mlo_hbm, lo_ref, sems.at[3], 0, 0, PB),
        lanes(olo_hbm, lo_ref, sems.at[4], PB - left, PB, left),
    ]
    start_all(coming)
    wide_ref[...] = jnp.zeros_like(wide_ref)
    slim_ref[...] = jnp.zeros_like(slim_ref)

    @pl.loop(0, count)
    def _(k):
        at = piece(k, rows)
        for flow in coming:
            flow.copy(k).wait()
        rhi, rlo = split2(r_ref[at])
        wide_ref[...] += dot(hi_ref[:, at], jnp.concatenate([rhi, rlo], axis=1), NN)
        slim_ref[...] += dot(lo_ref[:, at], rhi, NN)

    def block(n):
        rows = slice(n * LANES, (n + 1) * LANES)
        return wide_ref[rows, :LANES] + (wide_ref[rows, LANES:] + slim_ref[rows])

    for e in range(CHUNKS):
        a = block(e)
        put(out_ref, e, a)
        put(out_ref, CHUNKS + e, a.T)
    for e in range(c, CHUNKS):
        b = block(CHUNKS + e - c)
        put(out_ref, 2 * CHUNKS + e - c, b)
        if e > c:
            put(out_ref, 3 * CHUNKS + e - 2 * c - 1, b.T)


def arrived_units(c, mhi, mlo, ohi, olo, r):
    depth = r.shape[0]
    rows = row_block(depth)
    count = depth // rows
    units = len(step_units(c))
    lines = PB + (CHUNKS - c) * LANES
    return pl.pallas_call(
        functools.partial(step_kernel, c, count, rows),
        in_specs=[ANY] * 5,
        out_specs=pl.BlockSpec((GROUP, units, SUB, LANES)),
        out_shape=pltpu.HBM((GROUP, units, SUB, LANES), F32),
        scratch_shapes=[
            pltpu.VMEM((lines, depth), BF16),
            pltpu.VMEM((lines, depth), BF16),
            pltpu.VMEM((depth, LANES), F32),
            pltpu.VMEM((lines, 2 * LANES), F32),
            pltpu.VMEM((lines, LANES), F32),
            pltpu.SemaphoreType.DMA((5, count)),
        ],
        compiler_params=pltpu.CompilerParams(vmem_limit_bytes=WIDE),
        cost_estimate=pl.CostEstimate(
            flops=6 * depth * lines * LANES, bytes_accessed=4 * depth * (lines + LANES), transcendentals=0
        ),
        name="arrived_units",
    )(in_hbm(mhi), in_hbm(mlo), in_hbm(ohi), in_hbm(olo), in_hbm(r))


def squares(parts_ref, unit, flag):
    gram = parts_ref[0, unit]
    for n in range(1, GROUP):
        gram = gram + parts_ref[n, unit]
    return jnp.where(flag != 0, gram * gram, 0.0)


def early_kernel(names, kept, flags_ref, *refs):
    part_refs, out_ref = refs[:-1], refs[-1]
    n = 0
    if kept:
        n = part_refs[0].shape[0]
        out_ref[:n] = part_refs[0][...]
        part_refs = part_refs[1:]
    for part_ref, units in zip(part_refs, names):
        for u, name in enumerate(units):
            out_ref[n] = squares(part_ref, u, flags_ref[FLAG[name]])
            n += 1
    for pad in range(n, out_ref.shape[0]):
        out_ref[pad] = jnp.zeros((SUB, LANES), F32)


def early_tiles(names, flags, parts, count, kept=()):
    return pl.pallas_call(
        functools.partial(early_kernel, names, len(kept)),
        in_specs=[IN_SMEM] + [IN_VMEM] * (len(kept) + len(parts)),
        out_specs=IN_VMEM,
        out_shape=pltpu.HBM((count, SUB, LANES), F32),
        compiler_params=pltpu.CompilerParams(vmem_limit_bytes=VMEM),
        name="early_tiles",
    )(flags, *[whole(x) for x in (*kept, *parts)])


def send_kernel(slots, flags_ref, pick_ref, source_ref, spread_ref, *refs):
    term_refs, out_ref, held_ref = refs[:-2], refs[-2], refs[-1]
    size = held_ref.shape[1]
    per = out_ref.shape[1] - size
    for kind, units in enumerate(slots):
        for n, (u, name) in enumerate(units):
            gram = term_refs[0][u]
            for term_ref in term_refs[1:]:
                gram = gram + term_ref[u]
            held_ref[kind, n] = jnp.where(flags_ref[FLAG[name]] != 0, gram * gram, 0.0)
        for n in range(len(units), size):
            held_ref[kind, n] = jnp.zeros((SUB, LANES), F32)

    @pl.loop(0, PTS)
    def _(k):
        out_ref[k, :size] = held_ref[pick_ref[k]]
        for n in range(per):
            at = source_ref[k * per + n]
            out_ref[k, size + n] = jnp.where(at >= 0, spread_ref[jnp.maximum(at, 0)], 0.0)


def sendings(slots, flags, pick, source, spread, terms):
    size = max(len(units) for units in slots)
    per = spread.shape[0] // PTS
    return pl.pallas_call(
        functools.partial(send_kernel, slots),
        in_specs=[IN_SMEM] * 3 + [IN_VMEM] * (1 + len(terms)),
        out_specs=IN_VMEM,
        out_shape=jax.ShapeDtypeStruct((PTS, size + per, SUB, LANES), F32),
        scratch_shapes=[pltpu.VMEM((len(slots), size, SUB, LANES), F32)],
        compiler_params=pltpu.CompilerParams(vmem_limit_bytes=VMEM),
        name="sendings",
    )(flags, pick, source, whole(spread), *[whole(x) for x in terms])


def final_kernel(early_at, late_at, where_ref, got_ref, out_ref):
    def unit(name, e, c):
        if (name, e, c) in early_at:
            return got_ref[early_at[(name, e, c)]]
        kind, slot = late_at[(name, e, c)]
        got = got_ref[where_ref[1 + kind], slot]
        return jnp.where(where_ref[4] != 0, got, 0.0) if kind == 2 else got

    groups = ("c", "am", "b", "ar")
    sides = [jnp.concatenate([unit(g, e, c) for g in groups for e in range(CHUNKS)], axis=0).T for c in range(CHUNKS)]
    placed = turned_back(jnp.concatenate(sides, axis=0))
    for g in range(len(groups)):
        out_ref[lax.rem(g + 2 * where_ref[0], 4)] = placed[g * SHARE:(g + 1) * SHARE]


def final_tiles(early_at, late_at, where, got):
    return pl.pallas_call(
        functools.partial(final_kernel, early_at, late_at),
        in_specs=[IN_SMEM, IN_VMEM],
        out_specs=IN_VMEM,
        out_shape=jax.ShapeDtypeStruct((4, SHARE, PB), F32),
        compiler_params=pltpu.CompilerParams(vmem_limit_bytes=VMEM),
        name="final_tiles",
    )(where, whole(got))


def shared_out(x, at, onto):
    parts = [lax.dynamic_index_in_dim(x, (at + d) % SIDE, 0, keepdims=False) for d in range(SIDE)]
    return parts[:1] + [lax.ppermute(parts[d], "bas", [(j, onto(j, d)) for j in range(GROUP)]) for d in range(1, SIDE)]


def after(x, *others):
    return lax.optimization_barrier((x,) + others)[0]


def body(orbitals, owner_perm, pair_reach):
    me = lax.axis_index("pts")
    chips = PTS // 2
    swap = [(p, p ^ 1) for p in range(PTS)]
    onward = [(2 * z, (2 * z - 2) % PTS) for z in range(chips)] + [(2 * z + 1, (2 * z + 3) % PTS) for z in range(chips)]

    ids = jnp.arange(PTS, dtype=jnp.int32)
    three = jnp.arange(3, dtype=jnp.int32)[:, None]
    first_of = me + (three == 2) - (me % 2) * (three + 1)
    apart = (three == 1).astype(jnp.int32)
    live = (ids == first_of) & (apart < pair_reach[None, :]) & (ids + apart + 1 < PTS)
    flags = jnp.sum(live.astype(jnp.int32), axis=1)
    block = jnp.sum(jnp.where(owner_perm[:, None] == ids[None, :], ids[:, None], 0), axis=0)
    partner = block - 2 + 4 * (block % 2)
    there = (partner >= 0) & (partner < PTS)
    partner = jnp.clip(partner, 0, PTS - 1)
    mine = ids == me
    five = jnp.arange(5, dtype=jnp.int32)[:, None]
    facts = jnp.where(five == 0, block % 2, jnp.where(five == 1, block, jnp.where(five == 2, block ^ 1, partner)))
    facts = jnp.where(five == 4, there.astype(jnp.int32), facts)
    where = jnp.sum(jnp.where(mine, facts, 0), axis=1)
    pick = jnp.where(block == me, 0, jnp.where(block == (me ^ 1), 1, 2))

    other = lax.ppermute(orbitals, "pts", swap)
    first, second, mhi, mlo = chunks(orbitals, 0, 2, True)
    ohi, olo, local = local_units(other, mhi, mlo)
    sent = [first, after(second, other), *chunks(after(orbitals, local), 2, 2)]
    arrived = []
    for c, x in enumerate(sent):
        arrived.append(lax.ppermute(x if c < 2 else after(x, arrived[0]), "pts", onward))

    to_sum = lambda x: lax.all_to_all(x, "bas", 0, 0)
    kinds = [[("c", e, c, 0) for e in range(CHUNKS) for c in range(CHUNKS)]] + [step_units(c) for c in range(CHUNKS)]
    names = [[u[0] for u in k] for k in kinds]
    flat = [u for k in kinds[:EARLY] for u in k]
    per = -(-len(flat) // PTS)
    kind = jnp.array([u[3] for u in flat] + [0] * (per * PTS - len(flat)), jnp.int32).reshape(PTS, per)
    kind = jnp.sum(jnp.where(mine[:, None], kind, 0), axis=0)[None, :]
    source = jnp.where(kind == 0, block[:, None], jnp.where(kind == 1, block[:, None] ^ 1, partner[:, None]))
    source = source * per + jnp.arange(per)[None, :]
    source = jnp.where((kind == 2) & ~there[:, None], -1, source).reshape(-1)

    units = [local]
    parts = [to_sum(units[0])]

    def multiply(c, *first):
        units.append(arrived_units(c, mhi, mlo, ohi, olo, after(arrived[c], units[-1], *first)))

    multiply(0, flags, where, pick, source)
    parts.append(to_sum(units[1]))
    multiply(1, parts[0])
    parts.append(to_sum(units[2]))
    multiply(2, parts[1])
    parts.append(to_sum(units[3]))
    held = [after(x, units[3]) for x in parts[:3]]
    early = early_tiles(names[:3], flags, held, sum(len(x) for x in names[:3]))
    multiply(3, early)
    place = lax.axis_index("bas")
    along = shared_out(
        units[4].reshape((SIDE, SIDE) + units[4].shape[1:]),
        place // SIDE,
        lambda j, d: (j // SIDE + d) % SIDE * SIDE + j % SIDE,
    )
    early = early_tiles(names[3:EARLY], flags, [after(x, units[4]) for x in parts[3:EARLY]], per * PTS, (early,))
    spread = lax.all_to_all(early.reshape(PTS, per, SUB, LANES), "pts", 0, 0).reshape(PTS * per, SUB, LANES)
    line = along[0] + along[1] + along[2] + along[3]
    terms = shared_out(line, place % SIDE, lambda j, d: j // SIDE * SIDE + (j % SIDE + d) % SIDE)
    slots = [[], [], []]
    late_at = {}
    for u, (name, e, c, owner) in enumerate(kinds[EARLY]):
        late_at[(name, e, c)] = (owner, len(slots[owner]))
        slots[owner].append((u, name))
    size = max(len(x) for x in slots)
    early_at = {u[:3]: (n // per, size + n % per) for n, u in enumerate(flat)}
    got = lax.all_to_all(sendings(slots, flags, pick, source, spread, terms), "pts", 0, 0)
    return final_tiles(early_at, late_at, where, got)[None]


def solution(mesh):
    return jax.shard_map(
        body,
        mesh=mesh,
        in_specs=(P("bas", "pts"), P(), P()),
        out_specs=P("pts", None, "bas", None),
        check_vma=False,
    )
```

```python
import functools

import jax
import jax.numpy as jnp
from jax import lax
from jax.experimental import pallas as pl
from jax.experimental.pallas import tpu as pltpu
from jax.sharding import PartitionSpec as P

PB = 512
SHARE = 32
LANES = 128
SUB = 8
CHUNKS = PB // LANES
GROUP = LANES // SUB
SIDE = 4
PTS = 16
VMEM = 14 * 1024 * 1024
WIDE = 32 * 1024 * 1024
F32 = jnp.float32
BF16 = jnp.bfloat16
NT = (((1,), (1,)), ((), ()))
NN = (((1,), (0,)), ((), ()))


def whole(x):
    return pltpu.with_memory_space_constraint(x, pltpu.VMEM)


def in_hbm(x):
    return pltpu.with_memory_space_constraint(x, pltpu.HBM)


IN_VMEM = pl.BlockSpec(memory_space=pltpu.VMEM)
IN_SMEM = pl.BlockSpec(memory_space=pltpu.SMEM)
FLAG = {"c": 0, "am": 1, "ar": 1, "b": 2}
EARLY = 4


def dot(a, b, dims):
    return lax.dot_general(a, b, dims, preferred_element_type=F32)


def split2(x):
    hi = x.astype(BF16)
    return hi, (x - hi.astype(F32)).astype(BF16)


def row_block(depth, most=768):
    for size in (768, 640, 512, 384, 256, 128):
        if size <= most and depth % size == 0:
            return size
    return depth


ANY = pl.BlockSpec(memory_space=pl.ANY)


def piece(k, rows):
    return pl.ds(pl.multiple_of(k * rows, rows), rows)


class Flow:
    def __init__(self, src, dst, sems, count):
        self.src, self.dst, self.sems, self.count = src, dst, sems, count

    def copy(self, k):
        return pltpu.make_async_copy(self.src(k), self.dst(k), self.sems.at[k])

    def start(self):
        for k in range(self.count):
            self.copy(k).start()

    def wait(self):
        for k in range(self.count):
            self.copy(k).wait()


def by_rows(src, dst, sems, rows, count):
    return Flow(lambda k: src.at[piece(k, rows)], lambda k: dst.at[piece(k, rows)], sems, count)


def by_lanes(src, dst, sems, rows, count):
    return Flow(lambda k: src.at[:, piece(k, rows)], lambda k: dst.at[:, piece(k, rows)], sems, count)


def start_all(flows):
    for k in range(flows[0].count):
        for flow in flows:
            flow.copy(k).start()


def turned(x):
    t = x.T
    return jnp.swapaxes(t.reshape(GROUP, CHUNKS, SUB, t.shape[1]), 0, 1).reshape(t.shape)


def turned_back(t):
    x = jnp.swapaxes(t.reshape(CHUNKS, GROUP, SUB, t.shape[1]), 0, 1).reshape(t.shape)
    return x.T


def chunks_kernel(chunk0, number, count, rows, x_hbm, *refs):
    outs = (len(refs) - 3) // 2
    out_hbm, (x_ref, *out_refs, in_sems, out_sems) = refs[:outs], refs[outs:]
    coming = by_rows(x_hbm, x_ref, in_sems, rows, count)
    going = [
        (by_rows if n < number else by_lanes)(ref, out_hbm[n], out_sems.at[n], rows, count)
        for n, ref in enumerate(out_refs)
    ]
    coming.start()

    @pl.loop(0, count)
    def _(k):
        coming.copy(k).wait()
        at = piece(k, rows)
        t = turned(x_ref[at])
        for n in range(number):
            out_refs[n][at] = t[(chunk0 + n) * LANES:(chunk0 + n + 1) * LANES].T
        if outs > number:
            out_refs[number][:, at], out_refs[number + 1][:, at] = split2(t)
        for flow in going:
            flow.copy(k).start()

    for flow in going:
        flow.wait()


def chunks(x, chunk0, number, with_turned=False):
    depth = x.shape[0]
    rows = row_block(depth)
    count = depth // rows
    kinds = [((depth, LANES), F32)] * number + [((PB, depth), BF16)] * (2 if with_turned else 0)
    return pl.pallas_call(
        functools.partial(chunks_kernel, chunk0, number, count, rows),
        in_specs=[ANY],
        out_specs=[ANY] * len(kinds),
        out_shape=[pltpu.HBM(*kind) for kind in kinds],
        scratch_shapes=[pltpu.VMEM((depth, PB), F32)]
        + [pltpu.VMEM(*kind) for kind in kinds]
        + [pltpu.SemaphoreType.DMA((count,)), pltpu.SemaphoreType.DMA((len(kinds), count))],
        compiler_params=pltpu.CompilerParams(vmem_limit_bytes=WIDE),
        cost_estimate=pl.CostEstimate(
            flops=9 * depth * PB * PB, bytes_accessed=4 * depth * (PB + LANES * number), transcendentals=0
        ),
        name="chunks",
    )(in_hbm(x))


def local_kernel(
    count, rows, o_hbm, mhi_hbm, mlo_hbm, ohi_hbm, olo_hbm, out_ref,
    o_ref, mhi_ref, mlo_ref, ohi_ref, olo_ref, acc_ref, in_sems, out_sems,
):
    coming = [
        by_rows(o_hbm, o_ref, in_sems.at[0], rows, count),
        by_lanes(mhi_hbm, mhi_ref, in_sems.at[1], rows, count),
        by_lanes(mlo_hbm, mlo_ref, in_sems.at[2], rows, count),
    ]
    going = [
        by_lanes(ohi_ref, ohi_hbm, out_sems.at[0], rows, count),
        by_lanes(olo_ref, olo_hbm, out_sems.at[1], rows, count),
    ]
    start_all(coming)
    acc_ref[...] = jnp.zeros_like(acc_ref)

    @pl.loop(0, count)
    def _(k):
        at = piece(k, rows)
        for flow in coming:
            flow.copy(k).wait()
        ohi, olo = split2(turned(o_ref[at]))
        ohi_ref[:, at] = ohi
        olo_ref[:, at] = olo
        mhi = mhi_ref[:, at]
        acc_ref[...] += dot(mhi, ohi, NT) + dot(mhi, olo, NT) + dot(mlo_ref[:, at], ohi, NT)
        for flow in going:
            flow.copy(k).start()

    for e in range(CHUNKS):
        for c in range(CHUNKS):
            put(out_ref, CHUNKS * e + c, acc_ref[e * LANES:(e + 1) * LANES, c * LANES:(c + 1) * LANES])
    for flow in going:
        flow.wait()


def local_units(other, mhi, mlo):
    depth = other.shape[0]
    rows = row_block(depth)
    count = depth // rows
    units = CHUNKS * CHUNKS
    wide = pltpu.VMEM((PB, depth), BF16)
    return pl.pallas_call(
        functools.partial(local_kernel, count, rows),
        in_specs=[ANY] * 3,
        out_specs=[ANY, ANY, pl.BlockSpec((GROUP, units, SUB, LANES))],
        out_shape=[pltpu.HBM((PB, depth), BF16)] * 2 + [pltpu.HBM((GROUP, units, SUB, LANES), F32)],
        scratch_shapes=[
            pltpu.VMEM((depth, PB), F32), wide, wide, wide, wide,
            pltpu.VMEM((PB, PB), F32),
            pltpu.SemaphoreType.DMA((3, count)),
            pltpu.SemaphoreType.DMA((2, count)),
        ],
        compiler_params=pltpu.CompilerParams(vmem_limit_bytes=WIDE),
        cost_estimate=pl.CostEstimate(flops=10 * depth * PB * PB, bytes_accessed=12 * depth * PB, transcendentals=0),
        name="local_units",
    )(in_hbm(other), in_hbm(mhi), in_hbm(mlo))


def put(out_ref, unit, block):
    out_ref[:, unit] = block.reshape(GROUP, SUB, LANES)


IN_VMEM = pl.BlockSpec(memory_space=pltpu.VMEM)
IN_SMEM = pl.BlockSpec(memory_space=pltpu.SMEM)
FLAG = {"c": 0, "am": 1, "ar": 1, "b": 2}
EARLY = 4


def step_units(c):
    units = [("am", e, c, 0) for e in range(CHUNKS)]
    units += [("ar", c, e, 2) for e in range(CHUNKS)]
    units += [("b", e, c, 1) for e in range(c, CHUNKS)]
    units += [("b", c, e, 2) for e in range(c + 1, CHUNKS)]
    return units


def step_kernel(
    c, count, rows, mhi_hbm, mlo_hbm, ohi_hbm, olo_hbm, r_hbm, out_ref,
    hi_ref, lo_ref, r_ref, wide_ref, slim_ref, sems,
):
    left = (CHUNKS - c) * LANES

    def lanes(src, dst, sem, first, base, n):
        return Flow(
            lambda k: src.at[pl.ds(first, n), piece(k, rows)], lambda k: dst.at[pl.ds(base, n), piece(k, rows)], sem, count
        )

    coming = [
        by_rows(r_hbm, r_ref, sems.at[0], rows, count),
        lanes(mhi_hbm, hi_ref, sems.at[1], 0, 0, PB),
        lanes(ohi_hbm, hi_ref, sems.at[2], PB - left, PB, left),
        lanes(mlo_hbm, lo_ref, sems.at[3], 0, 0, PB),
        lanes(olo_hbm, lo_ref, sems.at[4], PB - left, PB, left),
    ]
    start_all(coming)
    wide_ref[...] = jnp.zeros_like(wide_ref)
    slim_ref[...] = jnp.zeros_like(slim_ref)

    @pl.loop(0, count)
    def _(k):
        at = piece(k, rows)
        for flow in coming:
            flow.copy(k).wait()
        rhi, rlo = split2(r_ref[at])
        wide_ref[...] += dot(hi_ref[:, at], jnp.concatenate([rhi, rlo], axis=1), NN)
        slim_ref[...] += dot(lo_ref[:, at], rhi, NN)

    def block(n):
        rows = slice(n * LANES, (n + 1) * LANES)
        return wide_ref[rows, :LANES] + (wide_ref[rows, LANES:] + slim_ref[rows])

    for e in range(CHUNKS):
        a = block(e)
        put(out_ref, e, a)
        put(out_ref, CHUNKS + e, a.T)
    for e in range(c, CHUNKS):
        b = block(CHUNKS + e - c)
        put(out_ref, 2 * CHUNKS + e - c, b)
        if e > c:
            put(out_ref, 3 * CHUNKS + e - 2 * c - 1, b.T)


def arrived_units(c, mhi, mlo, ohi, olo, r):
    depth = r.shape[0]
    rows = row_block(depth)
    count = depth // rows
    units = len(step_units(c))
    lines = PB + (CHUNKS - c) * LANES
    return pl.pallas_call(
        functools.partial(step_kernel, c, count, rows),
        in_specs=[ANY] * 5,
        out_specs=pl.BlockSpec((GROUP, units, SUB, LANES)),
        out_shape=pltpu.HBM((GROUP, units, SUB, LANES), F32),
        scratch_shapes=[
            pltpu.VMEM((lines, depth), BF16),
            pltpu.VMEM((lines, depth), BF16),
            pltpu.VMEM((depth, LANES), F32),
            pltpu.VMEM((lines, 2 * LANES), F32),
            pltpu.VMEM((lines, LANES), F32),
            pltpu.SemaphoreType.DMA((5, count)),
        ],
        compiler_params=pltpu.CompilerParams(vmem_limit_bytes=WIDE),
        cost_estimate=pl.CostEstimate(
            flops=6 * depth * lines * LANES, bytes_accessed=4 * depth * (lines + LANES), transcendentals=0
        ),
        name="arrived_units",
    )(in_hbm(mhi), in_hbm(mlo), in_hbm(ohi), in_hbm(olo), in_hbm(r))


def squares(parts_ref, unit, flag):
    gram = parts_ref[0, unit]
    for n in range(1, GROUP):
        gram = gram + parts_ref[n, unit]
    return jnp.where(flag != 0, gram * gram, 0.0)


def early_kernel(names, kept, flags_ref, *refs):
    part_refs, out_ref = refs[:-1], refs[-1]
    n = 0
    if kept:
        n = part_refs[0].shape[0]
        out_ref[:n] = part_refs[0][...]
        part_refs = part_refs[1:]
    for part_ref, units in zip(part_refs, names):
        for u, name in enumerate(units):
            out_ref[n] = squares(part_ref, u, flags_ref[FLAG[name]])
            n += 1
    for pad in range(n, out_ref.shape[0]):
        out_ref[pad] = jnp.zeros((SUB, LANES), F32)


def early_tiles(names, flags, parts, count, kept=()):
    return pl.pallas_call(
        functools.partial(early_kernel, names, len(kept)),
        in_specs=[IN_SMEM] + [IN_VMEM] * (len(kept) + len(parts)),
        out_specs=IN_VMEM,
        out_shape=pltpu.HBM((count, SUB, LANES), F32),
        compiler_params=pltpu.CompilerParams(vmem_limit_bytes=VMEM),
        name="early_tiles",
    )(flags, *[whole(x) for x in (*kept, *parts)])


def send_kernel(slots, flags_ref, pick_ref, source_ref, spread_ref, *refs):
    term_refs, out_ref, held_ref = refs[:-2], refs[-2], refs[-1]
    size = held_ref.shape[1]
    per = out_ref.shape[1] - size
    for kind, units in enumerate(slots):
        for n, (u, name) in enumerate(units):
            gram = term_refs[0][u]
            for term_ref in term_refs[1:]:
                gram = gram + term_ref[u]
            held_ref[kind, n] = jnp.where(flags_ref[FLAG[name]] != 0, gram * gram, 0.0)
        for n in range(len(units), size):
            held_ref[kind, n] = jnp.zeros((SUB, LANES), F32)

    @pl.loop(0, PTS)
    def _(k):
        out_ref[k, :size] = held_ref[pick_ref[k]]
        for n in range(per):
            at = source_ref[k * per + n]
            out_ref[k, size + n] = jnp.where(at >= 0, spread_ref[jnp.maximum(at, 0)], 0.0)


def sendings(slots, flags, pick, source, spread, terms):
    size = max(len(units) for units in slots)
    per = spread.shape[0] // PTS
    return pl.pallas_call(
        functools.partial(send_kernel, slots),
        in_specs=[IN_SMEM] * 3 + [IN_VMEM] * (1 + len(terms)),
        out_specs=IN_VMEM,
        out_shape=jax.ShapeDtypeStruct((PTS, size + per, SUB, LANES), F32),
        scratch_shapes=[pltpu.VMEM((len(slots), size, SUB, LANES), F32)],
        compiler_params=pltpu.CompilerParams(vmem_limit_bytes=VMEM),
        name="sendings",
    )(flags, pick, source, whole(spread), *[whole(x) for x in terms])


def final_kernel(early_at, late_at, where_ref, got_ref, out_ref):
    def unit(name, e, c):
        if (name, e, c) in early_at:
            return got_ref[early_at[(name, e, c)]]
        kind, slot = late_at[(name, e, c)]
        got = got_ref[where_ref[1 + kind], slot]
        return jnp.where(where_ref[4] != 0, got, 0.0) if kind == 2 else got

    groups = ("c", "am", "b", "ar")
    sides = [jnp.concatenate([unit(g, e, c) for g in groups for e in range(CHUNKS)], axis=0).T for c in range(CHUNKS)]
    placed = turned_back(jnp.concatenate(sides, axis=0))
    for g in range(len(groups)):
        out_ref[lax.rem(g + 2 * where_ref[0], 4)] = placed[g * SHARE:(g + 1) * SHARE]


def final_tiles(early_at, late_at, where, got):
    return pl.pallas_call(
        functools.partial(final_kernel, early_at, late_at),
        in_specs=[IN_SMEM, IN_VMEM],
        out_specs=IN_VMEM,
        out_shape=jax.ShapeDtypeStruct((4, SHARE, PB), F32),
        compiler_params=pltpu.CompilerParams(vmem_limit_bytes=VMEM),
        name="final_tiles",
    )(where, whole(got))


def shared_out(x, at, onto):
    parts = [lax.dynamic_index_in_dim(x, (at + d) % SIDE, 0, keepdims=False) for d in range(SIDE)]
    return parts[:1] + [lax.ppermute(parts[d], "bas", [(j, onto(j, d)) for j in range(GROUP)]) for d in range(1, SIDE)]


def after(x, *others):
    return lax.optimization_barrier((x,) + others)[0]


def body(orbitals, owner_perm, pair_reach):
    me = lax.axis_index("pts")
    chips = PTS // 2
    swap = [(p, p ^ 1) for p in range(PTS)]
    onward = [(2 * z, (2 * z - 2) % PTS) for z in range(chips)] + [(2 * z + 1, (2 * z + 3) % PTS) for z in range(chips)]

    ids = jnp.arange(PTS, dtype=jnp.int32)
    three = jnp.arange(3, dtype=jnp.int32)[:, None]
    first_of = me + (three == 2) - (me % 2) * (three + 1)
    apart = (three == 1).astype(jnp.int32)
    live = (ids == first_of) & (apart < pair_reach[None, :]) & (ids + apart + 1 < PTS)
    flags = jnp.sum(live.astype(jnp.int32), axis=1)
    block = jnp.sum(jnp.where(owner_perm[:, None] == ids[None, :], ids[:, None], 0), axis=0)
    partner = block - 2 + 4 * (block % 2)
    there = (partner >= 0) & (partner < PTS)
    partner = jnp.clip(partner, 0, PTS - 1)
    mine = ids == me
    five = jnp.arange(5, dtype=jnp.int32)[:, None]
    facts = jnp.where(five == 0, block % 2, jnp.where(five == 1, block, jnp.where(five == 2, block ^ 1, partner)))
    facts = jnp.where(five == 4, there.astype(jnp.int32), facts)
    where = jnp.sum(jnp.where(mine, facts, 0), axis=1)
    pick = jnp.where(block == me, 0, jnp.where(block == (me ^ 1), 1, 2))

    other = lax.ppermute(orbitals, "pts", swap)
    (first,) = chunks(orbitals, 0, 1)
    second, mhi, mlo = chunks(after(orbitals, first), 1, 1, True)
    ohi, olo, local = local_units(after(other, second), mhi, mlo)
    sent = [first, second, *chunks(after(orbitals, local), 2, 2)]
    arrived = []
    for c, x in enumerate(sent):
        arrived.append(lax.ppermute(x if c < 2 else after(x, arrived[0]), "pts", onward))

    to_sum = lambda x: lax.all_to_all(x, "bas", 0, 0)
    kinds = [[("c", e, c, 0) for e in range(CHUNKS) for c in range(CHUNKS)]] + [step_units(c) for c in range(CHUNKS)]
    names = [[u[0] for u in k] for k in kinds]
    flat = [u for k in kinds[:EARLY] for u in k]
    per = -(-len(flat) // PTS)
    kind = jnp.array([u[3] for u in flat] + [0] * (per * PTS - len(flat)), jnp.int32).reshape(PTS, per)
    kind = jnp.sum(jnp.where(mine[:, None], kind, 0), axis=0)[None, :]
    source = jnp.where(kind == 0, block[:, None], jnp.where(kind == 1, block[:, None] ^ 1, partner[:, None]))
    source = source * per + jnp.arange(per)[None, :]
    source = jnp.where((kind == 2) & ~there[:, None], -1, source).reshape(-1)

    units = [local]
    parts = [to_sum(units[0])]

    def multiply(c, *first):
        units.append(arrived_units(c, mhi, mlo, ohi, olo, after(arrived[c], units[-1], *first)))

    multiply(0, flags, where, pick, source)
    parts.append(to_sum(units[1]))
    multiply(1, parts[0])
    parts.append(to_sum(units[2]))
    multiply(2, parts[1])
    parts.append(to_sum(units[3]))
    held = [after(x, units[3]) for x in parts[:3]]
    early = early_tiles(names[:3], flags, held, sum(len(x) for x in names[:3]))
    multiply(3, early)
    place = lax.axis_index("bas")
    along = shared_out(
        units[4].reshape((SIDE, SIDE) + units[4].shape[1:]),
        place // SIDE,
        lambda j, d: (j // SIDE + d) % SIDE * SIDE + j % SIDE,
    )
    early = early_tiles(names[3:EARLY], flags, [after(x, units[4]) for x in parts[3:EARLY]], per * PTS, (early,))
    spread = lax.all_to_all(early.reshape(PTS, per, SUB, LANES), "pts", 0, 0).reshape(PTS * per, SUB, LANES)
    line = along[0] + along[1] + along[2] + along[3]
    terms = shared_out(line, place % SIDE, lambda j, d: j // SIDE * SIDE + (j % SIDE + d) % SIDE)
    slots = [[], [], []]
    late_at = {}
    for u, (name, e, c, owner) in enumerate(kinds[EARLY]):
        late_at[(name, e, c)] = (owner, len(slots[owner]))
        slots[owner].append((u, name))
    size = max(len(x) for x in slots)
    early_at = {u[:3]: (n // per, size + n % per) for n, u in enumerate(flat)}
    got = lax.all_to_all(sendings(slots, flags, pick, source, spread, terms), "pts", 0, 0)
    return final_tiles(early_at, late_at, where, got)[None]


def solution(mesh):
    return jax.shard_map(
        body,
        mesh=mesh,
        in_specs=(P("bas", "pts"), P(), P()),
        out_specs=P("pts", None, "bas", None),
        check_vma=False,
    )
```

```python
import functools

import jax
import jax.numpy as jnp
from jax import lax
from jax.experimental import pallas as pl
from jax.experimental.pallas import tpu as pltpu
from jax.sharding import PartitionSpec as P

PB = 512
SHARE = 32
LANES = 128
SUB = 8
CHUNKS = PB // LANES
GROUP = LANES // SUB
SIDE = 4
PTS = 16
VMEM = 14 * 1024 * 1024
WIDE = 32 * 1024 * 1024
F32 = jnp.float32
BF16 = jnp.bfloat16
NT = (((1,), (1,)), ((), ()))
NN = (((1,), (0,)), ((), ()))


def whole(x):
    return pltpu.with_memory_space_constraint(x, pltpu.VMEM)


def in_hbm(x):
    return pltpu.with_memory_space_constraint(x, pltpu.HBM)


IN_VMEM = pl.BlockSpec(memory_space=pltpu.VMEM)
IN_SMEM = pl.BlockSpec(memory_space=pltpu.SMEM)
FLAG = {"c": 0, "am": 1, "ar": 1, "b": 2}
EARLY = 4


def dot(a, b, dims):
    return lax.dot_general(a, b, dims, preferred_element_type=F32)


def split2(x):
    hi = x.astype(BF16)
    return hi, (x - hi.astype(F32)).astype(BF16)


def row_block(depth, most=768):
    for size in (768, 640, 512, 384, 256, 128):
        if size <= most and depth % size == 0:
            return size
    return depth


ANY = pl.BlockSpec(memory_space=pl.ANY)


def piece(k, rows):
    return pl.ds(pl.multiple_of(k * rows, rows), rows)


class Flow:
    def __init__(self, src, dst, sems, count):
        self.src, self.dst, self.sems, self.count = src, dst, sems, count

    def copy(self, k):
        return pltpu.make_async_copy(self.src(k), self.dst(k), self.sems.at[k])

    def start(self):
        for k in range(self.count):
            self.copy(k).start()

    def wait(self):
        for k in range(self.count):
            self.copy(k).wait()


def by_rows(src, dst, sems, rows, count):
    return Flow(lambda k: src.at[piece(k, rows)], lambda k: dst.at[piece(k, rows)], sems, count)


def by_lanes(src, dst, sems, rows, count):
    return Flow(lambda k: src.at[:, piece(k, rows)], lambda k: dst.at[:, piece(k, rows)], sems, count)


def start_all(flows):
    for k in range(flows[0].count):
        for flow in flows:
            flow.copy(k).start()


def turned(x):
    t = x.T
    return jnp.swapaxes(t.reshape(GROUP, CHUNKS, SUB, t.shape[1]), 0, 1).reshape(t.shape)


def turned_back(t):
    x = jnp.swapaxes(t.reshape(CHUNKS, GROUP, SUB, t.shape[1]), 0, 1).reshape(t.shape)
    return x.T


def chunks_kernel(chunk0, number, count, rows, x_hbm, *refs):
    outs = (len(refs) - 3) // 2
    out_hbm, (x_ref, *out_refs, in_sems, out_sems) = refs[:outs], refs[outs:]
    coming = by_rows(x_hbm, x_ref, in_sems, rows, count)
    going = [
        (by_rows if n < number else by_lanes)(ref, out_hbm[n], out_sems.at[n], rows, count)
        for n, ref in enumerate(out_refs)
    ]
    coming.start()

    @pl.loop(0, count)
    def _(k):
        coming.copy(k).wait()
        at = piece(k, rows)
        t = turned(x_ref[at])
        for n in range(number):
            out_refs[n][at] = t[(chunk0 + n) * LANES:(chunk0 + n + 1) * LANES].T
        if outs > number:
            out_refs[number][:, at], out_refs[number + 1][:, at] = split2(t)
        for flow in going:
            flow.copy(k).start()

    for flow in going:
        flow.wait()


def chunks(x, chunk0, number, with_turned=False):
    depth = x.shape[0]
    rows = row_block(depth)
    count = depth // rows
    kinds = [((depth, LANES), F32)] * number + [((PB, depth), BF16)] * (2 if with_turned else 0)
    return pl.pallas_call(
        functools.partial(chunks_kernel, chunk0, number, count, rows),
        in_specs=[ANY],
        out_specs=[ANY] * len(kinds),
        out_shape=[pltpu.HBM(*kind) for kind in kinds],
        scratch_shapes=[pltpu.VMEM((depth, PB), F32)]
        + [pltpu.VMEM(*kind) for kind in kinds]
        + [pltpu.SemaphoreType.DMA((count,)), pltpu.SemaphoreType.DMA((len(kinds), count))],
        compiler_params=pltpu.CompilerParams(vmem_limit_bytes=WIDE),
        cost_estimate=pl.CostEstimate(
            flops=9 * depth * PB * PB, bytes_accessed=4 * depth * (PB + LANES * number), transcendentals=0
        ),
        name="chunks",
    )(in_hbm(x))


def local_kernel(
    count, rows, o_hbm, mhi_hbm, mlo_hbm, ohi_hbm, olo_hbm, out_ref,
    o_ref, mhi_ref, mlo_ref, ohi_ref, olo_ref, acc_ref, in_sems, out_sems,
):
    coming = [
        by_rows(o_hbm, o_ref, in_sems.at[0], rows, count),
        by_lanes(mhi_hbm, mhi_ref, in_sems.at[1], rows, count),
        by_lanes(mlo_hbm, mlo_ref, in_sems.at[2], rows, count),
    ]
    going = [
        by_lanes(ohi_ref, ohi_hbm, out_sems.at[0], rows, count),
        by_lanes(olo_ref, olo_hbm, out_sems.at[1], rows, count),
    ]
    start_all(coming)
    acc_ref[...] = jnp.zeros_like(acc_ref)

    @pl.loop(0, count)
    def _(k):
        at = piece(k, rows)
        for flow in coming:
            flow.copy(k).wait()
        ohi, olo = split2(turned(o_ref[at]))
        ohi_ref[:, at] = ohi
        olo_ref[:, at] = olo
        mhi = mhi_ref[:, at]
        acc_ref[...] += dot(mhi, ohi, NT) + dot(mhi, olo, NT) + dot(mlo_ref[:, at], ohi, NT)
        for flow in going:
            flow.copy(k).start()

    for e in range(CHUNKS):
        for c in range(CHUNKS):
            put(out_ref, CHUNKS * e + c, acc_ref[e * LANES:(e + 1) * LANES, c * LANES:(c + 1) * LANES])
    for flow in going:
        flow.wait()


def local_units(other, mhi, mlo):
    depth = other.shape[0]
    rows = row_block(depth)
    count = depth // rows
    units = CHUNKS * CHUNKS
    wide = pltpu.VMEM((PB, depth), BF16)
    return pl.pallas_call(
        functools.partial(local_kernel, count, rows),
        in_specs=[ANY] * 3,
        out_specs=[ANY, ANY, pl.BlockSpec((GROUP, units, SUB, LANES))],
        out_shape=[pltpu.HBM((PB, depth), BF16)] * 2 + [pltpu.HBM((GROUP, units, SUB, LANES), F32)],
        scratch_shapes=[
            pltpu.VMEM((depth, PB), F32), wide, wide, wide, wide,
            pltpu.VMEM((PB, PB), F32),
            pltpu.SemaphoreType.DMA((3, count)),
            pltpu.SemaphoreType.DMA((2, count)),
        ],
        compiler_params=pltpu.CompilerParams(vmem_limit_bytes=WIDE),
        cost_estimate=pl.CostEstimate(flops=10 * depth * PB * PB, bytes_accessed=12 * depth * PB, transcendentals=0),
        name="local_units",
    )(in_hbm(other), in_hbm(mhi), in_hbm(mlo))


def put(out_ref, unit, block):
    out_ref[:, unit] = block.reshape(GROUP, SUB, LANES)


IN_VMEM = pl.BlockSpec(memory_space=pltpu.VMEM)
IN_SMEM = pl.BlockSpec(memory_space=pltpu.SMEM)
FLAG = {"c": 0, "am": 1, "ar": 1, "b": 2}
EARLY = 4


def step_units(c):
    units = [("am", e, c, 0) for e in range(CHUNKS)]
    units += [("ar", c, e, 2) for e in range(CHUNKS)]
    units += [("b", e, c, 1) for e in range(c, CHUNKS)]
    units += [("b", c, e, 2) for e in range(c + 1, CHUNKS)]
    return units


def step_kernel(c, begin, count, rows, first, last, apart, *refs):
    if apart:
        place_ref, refs = refs[0], refs[1:]
    mhi_hbm, mlo_hbm, ohi_hbm, olo_hbm, r_hbm, refs = *refs[:5], refs[5:]
    if not first:
        wide_hbm, slim_hbm, refs = *refs[:2], refs[2:]
    outs = 2 if not last else SIDE if apart else 1
    out_refs, (hi_ref, lo_ref, r_ref, wide_ref, slim_ref, units_ref, sems, total_sems) = refs[:outs], refs[outs:]
    left = (CHUNKS - c) * LANES

    def lanes(src, dst, sem, at, base, n):
        return Flow(
            lambda k: src.at[pl.ds(at, n), piece(begin + k, rows)],
            lambda k: dst.at[pl.ds(base, n), piece(k, rows)],
            sem,
            count,
        )

    coming = [
        by_rows(r_hbm, r_ref, sems.at[0], rows, count),
        lanes(mhi_hbm, hi_ref, sems.at[1], 0, 0, PB),
        lanes(ohi_hbm, hi_ref, sems.at[2], PB - left, PB, left),
        lanes(mlo_hbm, lo_ref, sems.at[3], 0, 0, PB),
        lanes(olo_hbm, lo_ref, sems.at[4], PB - left, PB, left),
    ]
    totals = []
    if first:
        wide_ref[...] = jnp.zeros_like(wide_ref)
        slim_ref[...] = jnp.zeros_like(slim_ref)
    else:
        totals = [
            pltpu.make_async_copy(wide_hbm, wide_ref, total_sems.at[0]),
            pltpu.make_async_copy(slim_hbm, slim_ref, total_sems.at[1]),
        ]
    for total in totals:
        total.start()
    start_all(coming)
    for total in totals:
        total.wait()

    @pl.loop(0, count)
    def _(k):
        at = piece(k, rows)
        for flow in coming:
            flow.copy(k).wait()
        rhi, rlo = split2(r_ref[at])
        wide_ref[...] += dot(hi_ref[:, at], jnp.concatenate([rhi, rlo], axis=1), NN)
        slim_ref[...] += dot(lo_ref[:, at], rhi, NN)

    if not last:
        out_refs[0][...] = wide_ref[...]
        out_refs[1][...] = slim_ref[...]
        return

    def block(n):
        rows = slice(n * LANES, (n + 1) * LANES)
        return wide_ref[rows, :LANES] + (wide_ref[rows, LANES:] + slim_ref[rows])

    out_ref = units_ref if apart else out_refs[0]
    for e in range(CHUNKS):
        a = block(e)
        put(out_ref, e, a)
        put(out_ref, CHUNKS + e, a.T)
    for e in range(c, CHUNKS):
        b = block(CHUNKS + e - c)
        put(out_ref, 2 * CHUNKS + e - c, b)
        if e > c:
            put(out_ref, 3 * CHUNKS + e - 2 * c - 1, b.T)
    if apart:
        for d in range(SIDE):
            out_refs[d][...] = units_ref[pl.ds(lax.rem(place_ref[0] + d, SIDE) * SIDE, SIDE)]


def arrived_units(c, mhi, mlo, ohi, olo, r, begin=0, totals=None, last=True, place=None):
    depth = r.shape[0]
    rows = row_block(mhi.shape[1])
    count = depth // rows
    units = len(step_units(c))
    lines = PB + (CHUNKS - c) * LANES
    apart = place is not None
    whole_units = (GROUP, units, SUB, LANES)
    if not last:
        shapes = [pltpu.HBM((lines, 2 * LANES), F32), pltpu.HBM((lines, LANES), F32)]
    elif apart:
        shapes = [jax.ShapeDtypeStruct((SIDE, units, SUB, LANES), F32)] * SIDE
    else:
        shapes = [pltpu.HBM(whole_units, F32)]
    got = pl.pallas_call(
        functools.partial(step_kernel, c, begin // rows, count, rows, totals is None, last, apart),
        in_specs=[IN_SMEM] * apart + [ANY] * (5 if totals is None else 7),
        out_specs=[pl.BlockSpec(shape.shape) for shape in shapes],
        out_shape=shapes,
        scratch_shapes=[
            pltpu.VMEM((lines, depth), BF16),
            pltpu.VMEM((lines, depth), BF16),
            pltpu.VMEM((depth, LANES), F32),
            pltpu.VMEM((lines, 2 * LANES), F32),
            pltpu.VMEM((lines, LANES), F32),
            pltpu.VMEM(whole_units, F32),
            pltpu.SemaphoreType.DMA((5, count)),
            pltpu.SemaphoreType.DMA((2,)),
        ],
        compiler_params=pltpu.CompilerParams(vmem_limit_bytes=WIDE),
        cost_estimate=pl.CostEstimate(
            flops=6 * depth * lines * LANES, bytes_accessed=4 * depth * (lines + LANES), transcendentals=0
        ),
        name="arrived_units",
    )(*([place] if apart else []), *[in_hbm(x) for x in (mhi, mlo, ohi, olo, r, *(totals or ()))])
    return got if apart or not last else got[0]


def squares(parts_ref, unit, flag):
    gram = parts_ref[0, unit]
    for n in range(1, GROUP):
        gram = gram + parts_ref[n, unit]
    return jnp.where(flag != 0, gram * gram, 0.0)


def early_kernel(names, kept, flags_ref, *refs):
    part_refs, out_ref = refs[:-1], refs[-1]
    n = 0
    if kept:
        n = part_refs[0].shape[0]
        out_ref[:n] = part_refs[0][...]
        part_refs = part_refs[1:]
    for part_ref, units in zip(part_refs, names):
        for u, name in enumerate(units):
            out_ref[n] = squares(part_ref, u, flags_ref[FLAG[name]])
            n += 1
    for pad in range(n, out_ref.shape[0]):
        out_ref[pad] = jnp.zeros((SUB, LANES), F32)


def early_tiles(names, flags, parts, count, kept=()):
    return pl.pallas_call(
        functools.partial(early_kernel, names, len(kept)),
        in_specs=[IN_SMEM] + [IN_VMEM] * (len(kept) + len(parts)),
        out_specs=IN_VMEM,
        out_shape=pltpu.HBM((count, SUB, LANES), F32),
        compiler_params=pltpu.CompilerParams(vmem_limit_bytes=VMEM),
        name="early_tiles",
    )(flags, *[whole(x) for x in (*kept, *parts)])


def send_kernel(slots, flags_ref, pick_ref, source_ref, spread_ref, *refs):
    term_refs, out_ref, held_ref = refs[:-2], refs[-2], refs[-1]
    size = held_ref.shape[1]
    per = out_ref.shape[1] - size
    for kind, units in enumerate(slots):
        for n, (u, name) in enumerate(units):
            gram = term_refs[0][u]
            for term_ref in term_refs[1:]:
                gram = gram + term_ref[u]
            held_ref[kind, n] = jnp.where(flags_ref[FLAG[name]] != 0, gram * gram, 0.0)
        for n in range(len(units), size):
            held_ref[kind, n] = jnp.zeros((SUB, LANES), F32)

    @pl.loop(0, PTS)
    def _(k):
        out_ref[k, :size] = held_ref[pick_ref[k]]
        for n in range(per):
            at = source_ref[k * per + n]
            out_ref[k, size + n] = jnp.where(at >= 0, spread_ref[jnp.maximum(at, 0)], 0.0)


def sendings(slots, flags, pick, source, spread, terms):
    size = max(len(units) for units in slots)
    per = spread.shape[0] // PTS
    return pl.pallas_call(
        functools.partial(send_kernel, slots),
        in_specs=[IN_SMEM] * 3 + [IN_VMEM] * (1 + len(terms)),
        out_specs=IN_VMEM,
        out_shape=jax.ShapeDtypeStruct((PTS, size + per, SUB, LANES), F32),
        scratch_shapes=[pltpu.VMEM((len(slots), size, SUB, LANES), F32)],
        compiler_params=pltpu.CompilerParams(vmem_limit_bytes=VMEM),
        name="sendings",
    )(flags, pick, source, whole(spread), *[whole(x) for x in terms])


def final_kernel(early_at, late_at, where_ref, got_ref, out_ref):
    def unit(name, e, c):
        if (name, e, c) in early_at:
            return got_ref[early_at[(name, e, c)]]
        kind, slot = late_at[(name, e, c)]
        got = got_ref[where_ref[1 + kind], slot]
        return jnp.where(where_ref[4] != 0, got, 0.0) if kind == 2 else got

    groups = ("c", "am", "b", "ar")
    sides = [jnp.concatenate([unit(g, e, c) for g in groups for e in range(CHUNKS)], axis=0).T for c in range(CHUNKS)]
    placed = turned_back(jnp.concatenate(sides, axis=0))
    for g in range(len(groups)):
        out_ref[lax.rem(g + 2 * where_ref[0], 4)] = placed[g * SHARE:(g + 1) * SHARE]


def final_tiles(early_at, late_at, where, got):
    return pl.pallas_call(
        functools.partial(final_kernel, early_at, late_at),
        in_specs=[IN_SMEM, IN_VMEM],
        out_specs=IN_VMEM,
        out_shape=jax.ShapeDtypeStruct((4, SHARE, PB), F32),
        compiler_params=pltpu.CompilerParams(vmem_limit_bytes=VMEM),
        name="final_tiles",
    )(where, whole(got))


def shared_out(parts, onto):
    return [parts[0]] + [
        lax.ppermute(parts[d], "bas", [(j, onto(j, d)) for j in range(GROUP)]) for d in range(1, SIDE)
    ]


def after(x, *others):
    return lax.optimization_barrier((x,) + others)[0]


def body(orbitals, owner_perm, pair_reach):
    me = lax.axis_index("pts")
    chips = PTS // 2
    swap = [(p, p ^ 1) for p in range(PTS)]
    onward = [(2 * z, (2 * z - 2) % PTS) for z in range(chips)] + [(2 * z + 1, (2 * z + 3) % PTS) for z in range(chips)]

    ids = jnp.arange(PTS, dtype=jnp.int32)
    three = jnp.arange(3, dtype=jnp.int32)[:, None]
    first_of = me + (three == 2) - (me % 2) * (three + 1)
    apart = (three == 1).astype(jnp.int32)
    live = (ids == first_of) & (apart < pair_reach[None, :]) & (ids + apart + 1 < PTS)
    flags = jnp.sum(live.astype(jnp.int32), axis=1)
    block = jnp.sum(jnp.where(owner_perm[:, None] == ids[None, :], ids[:, None], 0), axis=0)
    partner = block - 2 + 4 * (block % 2)
    there = (partner >= 0) & (partner < PTS)
    partner = jnp.clip(partner, 0, PTS - 1)
    mine = ids == me
    five = jnp.arange(5, dtype=jnp.int32)[:, None]
    facts = jnp.where(five == 0, block % 2, jnp.where(five == 1, block, jnp.where(five == 2, block ^ 1, partner)))
    facts = jnp.where(five == 4, there.astype(jnp.int32), facts)
    where = jnp.sum(jnp.where(mine, facts, 0), axis=1)
    pick = jnp.where(block == me, 0, jnp.where(block == (me ^ 1), 1, 2))

    other = lax.ppermute(orbitals, "pts", swap)
    (first,) = chunks(orbitals, 0, 1)
    second, mhi, mlo = chunks(after(orbitals, first), 1, 1, True)
    ohi, olo, local = local_units(after(other, second), mhi, mlo)
    third, fourth = chunks(after(orbitals, local), 2, 2)
    cut = 2 * row_block(fourth.shape[0])
    sent = [first, second, third, fourth[:cut], fourth[cut:]]
    arrived = []
    for c, x in enumerate(sent):
        arrived.append(lax.ppermute(x if c < 2 else after(x, arrived[0]), "pts", onward))

    to_sum = lambda x: lax.all_to_all(x, "bas", 0, 0)
    kinds = [[("c", e, c, 0) for e in range(CHUNKS) for c in range(CHUNKS)]] + [step_units(c) for c in range(CHUNKS)]
    names = [[u[0] for u in k] for k in kinds]
    flat = [u for k in kinds[:EARLY] for u in k]
    per = -(-len(flat) // PTS)
    kind = jnp.array([u[3] for u in flat] + [0] * (per * PTS - len(flat)), jnp.int32).reshape(PTS, per)
    kind = jnp.sum(jnp.where(mine[:, None], kind, 0), axis=0)[None, :]
    source = jnp.where(kind == 0, block[:, None], jnp.where(kind == 1, block[:, None] ^ 1, partner[:, None]))
    source = source * per + jnp.arange(per)[None, :]
    source = jnp.where((kind == 2) & ~there[:, None], -1, source).reshape(-1)

    units = [local]
    parts = [to_sum(units[0])]

    def multiply(c, *first):
        units.append(arrived_units(c, mhi, mlo, ohi, olo, after(arrived[c], units[-1], *first)))

    multiply(0, flags, where, pick, source)
    parts.append(to_sum(units[1]))
    multiply(1, parts[0])
    parts.append(to_sum(units[2]))
    multiply(2, parts[1])
    place = lax.axis_index("bas")
    totals = arrived_units(3, mhi, mlo, ohi, olo, after(arrived[3], units[3]), last=False)
    early = early_tiles(names[:2], flags, [after(x, units[3]) for x in parts[:2]], sum(len(x) for x in names[:2]))
    parts.append(to_sum(after(units[3], *totals, early)))
    along = arrived_units(
        3, mhi, mlo, ohi, olo, after(arrived[4], *totals, early), begin=arrived[3].shape[0], totals=totals,
        place=(place // SIDE).astype(jnp.int32)[None],
    )
    early = early_tiles(
        names[2:EARLY], flags, [after(x, along[0]) for x in parts[2:EARLY]], per * PTS, (early,)
    )
    spread = lax.all_to_all(early.reshape(PTS, per, SUB, LANES), "pts", 0, 0).reshape(PTS * per, SUB, LANES)
    along = shared_out(along, lambda j, d: (j // SIDE + d) % SIDE * SIDE + j % SIDE)
    line = along[0] + along[1] + along[2] + along[3]
    onward_parts = [lax.dynamic_index_in_dim(line, (place % SIDE + d) % SIDE, 0, keepdims=False) for d in range(SIDE)]
    terms = shared_out(onward_parts, lambda j, d: j // SIDE * SIDE + (j % SIDE + d) % SIDE)
    slots = [[], [], []]
    late_at = {}
    for u, (name, e, c, owner) in enumerate(kinds[EARLY]):
        late_at[(name, e, c)] = (owner, len(slots[owner]))
        slots[owner].append((u, name))
    size = max(len(x) for x in slots)
    early_at = {u[:3]: (n // per, size + n % per) for n, u in enumerate(flat)}
    got = lax.all_to_all(sendings(slots, flags, pick, source, spread, terms), "pts", 0, 0)
    return final_tiles(early_at, late_at, where, got)[None]


def solution(mesh):
    return jax.shard_map(
        body,
        mesh=mesh,
        in_specs=(P("bas", "pts"), P(), P()),
        out_specs=P("pts", None, "bas", None),
        check_vma=False,
    )
```

```python
import functools

import jax
import jax.numpy as jnp
from jax import lax
from jax.experimental import pallas as pl
from jax.experimental.pallas import tpu as pltpu
from jax.sharding import PartitionSpec as P

PB = 512
SHARE = 32
LANES = 128
SUB = 8
CHUNKS = PB // LANES
GROUP = LANES // SUB
SIDE = 4
PTS = 16
VMEM = 14 * 1024 * 1024
WIDE = 32 * 1024 * 1024
F32 = jnp.float32
BF16 = jnp.bfloat16
NT = (((1,), (1,)), ((), ()))
NN = (((1,), (0,)), ((), ()))


def whole(x):
    return pltpu.with_memory_space_constraint(x, pltpu.VMEM)


def in_hbm(x):
    return pltpu.with_memory_space_constraint(x, pltpu.HBM)


IN_VMEM = pl.BlockSpec(memory_space=pltpu.VMEM)
IN_SMEM = pl.BlockSpec(memory_space=pltpu.SMEM)
FLAG = {"c": 0, "am": 1, "ar": 1, "b": 2}
EARLY = 4


def dot(a, b, dims):
    return lax.dot_general(a, b, dims, preferred_element_type=F32)


def split2(x):
    hi = x.astype(BF16)
    return hi, (x - hi.astype(F32)).astype(BF16)


def row_block(depth, most=768):
    for size in (768, 640, 512, 384, 256, 128):
        if size <= most and depth % size == 0:
            return size
    return depth


ANY = pl.BlockSpec(memory_space=pl.ANY)


def piece(k, rows):
    return pl.ds(pl.multiple_of(k * rows, rows), rows)


class Flow:
    def __init__(self, src, dst, sems, count):
        self.src, self.dst, self.sems, self.count = src, dst, sems, count

    def copy(self, k):
        return pltpu.make_async_copy(self.src(k), self.dst(k), self.sems.at[k])

    def start(self):
        for k in range(self.count):
            self.copy(k).start()

    def wait(self):
        for k in range(self.count):
            self.copy(k).wait()


def by_rows(src, dst, sems, rows, count):
    return Flow(lambda k: src.at[piece(k, rows)], lambda k: dst.at[piece(k, rows)], sems, count)


def by_lanes(src, dst, sems, rows, count):
    return Flow(lambda k: src.at[:, piece(k, rows)], lambda k: dst.at[:, piece(k, rows)], sems, count)


def start_all(flows):
    for k in range(flows[0].count):
        for flow in flows:
            flow.copy(k).start()


def turned(x):
    t = x.T
    return jnp.swapaxes(t.reshape(GROUP, CHUNKS, SUB, t.shape[1]), 0, 1).reshape(t.shape)


def turned_back(t):
    x = jnp.swapaxes(t.reshape(CHUNKS, GROUP, SUB, t.shape[1]), 0, 1).reshape(t.shape)
    return x.T


def chunks_kernel(chunk0, number, count, rows, x_hbm, *refs):
    outs = (len(refs) - 3) // 2
    out_hbm, (x_ref, *out_refs, in_sems, out_sems) = refs[:outs], refs[outs:]
    coming = by_rows(x_hbm, x_ref, in_sems, rows, count)
    going = [
        (by_rows if n < number else by_lanes)(ref, out_hbm[n], out_sems.at[n], rows, count)
        for n, ref in enumerate(out_refs)
    ]
    coming.start()

    @pl.loop(0, count)
    def _(k):
        coming.copy(k).wait()
        at = piece(k, rows)
        t = turned(x_ref[at])
        for n in range(number):
            out_refs[n][at] = t[(chunk0 + n) * LANES:(chunk0 + n + 1) * LANES].T
        if outs > number:
            out_refs[number][:, at], out_refs[number + 1][:, at] = split2(t)
        for flow in going:
            flow.copy(k).start()

    for flow in going:
        flow.wait()


def chunks(x, chunk0, number, with_turned=False):
    depth = x.shape[0]
    rows = row_block(depth)
    count = depth // rows
    kinds = [((depth, LANES), F32)] * number + [((PB, depth), BF16)] * (2 if with_turned else 0)
    return pl.pallas_call(
        functools.partial(chunks_kernel, chunk0, number, count, rows),
        in_specs=[ANY],
        out_specs=[ANY] * len(kinds),
        out_shape=[pltpu.HBM(*kind) for kind in kinds],
        scratch_shapes=[pltpu.VMEM((depth, PB), F32)]
        + [pltpu.VMEM(*kind) for kind in kinds]
        + [pltpu.SemaphoreType.DMA((count,)), pltpu.SemaphoreType.DMA((len(kinds), count))],
        compiler_params=pltpu.CompilerParams(vmem_limit_bytes=WIDE),
        cost_estimate=pl.CostEstimate(
            flops=9 * depth * PB * PB, bytes_accessed=4 * depth * (PB + LANES * number), transcendentals=0
        ),
        name="chunks",
    )(in_hbm(x))


def local_kernel(
    count, rows, o_hbm, mhi_hbm, mlo_hbm, ohi_hbm, olo_hbm, out_ref,
    o_ref, mhi_ref, mlo_ref, ohi_ref, olo_ref, acc_ref, in_sems, out_sems,
):
    coming = [
        by_rows(o_hbm, o_ref, in_sems.at[0], rows, count),
        by_lanes(mhi_hbm, mhi_ref, in_sems.at[1], rows, count),
        by_lanes(mlo_hbm, mlo_ref, in_sems.at[2], rows, count),
    ]
    going = [
        by_lanes(ohi_ref, ohi_hbm, out_sems.at[0], rows, count),
        by_lanes(olo_ref, olo_hbm, out_sems.at[1], rows, count),
    ]
    start_all(coming)
    acc_ref[...] = jnp.zeros_like(acc_ref)

    @pl.loop(0, count)
    def _(k):
        at = piece(k, rows)
        for flow in coming:
            flow.copy(k).wait()
        ohi, olo = split2(turned(o_ref[at]))
        ohi_ref[:, at] = ohi
        olo_ref[:, at] = olo
        mhi = mhi_ref[:, at]
        acc_ref[...] += dot(mhi, ohi, NT) + dot(mhi, olo, NT) + dot(mlo_ref[:, at], ohi, NT)
        for flow in going:
            flow.copy(k).start()

    for e in range(CHUNKS):
        for c in range(CHUNKS):
            put(out_ref, CHUNKS * e + c, acc_ref[e * LANES:(e + 1) * LANES, c * LANES:(c + 1) * LANES])
    for flow in going:
        flow.wait()


def local_units(other, mhi, mlo):
    depth = other.shape[0]
    rows = row_block(depth)
    count = depth // rows
    units = CHUNKS * CHUNKS
    wide = pltpu.VMEM((PB, depth), BF16)
    return pl.pallas_call(
        functools.partial(local_kernel, count, rows),
        in_specs=[ANY] * 3,
        out_specs=[ANY, ANY, pl.BlockSpec((GROUP, units, SUB, LANES))],
        out_shape=[pltpu.HBM((PB, depth), BF16)] * 2 + [pltpu.HBM((GROUP, units, SUB, LANES), F32)],
        scratch_shapes=[
            pltpu.VMEM((depth, PB), F32), wide, wide, wide, wide,
            pltpu.VMEM((PB, PB), F32),
            pltpu.SemaphoreType.DMA((3, count)),
            pltpu.SemaphoreType.DMA((2, count)),
        ],
        compiler_params=pltpu.CompilerParams(vmem_limit_bytes=WIDE),
        cost_estimate=pl.CostEstimate(flops=10 * depth * PB * PB, bytes_accessed=12 * depth * PB, transcendentals=0),
        name="local_units",
    )(in_hbm(other), in_hbm(mhi), in_hbm(mlo))


def put(out_ref, unit, block):
    out_ref[:, unit] = block.reshape(GROUP, SUB, LANES)


IN_VMEM = pl.BlockSpec(memory_space=pltpu.VMEM)
IN_SMEM = pl.BlockSpec(memory_space=pltpu.SMEM)
FLAG = {"c": 0, "am": 1, "ar": 1, "b": 2}
EARLY = 4


def step_units(c):
    units = [("am", e, c, 0) for e in range(CHUNKS)]
    units += [("ar", c, e, 2) for e in range(CHUNKS)]
    units += [("b", e, c, 1) for e in range(c, CHUNKS)]
    units += [("b", c, e, 2) for e in range(c + 1, CHUNKS)]
    return units


def step_kernel(c, count, rows, apart, *refs):
    if apart:
        place_ref, refs = refs[0], refs[1:]
    mhi_hbm, mlo_hbm, ohi_hbm, olo_hbm, r_hbm, refs = *refs[:5], refs[5:]
    outs = SIDE if apart else 1
    out_refs, (hi_ref, lo_ref, r_ref, wide_ref, slim_ref, units_ref, sems) = refs[:outs], refs[outs:]
    left = (CHUNKS - c) * LANES

    def lanes(src, dst, sem, at, base, n):
        return Flow(
            lambda k: src.at[pl.ds(at, n), piece(k, rows)],
            lambda k: dst.at[pl.ds(base, n), piece(k, rows)],
            sem,
            count,
        )

    coming = [
        by_rows(r_hbm, r_ref, sems.at[0], rows, count),
        lanes(mhi_hbm, hi_ref, sems.at[1], 0, 0, PB),
        lanes(ohi_hbm, hi_ref, sems.at[2], PB - left, PB, left),
        lanes(mlo_hbm, lo_ref, sems.at[3], 0, 0, PB),
        lanes(olo_hbm, lo_ref, sems.at[4], PB - left, PB, left),
    ]
    start_all(coming)
    wide_ref[...] = jnp.zeros_like(wide_ref)
    slim_ref[...] = jnp.zeros_like(slim_ref)

    @pl.loop(0, count)
    def _(k):
        at = piece(k, rows)
        for flow in coming:
            flow.copy(k).wait()
        rhi, rlo = split2(r_ref[at])
        wide_ref[...] += dot(hi_ref[:, at], jnp.concatenate([rhi, rlo], axis=1), NN)
        slim_ref[...] += dot(lo_ref[:, at], rhi, NN)

    def block(n):
        rows = slice(n * LANES, (n + 1) * LANES)
        return wide_ref[rows, :LANES] + (wide_ref[rows, LANES:] + slim_ref[rows])

    out_ref = units_ref if apart else out_refs[0]
    for e in range(CHUNKS):
        a = block(e)
        put(out_ref, e, a)
        put(out_ref, CHUNKS + e, a.T)
    for e in range(c, CHUNKS):
        b = block(CHUNKS + e - c)
        put(out_ref, 2 * CHUNKS + e - c, b)
        if e > c:
            put(out_ref, 3 * CHUNKS + e - 2 * c - 1, b.T)
    if apart:
        for d in range(SIDE):
            out_refs[d][...] = units_ref[pl.ds(lax.rem(place_ref[0] + d, SIDE) * SIDE, SIDE)]


def arrived_units(c, mhi, mlo, ohi, olo, r, place=None):
    depth = r.shape[0]
    rows = row_block(mhi.shape[1])
    count = depth // rows
    units = len(step_units(c))
    lines = PB + (CHUNKS - c) * LANES
    apart = place is not None
    whole_units = (GROUP, units, SUB, LANES)
    if apart:
        shapes = [jax.ShapeDtypeStruct((SIDE, units, SUB, LANES), F32)] * SIDE
    else:
        shapes = [pltpu.HBM(whole_units, F32)]
    got = pl.pallas_call(
        functools.partial(step_kernel, c, count, rows, apart),
        in_specs=[IN_SMEM] * apart + [ANY] * 5,
        out_specs=[pl.BlockSpec(shape.shape) for shape in shapes],
        out_shape=shapes,
        scratch_shapes=[
            pltpu.VMEM((lines, depth), BF16),
            pltpu.VMEM((lines, depth), BF16),
            pltpu.VMEM((depth, LANES), F32),
            pltpu.VMEM((lines, 2 * LANES), F32),
            pltpu.VMEM((lines, LANES), F32),
            pltpu.VMEM(whole_units, F32),
            pltpu.SemaphoreType.DMA((5, count)),
        ],
        compiler_params=pltpu.CompilerParams(vmem_limit_bytes=WIDE),
        cost_estimate=pl.CostEstimate(
            flops=6 * depth * lines * LANES, bytes_accessed=4 * depth * (lines + LANES), transcendentals=0
        ),
        name="arrived_units",
    )(*([place] if apart else []), *[in_hbm(x) for x in (mhi, mlo, ohi, olo, r)])
    return got if apart else got[0]


def squares(parts_ref, unit, flag):
    gram = parts_ref[0, unit]
    for n in range(1, GROUP):
        gram = gram + parts_ref[n, unit]
    return jnp.where(flag != 0, gram * gram, 0.0)


def early_kernel(names, kept, flags_ref, *refs):
    part_refs, out_ref = refs[:-1], refs[-1]
    n = 0
    if kept:
        n = part_refs[0].shape[0]
        out_ref[:n] = part_refs[0][...]
        part_refs = part_refs[1:]
    for part_ref, units in zip(part_refs, names):
        for u, name in enumerate(units):
            out_ref[n] = squares(part_ref, u, flags_ref[FLAG[name]])
            n += 1
    for pad in range(n, out_ref.shape[0]):
        out_ref[pad] = jnp.zeros((SUB, LANES), F32)


def early_tiles(names, flags, parts, count, kept=()):
    return pl.pallas_call(
        functools.partial(early_kernel, names, len(kept)),
        in_specs=[IN_SMEM] + [IN_VMEM] * (len(kept) + len(parts)),
        out_specs=IN_VMEM,
        out_shape=pltpu.HBM((count, SUB, LANES), F32),
        compiler_params=pltpu.CompilerParams(vmem_limit_bytes=VMEM),
        name="early_tiles",
    )(flags, *[whole(x) for x in (*kept, *parts)])


def send_kernel(slots, flags_ref, pick_ref, source_ref, spread_ref, *refs):
    term_refs, out_ref, held_ref = refs[:-2], refs[-2], refs[-1]
    size = held_ref.shape[1]
    per = out_ref.shape[1] - size
    for kind, units in enumerate(slots):
        for n, (u, name) in enumerate(units):
            gram = term_refs[0][u]
            for term_ref in term_refs[1:]:
                gram = gram + term_ref[u]
            held_ref[kind, n] = jnp.where(flags_ref[FLAG[name]] != 0, gram * gram, 0.0)
        for n in range(len(units), size):
            held_ref[kind, n] = jnp.zeros((SUB, LANES), F32)

    @pl.loop(0, PTS)
    def _(k):
        out_ref[k, :size] = held_ref[pick_ref[k]]
        for n in range(per):
            at = source_ref[k * per + n]
            out_ref[k, size + n] = jnp.where(at >= 0, spread_ref[jnp.maximum(at, 0)], 0.0)


def sendings(slots, flags, pick, source, spread, terms):
    size = max(len(units) for units in slots)
    per = spread.shape[0] // PTS
    return pl.pallas_call(
        functools.partial(send_kernel, slots),
        in_specs=[IN_SMEM] * 3 + [IN_VMEM] * (1 + len(terms)),
        out_specs=IN_VMEM,
        out_shape=jax.ShapeDtypeStruct((PTS, size + per, SUB, LANES), F32),
        scratch_shapes=[pltpu.VMEM((len(slots), size, SUB, LANES), F32)],
        compiler_params=pltpu.CompilerParams(vmem_limit_bytes=VMEM),
        name="sendings",
    )(flags, pick, source, whole(spread), *[whole(x) for x in terms])


def final_kernel(early_at, late_at, where_ref, got_ref, out_ref):
    def unit(name, e, c):
        if (name, e, c) in early_at:
            return got_ref[early_at[(name, e, c)]]
        kind, slot = late_at[(name, e, c)]
        got = got_ref[where_ref[1 + kind], slot]
        return jnp.where(where_ref[4] != 0, got, 0.0) if kind == 2 else got

    groups = ("c", "am", "b", "ar")
    sides = [jnp.concatenate([unit(g, e, c) for g in groups for e in range(CHUNKS)], axis=0).T for c in range(CHUNKS)]
    placed = turned_back(jnp.concatenate(sides, axis=0))
    for g in range(len(groups)):
        out_ref[lax.rem(g + 2 * where_ref[0], 4)] = placed[g * SHARE:(g + 1) * SHARE]


def final_tiles(early_at, late_at, where, got):
    return pl.pallas_call(
        functools.partial(final_kernel, early_at, late_at),
        in_specs=[IN_SMEM, IN_VMEM],
        out_specs=IN_VMEM,
        out_shape=jax.ShapeDtypeStruct((4, SHARE, PB), F32),
        compiler_params=pltpu.CompilerParams(vmem_limit_bytes=VMEM),
        name="final_tiles",
    )(where, whole(got))


def shared_out(parts, onto):
    return [parts[0]] + [
        lax.ppermute(parts[d], "bas", [(j, onto(j, d)) for j in range(GROUP)]) for d in range(1, SIDE)
    ]


def after(x, *others):
    return lax.optimization_barrier((x,) + others)[0]


def body(orbitals, owner_perm, pair_reach):
    me = lax.axis_index("pts")
    chips = PTS // 2
    swap = [(p, p ^ 1) for p in range(PTS)]
    onward = [(2 * z, (2 * z - 2) % PTS) for z in range(chips)] + [(2 * z + 1, (2 * z + 3) % PTS) for z in range(chips)]

    ids = jnp.arange(PTS, dtype=jnp.int32)
    three = jnp.arange(3, dtype=jnp.int32)[:, None]
    first_of = me + (three == 2) - (me % 2) * (three + 1)
    apart = (three == 1).astype(jnp.int32)
    live = (ids == first_of) & (apart < pair_reach[None, :]) & (ids + apart + 1 < PTS)
    flags = jnp.sum(live.astype(jnp.int32), axis=1)
    block = jnp.sum(jnp.where(owner_perm[:, None] == ids[None, :], ids[:, None], 0), axis=0)
    partner = block - 2 + 4 * (block % 2)
    there = (partner >= 0) & (partner < PTS)
    partner = jnp.clip(partner, 0, PTS - 1)
    mine = ids == me
    five = jnp.arange(5, dtype=jnp.int32)[:, None]
    facts = jnp.where(five == 0, block % 2, jnp.where(five == 1, block, jnp.where(five == 2, block ^ 1, partner)))
    facts = jnp.where(five == 4, there.astype(jnp.int32), facts)
    where = jnp.sum(jnp.where(mine, facts, 0), axis=1)
    pick = jnp.where(block == me, 0, jnp.where(block == (me ^ 1), 1, 2))

    other = lax.ppermute(orbitals, "pts", swap)
    (first,) = chunks(orbitals, 0, 1)
    second, mhi, mlo = chunks(after(orbitals, first), 1, 1, True)
    ohi, olo, local = local_units(after(other, second), mhi, mlo)
    sent = [first, second, *chunks(after(orbitals, local), 2, 2)]
    arrived = []
    for c, x in enumerate(sent):
        arrived.append(lax.ppermute(x if c < 2 else after(x, arrived[0]), "pts", onward))

    to_sum = lambda x: lax.all_to_all(x, "bas", 0, 0)
    kinds = [[("c", e, c, 0) for e in range(CHUNKS) for c in range(CHUNKS)]] + [step_units(c) for c in range(CHUNKS)]
    names = [[u[0] for u in k] for k in kinds]
    flat = [u for k in kinds[:EARLY] for u in k]
    per = -(-len(flat) // PTS)
    kind = jnp.array([u[3] for u in flat] + [0] * (per * PTS - len(flat)), jnp.int32).reshape(PTS, per)
    kind = jnp.sum(jnp.where(mine[:, None], kind, 0), axis=0)[None, :]
    source = jnp.where(kind == 0, block[:, None], jnp.where(kind == 1, block[:, None] ^ 1, partner[:, None]))
    source = source * per + jnp.arange(per)[None, :]
    source = jnp.where((kind == 2) & ~there[:, None], -1, source).reshape(-1)

    units = [local]
    parts = [to_sum(units[0])]

    def multiply(c, *first):
        units.append(arrived_units(c, mhi, mlo, ohi, olo, after(arrived[c], units[-1], *first)))

    multiply(0, flags, where, pick, source)
    parts.append(to_sum(units[1]))
    multiply(1, parts[0])
    parts.append(to_sum(units[2]))
    multiply(2, parts[1])
    place = lax.axis_index("bas")
    early = early_tiles(names[:2], flags, [after(x, units[3]) for x in parts[:2]], sum(len(x) for x in names[:2]))
    parts.append(to_sum(after(units[3], early)))
    along = arrived_units(
        3, mhi, mlo, ohi, olo, after(arrived[3], units[3], parts[2]), place=(place // SIDE).astype(jnp.int32)[None]
    )
    early = early_tiles(
        names[2:EARLY], flags, [after(x, along[0]) for x in parts[2:EARLY]], per * PTS, (early,)
    )
    spread = lax.all_to_all(early.reshape(PTS, per, SUB, LANES), "pts", 0, 0).reshape(PTS * per, SUB, LANES)
    along = shared_out(along, lambda j, d: (j // SIDE + d) % SIDE * SIDE + j % SIDE)
    line = along[0] + along[1] + along[2] + along[3]
    onward_parts = [lax.dynamic_index_in_dim(line, (place % SIDE + d) % SIDE, 0, keepdims=False) for d in range(SIDE)]
    terms = shared_out(onward_parts, lambda j, d: j // SIDE * SIDE + (j % SIDE + d) % SIDE)
    slots = [[], [], []]
    late_at = {}
    for u, (name, e, c, owner) in enumerate(kinds[EARLY]):
        late_at[(name, e, c)] = (owner, len(slots[owner]))
        slots[owner].append((u, name))
    size = max(len(x) for x in slots)
    early_at = {u[:3]: (n // per, size + n % per) for n, u in enumerate(flat)}
    got = lax.all_to_all(sendings(slots, flags, pick, source, spread, terms), "pts", 0, 0)
    return final_tiles(early_at, late_at, where, got)[None]


def solution(mesh):
    return jax.shard_map(
        body,
        mesh=mesh,
        in_specs=(P("bas", "pts"), P(), P()),
        out_specs=P("pts", None, "bas", None),
        check_vma=False,
    )
```

```python
import functools

import jax
import jax.numpy as jnp
from jax import lax
from jax.experimental import pallas as pl
from jax.experimental.pallas import tpu as pltpu
from jax.sharding import PartitionSpec as P

PB = 512
SHARE = 32
LANES = 128
SUB = 8
CHUNKS = PB // LANES
GROUP = LANES // SUB
SIDE = 4
PTS = 16
VMEM = 14 * 1024 * 1024
WIDE = 32 * 1024 * 1024
F32 = jnp.float32
BF16 = jnp.bfloat16
NT = (((1,), (1,)), ((), ()))
NN = (((1,), (0,)), ((), ()))


def whole(x):
    return pltpu.with_memory_space_constraint(x, pltpu.VMEM)


def in_hbm(x):
    return pltpu.with_memory_space_constraint(x, pltpu.HBM)


IN_VMEM = pl.BlockSpec(memory_space=pltpu.VMEM)
IN_SMEM = pl.BlockSpec(memory_space=pltpu.SMEM)
FLAG = {"c": 0, "am": 1, "ar": 1, "b": 2}
EARLY = 4


def dot(a, b, dims):
    return lax.dot_general(a, b, dims, preferred_element_type=F32)


def split2(x):
    hi = x.astype(BF16)
    return hi, (x - hi.astype(F32)).astype(BF16)


def row_block(depth, most=768):
    for size in (768, 640, 512, 384, 256, 128):
        if size <= most and depth % size == 0:
            return size
    return depth


ANY = pl.BlockSpec(memory_space=pl.ANY)


def piece(k, rows):
    return pl.ds(pl.multiple_of(k * rows, rows), rows)


class Flow:
    def __init__(self, src, dst, sems, count):
        self.src, self.dst, self.sems, self.count = src, dst, sems, count

    def copy(self, k):
        return pltpu.make_async_copy(self.src(k), self.dst(k), self.sems.at[k])

    def start(self):
        for k in range(self.count):
            self.copy(k).start()

    def wait(self):
        for k in range(self.count):
            self.copy(k).wait()


def by_rows(src, dst, sems, rows, count):
    return Flow(lambda k: src.at[piece(k, rows)], lambda k: dst.at[piece(k, rows)], sems, count)


def by_lanes(src, dst, sems, rows, count):
    return Flow(lambda k: src.at[:, piece(k, rows)], lambda k: dst.at[:, piece(k, rows)], sems, count)


def start_all(flows):
    for k in range(flows[0].count):
        for flow in flows:
            flow.copy(k).start()


def turned(x):
    t = x.T
    return jnp.swapaxes(t.reshape(GROUP, CHUNKS, SUB, t.shape[1]), 0, 1).reshape(t.shape)


def turned_back(t):
    x = jnp.swapaxes(t.reshape(CHUNKS, GROUP, SUB, t.shape[1]), 0, 1).reshape(t.shape)
    return x.T


def chunks_kernel(chunk0, number, count, rows, x_hbm, *refs):
    outs = (len(refs) - 3) // 2
    out_hbm, (x_ref, *out_refs, in_sems, out_sems) = refs[:outs], refs[outs:]
    coming = by_rows(x_hbm, x_ref, in_sems, rows, count)
    going = [
        (by_rows if n < number else by_lanes)(ref, out_hbm[n], out_sems.at[n], rows, count)
        for n, ref in enumerate(out_refs)
    ]
    coming.start()

    @pl.loop(0, count)
    def _(k):
        coming.copy(k).wait()
        at = piece(k, rows)
        t = turned(x_ref[at])
        for n in range(number):
            out_refs[n][at] = t[(chunk0 + n) * LANES:(chunk0 + n + 1) * LANES].T
        if outs > number:
            out_refs[number][:, at], out_refs[number + 1][:, at] = split2(t)
        for flow in going:
            flow.copy(k).start()

    for flow in going:
        flow.wait()


def chunks(x, chunk0, number, with_turned=False):
    depth = x.shape[0]
    rows = row_block(depth)
    count = depth // rows
    kinds = [((depth, LANES), F32)] * number + [((PB, depth), BF16)] * (2 if with_turned else 0)
    return pl.pallas_call(
        functools.partial(chunks_kernel, chunk0, number, count, rows),
        in_specs=[ANY],
        out_specs=[ANY] * len(kinds),
        out_shape=[pltpu.HBM(*kind) for kind in kinds],
        scratch_shapes=[pltpu.VMEM((depth, PB), F32)]
        + [pltpu.VMEM(*kind) for kind in kinds]
        + [pltpu.SemaphoreType.DMA((count,)), pltpu.SemaphoreType.DMA((len(kinds), count))],
        compiler_params=pltpu.CompilerParams(vmem_limit_bytes=WIDE),
        cost_estimate=pl.CostEstimate(
            flops=9 * depth * PB * PB, bytes_accessed=4 * depth * (PB + LANES * number), transcendentals=0
        ),
        name="chunks",
    )(in_hbm(x))


def local_kernel(
    count, rows, o_hbm, mhi_hbm, mlo_hbm, ohi_hbm, olo_hbm, out_ref,
    o_ref, mhi_ref, mlo_ref, ohi_ref, olo_ref, acc_ref, in_sems, out_sems,
):
    coming = [
        by_rows(o_hbm, o_ref, in_sems.at[0], rows, count),
        by_lanes(mhi_hbm, mhi_ref, in_sems.at[1], rows, count),
        by_lanes(mlo_hbm, mlo_ref, in_sems.at[2], rows, count),
    ]
    going = [
        by_lanes(ohi_ref, ohi_hbm, out_sems.at[0], rows, count),
        by_lanes(olo_ref, olo_hbm, out_sems.at[1], rows, count),
    ]
    start_all(coming)
    acc_ref[...] = jnp.zeros_like(acc_ref)

    @pl.loop(0, count)
    def _(k):
        at = piece(k, rows)
        for flow in coming:
            flow.copy(k).wait()
        ohi, olo = split2(turned(o_ref[at]))
        ohi_ref[:, at] = ohi
        olo_ref[:, at] = olo
        mhi = mhi_ref[:, at]
        acc_ref[...] += dot(mhi, ohi, NT) + dot(mhi, olo, NT) + dot(mlo_ref[:, at], ohi, NT)
        for flow in going:
            flow.copy(k).start()

    for e in range(CHUNKS):
        for c in range(CHUNKS):
            put(out_ref, CHUNKS * e + c, acc_ref[e * LANES:(e + 1) * LANES, c * LANES:(c + 1) * LANES])
    for flow in going:
        flow.wait()


def local_units(other, mhi, mlo):
    depth = other.shape[0]
    rows = row_block(depth)
    count = depth // rows
    units = CHUNKS * CHUNKS
    wide = pltpu.VMEM((PB, depth), BF16)
    return pl.pallas_call(
        functools.partial(local_kernel, count, rows),
        in_specs=[ANY] * 3,
        out_specs=[ANY, ANY, pl.BlockSpec((GROUP, units, SUB, LANES))],
        out_shape=[pltpu.HBM((PB, depth), BF16)] * 2 + [pltpu.HBM((GROUP, units, SUB, LANES), F32)],
        scratch_shapes=[
            pltpu.VMEM((depth, PB), F32), wide, wide, wide, wide,
            pltpu.VMEM((PB, PB), F32),
            pltpu.SemaphoreType.DMA((3, count)),
            pltpu.SemaphoreType.DMA((2, count)),
        ],
        compiler_params=pltpu.CompilerParams(vmem_limit_bytes=WIDE),
        cost_estimate=pl.CostEstimate(flops=10 * depth * PB * PB, bytes_accessed=12 * depth * PB, transcendentals=0),
        name="local_units",
    )(in_hbm(other), in_hbm(mhi), in_hbm(mlo))


def put(out_ref, unit, block):
    out_ref[:, unit] = block.reshape(GROUP, SUB, LANES)


IN_VMEM = pl.BlockSpec(memory_space=pltpu.VMEM)
IN_SMEM = pl.BlockSpec(memory_space=pltpu.SMEM)
FLAG = {"c": 0, "am": 1, "ar": 1, "b": 2}
EARLY = 4


def step_units(c):
    units = [("am", e, c, 0) for e in range(CHUNKS)]
    units += [("ar", c, e, 2) for e in range(CHUNKS)]
    units += [("b", e, c, 1) for e in range(c, CHUNKS)]
    units += [("b", c, e, 2) for e in range(c + 1, CHUNKS)]
    return units


def step_kernel(c, count, rows, apart, *refs):
    if apart:
        place_ref, refs = refs[0], refs[1:]
    mhi_hbm, mlo_hbm, ohi_hbm, olo_hbm, r_hbm, refs = *refs[:5], refs[5:]
    outs = SIDE if apart else 1
    out_refs, (hi_ref, lo_ref, r_ref, wide_ref, slim_ref, units_ref, sems) = refs[:outs], refs[outs:]
    left = (CHUNKS - c) * LANES

    def lanes(src, dst, sem, at, base, n):
        return Flow(
            lambda k: src.at[pl.ds(at, n), piece(k, rows)],
            lambda k: dst.at[pl.ds(base, n), piece(k, rows)],
            sem,
            count,
        )

    coming = [
        by_rows(r_hbm, r_ref, sems.at[0], rows, count),
        lanes(mhi_hbm, hi_ref, sems.at[1], 0, 0, PB),
        lanes(ohi_hbm, hi_ref, sems.at[2], PB - left, PB, left),
        lanes(mlo_hbm, lo_ref, sems.at[3], 0, 0, PB),
        lanes(olo_hbm, lo_ref, sems.at[4], PB - left, PB, left),
    ]
    start_all(coming)
    wide_ref[...] = jnp.zeros_like(wide_ref)
    slim_ref[...] = jnp.zeros_like(slim_ref)

    @pl.loop(0, count)
    def _(k):
        at = piece(k, rows)
        for flow in coming:
            flow.copy(k).wait()
        rhi, rlo = split2(r_ref[at])
        wide_ref[...] += dot(hi_ref[:, at], jnp.concatenate([rhi, rlo], axis=1), NN)
        slim_ref[...] += dot(lo_ref[:, at], rhi, NN)

    def block(n):
        rows = slice(n * LANES, (n + 1) * LANES)
        return wide_ref[rows, :LANES] + (wide_ref[rows, LANES:] + slim_ref[rows])

    out_ref = units_ref if apart else out_refs[0]
    for e in range(CHUNKS):
        a = block(e)
        put(out_ref, e, a)
        put(out_ref, CHUNKS + e, a.T)
    for e in range(c, CHUNKS):
        b = block(CHUNKS + e - c)
        put(out_ref, 2 * CHUNKS + e - c, b)
        if e > c:
            put(out_ref, 3 * CHUNKS + e - 2 * c - 1, b.T)
    if apart:
        for d in range(SIDE):
            out_refs[d][...] = units_ref[pl.ds(lax.rem(place_ref[0] + d, SIDE) * SIDE, SIDE)]


def arrived_units(c, mhi, mlo, ohi, olo, r, place=None):
    depth = r.shape[0]
    rows = row_block(mhi.shape[1])
    count = depth // rows
    units = len(step_units(c))
    lines = PB + (CHUNKS - c) * LANES
    apart = place is not None
    whole_units = (GROUP, units, SUB, LANES)
    if apart:
        shapes = [jax.ShapeDtypeStruct((SIDE, units, SUB, LANES), F32)] * SIDE
    else:
        shapes = [pltpu.HBM(whole_units, F32)]
    got = pl.pallas_call(
        functools.partial(step_kernel, c, count, rows, apart),
        in_specs=[IN_SMEM] * apart + [ANY] * 5,
        out_specs=[pl.BlockSpec(shape.shape) for shape in shapes],
        out_shape=shapes,
        scratch_shapes=[
            pltpu.VMEM((lines, depth), BF16),
            pltpu.VMEM((lines, depth), BF16),
            pltpu.VMEM((depth, LANES), F32),
            pltpu.VMEM((lines, 2 * LANES), F32),
            pltpu.VMEM((lines, LANES), F32),
            pltpu.VMEM(whole_units, F32),
            pltpu.SemaphoreType.DMA((5, count)),
        ],
        compiler_params=pltpu.CompilerParams(vmem_limit_bytes=WIDE),
        cost_estimate=pl.CostEstimate(
            flops=6 * depth * lines * LANES, bytes_accessed=4 * depth * (lines + LANES), transcendentals=0
        ),
        name="arrived_units",
    )(*([place] if apart else []), *[in_hbm(x) for x in (mhi, mlo, ohi, olo, r)])
    return got if apart else got[0]


def squares(parts_ref, unit, flag):
    gram = parts_ref[0, unit]
    for n in range(1, GROUP):
        gram = gram + parts_ref[n, unit]
    return jnp.where(flag != 0, gram * gram, 0.0)


def early_kernel(names, kept, flags_ref, *refs):
    part_refs, out_ref = refs[:-1], refs[-1]
    n = 0
    if kept:
        n = part_refs[0].shape[0]
        out_ref[:n] = part_refs[0][...]
        part_refs = part_refs[1:]
    for part_ref, units in zip(part_refs, names):
        for u, name in enumerate(units):
            out_ref[n] = squares(part_ref, u, flags_ref[FLAG[name]])
            n += 1
    for pad in range(n, out_ref.shape[0]):
        out_ref[pad] = jnp.zeros((SUB, LANES), F32)


def early_tiles(names, flags, parts, count, kept=()):
    return pl.pallas_call(
        functools.partial(early_kernel, names, len(kept)),
        in_specs=[IN_SMEM] + [IN_VMEM] * (len(kept) + len(parts)),
        out_specs=IN_VMEM,
        out_shape=pltpu.HBM((count, SUB, LANES), F32),
        compiler_params=pltpu.CompilerParams(vmem_limit_bytes=VMEM),
        name="early_tiles",
    )(flags, *[whole(x) for x in (*kept, *parts)])


def send_kernel(slots, flags_ref, pick_ref, source_ref, spread_ref, *refs):
    term_refs, out_ref, held_ref = refs[:-2], refs[-2], refs[-1]
    size = held_ref.shape[1]
    per = out_ref.shape[1] - size
    for kind, units in enumerate(slots):
        for n, (u, name) in enumerate(units):
            gram = term_refs[0][u]
            for term_ref in term_refs[1:]:
                gram = gram + term_ref[u]
            held_ref[kind, n] = jnp.where(flags_ref[FLAG[name]] != 0, gram * gram, 0.0)
        for n in range(len(units), size):
            held_ref[kind, n] = jnp.zeros((SUB, LANES), F32)

    @pl.loop(0, PTS)
    def _(k):
        out_ref[k, :size] = held_ref[pick_ref[k]]
        for n in range(per):
            at = source_ref[k * per + n]
            out_ref[k, size + n] = jnp.where(at >= 0, spread_ref[jnp.maximum(at, 0)], 0.0)


def sendings(slots, flags, pick, source, spread, terms):
    size = max(len(units) for units in slots)
    per = spread.shape[0] // PTS
    return pl.pallas_call(
        functools.partial(send_kernel, slots),
        in_specs=[IN_SMEM] * 3 + [IN_VMEM] * (1 + len(terms)),
        out_specs=IN_VMEM,
        out_shape=jax.ShapeDtypeStruct((PTS, size + per, SUB, LANES), F32),
        scratch_shapes=[pltpu.VMEM((len(slots), size, SUB, LANES), F32)],
        compiler_params=pltpu.CompilerParams(vmem_limit_bytes=VMEM),
        name="sendings",
    )(flags, pick, source, whole(spread), *[whole(x) for x in terms])


def final_kernel(early_at, late_at, where_ref, got_ref, out_ref):
    def unit(name, e, c):
        if (name, e, c) in early_at:
            return got_ref[early_at[(name, e, c)]]
        kind, slot = late_at[(name, e, c)]
        got = got_ref[where_ref[1 + kind], slot]
        return jnp.where(where_ref[4] != 0, got, 0.0) if kind == 2 else got

    groups = ("c", "am", "b", "ar")
    sides = [jnp.concatenate([unit(g, e, c) for g in groups for e in range(CHUNKS)], axis=0).T for c in range(CHUNKS)]
    placed = turned_back(jnp.concatenate(sides, axis=0))
    for g in range(len(groups)):
        out_ref[lax.rem(g + 2 * where_ref[0], 4)] = placed[g * SHARE:(g + 1) * SHARE]


def final_tiles(early_at, late_at, where, got):
    return pl.pallas_call(
        functools.partial(final_kernel, early_at, late_at),
        in_specs=[IN_SMEM, IN_VMEM],
        out_specs=IN_VMEM,
        out_shape=jax.ShapeDtypeStruct((4, SHARE, PB), F32),
        compiler_params=pltpu.CompilerParams(vmem_limit_bytes=VMEM),
        name="final_tiles",
    )(where, whole(got))


def shared_out(parts, onto):
    return [parts[0]] + [
        lax.ppermute(parts[d], "bas", [(j, onto(j, d)) for j in range(GROUP)]) for d in range(1, SIDE)
    ]


def after(x, *others):
    return lax.optimization_barrier((x,) + others)[0]


def body(orbitals, owner_perm, pair_reach):
    me = lax.axis_index("pts")
    chips = PTS // 2
    swap = [(p, p ^ 1) for p in range(PTS)]
    onward = [(2 * z, (2 * z - 2) % PTS) for z in range(chips)] + [(2 * z + 1, (2 * z + 3) % PTS) for z in range(chips)]

    ids = jnp.arange(PTS, dtype=jnp.int32)
    three = jnp.arange(3, dtype=jnp.int32)[:, None]
    first_of = me + (three == 2) - (me % 2) * (three + 1)
    apart = (three == 1).astype(jnp.int32)
    live = (ids == first_of) & (apart < pair_reach[None, :]) & (ids + apart + 1 < PTS)
    flags = jnp.sum(live.astype(jnp.int32), axis=1)
    block = jnp.sum(jnp.where(owner_perm[:, None] == ids[None, :], ids[:, None], 0), axis=0)
    partner = block - 2 + 4 * (block % 2)
    there = (partner >= 0) & (partner < PTS)
    partner = jnp.clip(partner, 0, PTS - 1)
    mine = ids == me
    five = jnp.arange(5, dtype=jnp.int32)[:, None]
    facts = jnp.where(five == 0, block % 2, jnp.where(five == 1, block, jnp.where(five == 2, block ^ 1, partner)))
    facts = jnp.where(five == 4, there.astype(jnp.int32), facts)
    where = jnp.sum(jnp.where(mine, facts, 0), axis=1)
    pick = jnp.where(block == me, 0, jnp.where(block == (me ^ 1), 1, 2))

    other = lax.ppermute(orbitals, "pts", swap)
    (first,) = chunks(orbitals, 0, 1)
    *others, mhi, mlo = chunks(after(orbitals, first), 1, CHUNKS - 1, True)
    ohi, olo, local = local_units(after(other, others[0]), mhi, mlo)
    sent = [first, *others]
    arrived = []
    for c, x in enumerate(sent):
        arrived.append(lax.ppermute(x if c < 2 else after(x, arrived[0]), "pts", onward))

    to_sum = lambda x: lax.all_to_all(x, "bas", 0, 0)
    kinds = [[("c", e, c, 0) for e in range(CHUNKS) for c in range(CHUNKS)]] + [step_units(c) for c in range(CHUNKS)]
    names = [[u[0] for u in k] for k in kinds]
    flat = [u for k in kinds[:EARLY] for u in k]
    per = -(-len(flat) // PTS)
    kind = jnp.array([u[3] for u in flat] + [0] * (per * PTS - len(flat)), jnp.int32).reshape(PTS, per)
    kind = jnp.sum(jnp.where(mine[:, None], kind, 0), axis=0)[None, :]
    source = jnp.where(kind == 0, block[:, None], jnp.where(kind == 1, block[:, None] ^ 1, partner[:, None]))
    source = source * per + jnp.arange(per)[None, :]
    source = jnp.where((kind == 2) & ~there[:, None], -1, source).reshape(-1)

    units = [local]
    parts = [to_sum(units[0])]

    def multiply(c, *first):
        units.append(arrived_units(c, mhi, mlo, ohi, olo, after(arrived[c], units[-1], *first)))

    multiply(0, flags, where, pick, source)
    parts.append(to_sum(units[1]))
    multiply(1, parts[0])
    parts.append(to_sum(units[2]))
    multiply(2, parts[1])
    place = lax.axis_index("bas")
    early = early_tiles(names[:2], flags, [after(x, units[3]) for x in parts[:2]], sum(len(x) for x in names[:2]))
    parts.append(to_sum(after(units[3], early)))
    along = arrived_units(
        3, mhi, mlo, ohi, olo, after(arrived[3], units[3], parts[2]), place=(place // SIDE).astype(jnp.int32)[None]
    )
    early = early_tiles(
        names[2:EARLY], flags, [after(x, along[0]) for x in parts[2:EARLY]], per * PTS, (early,)
    )
    spread = lax.all_to_all(early.reshape(PTS, per, SUB, LANES), "pts", 0, 0).reshape(PTS * per, SUB, LANES)
    along = shared_out(along, lambda j, d: (j // SIDE + d) % SIDE * SIDE + j % SIDE)
    line = along[0] + along[1] + along[2] + along[3]
    onward_parts = [lax.dynamic_index_in_dim(line, (place % SIDE + d) % SIDE, 0, keepdims=False) for d in range(SIDE)]
    terms = shared_out(onward_parts, lambda j, d: j // SIDE * SIDE + (j % SIDE + d) % SIDE)
    slots = [[], [], []]
    late_at = {}
    for u, (name, e, c, owner) in enumerate(kinds[EARLY]):
        late_at[(name, e, c)] = (owner, len(slots[owner]))
        slots[owner].append((u, name))
    size = max(len(x) for x in slots)
    early_at = {u[:3]: (n // per, size + n % per) for n, u in enumerate(flat)}
    got = lax.all_to_all(sendings(slots, flags, pick, source, spread, terms), "pts", 0, 0)
    return final_tiles(early_at, late_at, where, got)[None]


def solution(mesh):
    return jax.shard_map(
        body,
        mesh=mesh,
        in_specs=(P("bas", "pts"), P(), P()),
        out_specs=P("pts", None, "bas", None),
        check_vma=False,
    )
```

```python
import functools

import jax
import jax.numpy as jnp
from jax import lax
from jax.experimental import pallas as pl
from jax.experimental.pallas import tpu as pltpu
from jax.sharding import PartitionSpec as P

PB = 512
SHARE = 32
LANES = 128
SUB = 8
CHUNKS = PB // LANES
GROUP = LANES // SUB
SIDE = 4
PTS = 16
VMEM = 14 * 1024 * 1024
WIDE = 32 * 1024 * 1024
F32 = jnp.float32
BF16 = jnp.bfloat16
NT = (((1,), (1,)), ((), ()))
NN = (((1,), (0,)), ((), ()))


def whole(x):
    return pltpu.with_memory_space_constraint(x, pltpu.VMEM)


def in_hbm(x):
    return pltpu.with_memory_space_constraint(x, pltpu.HBM)


IN_VMEM = pl.BlockSpec(memory_space=pltpu.VMEM)
IN_SMEM = pl.BlockSpec(memory_space=pltpu.SMEM)
FLAG = {"c": 0, "am": 1, "ar": 1, "b": 2}
EARLY = 4


def dot(a, b, dims):
    return lax.dot_general(a, b, dims, preferred_element_type=F32)


def split2(x):
    hi = x.astype(BF16)
    return hi, (x - hi.astype(F32)).astype(BF16)


def row_block(depth, most=768):
    for size in (768, 640, 512, 384, 256, 128):
        if size <= most and depth % size == 0:
            return size
    return depth


ANY = pl.BlockSpec(memory_space=pl.ANY)


def piece(k, rows):
    return pl.ds(pl.multiple_of(k * rows, rows), rows)


class Flow:
    def __init__(self, src, dst, sems, count):
        self.src, self.dst, self.sems, self.count = src, dst, sems, count

    def copy(self, k):
        return pltpu.make_async_copy(self.src(k), self.dst(k), self.sems.at[k])

    def start(self):
        for k in range(self.count):
            self.copy(k).start()

    def wait(self):
        for k in range(self.count):
            self.copy(k).wait()


def by_rows(src, dst, sems, rows, count):
    return Flow(lambda k: src.at[piece(k, rows)], lambda k: dst.at[piece(k, rows)], sems, count)


def by_lanes(src, dst, sems, rows, count):
    return Flow(lambda k: src.at[:, piece(k, rows)], lambda k: dst.at[:, piece(k, rows)], sems, count)


def start_all(flows):
    for k in range(flows[0].count):
        for flow in flows:
            flow.copy(k).start()


def turned(x):
    t = x.T
    return jnp.swapaxes(t.reshape(GROUP, CHUNKS, SUB, t.shape[1]), 0, 1).reshape(t.shape)


def turned_back(t):
    x = jnp.swapaxes(t.reshape(CHUNKS, GROUP, SUB, t.shape[1]), 0, 1).reshape(t.shape)
    return x.T


def chunks_kernel(chunk0, number, count, rows, x_hbm, *refs):
    outs = (len(refs) - 3) // 2
    out_hbm, (x_ref, *out_refs, in_sems, out_sems) = refs[:outs], refs[outs:]
    coming = by_rows(x_hbm, x_ref, in_sems, rows, count)
    going = [
        (by_rows if n < number else by_lanes)(ref, out_hbm[n], out_sems.at[n], rows, count)
        for n, ref in enumerate(out_refs)
    ]
    coming.start()

    @pl.loop(0, count)
    def _(k):
        coming.copy(k).wait()
        at = piece(k, rows)
        t = turned(x_ref[at])
        for n in range(number):
            out_refs[n][at] = t[(chunk0 + n) * LANES:(chunk0 + n + 1) * LANES].T
        if outs > number:
            out_refs[number][:, at], out_refs[number + 1][:, at] = split2(t)
        for flow in going:
            flow.copy(k).start()

    for flow in going:
        flow.wait()


def chunks(x, chunk0, number, with_turned=False):
    depth = x.shape[0]
    rows = row_block(depth)
    count = depth // rows
    kinds = [((depth, LANES), F32)] * number + [((PB, depth), BF16)] * (2 if with_turned else 0)
    return pl.pallas_call(
        functools.partial(chunks_kernel, chunk0, number, count, rows),
        in_specs=[ANY],
        out_specs=[ANY] * len(kinds),
        out_shape=[pltpu.HBM(*kind) for kind in kinds],
        scratch_shapes=[pltpu.VMEM((depth, PB), F32)]
        + [pltpu.VMEM(*kind) for kind in kinds]
        + [pltpu.SemaphoreType.DMA((count,)), pltpu.SemaphoreType.DMA((len(kinds), count))],
        compiler_params=pltpu.CompilerParams(vmem_limit_bytes=WIDE),
        cost_estimate=pl.CostEstimate(
            flops=9 * depth * PB * PB, bytes_accessed=4 * depth * (PB + LANES * number), transcendentals=0
        ),
        name="chunks",
    )(in_hbm(x))


def local_kernel(
    count, rows, o_hbm, mhi_hbm, mlo_hbm, ohi_hbm, olo_hbm, out_ref,
    o_ref, mhi_ref, mlo_ref, ohi_ref, olo_ref, acc_ref, in_sems, out_sems,
):
    coming = [
        by_rows(o_hbm, o_ref, in_sems.at[0], rows, count),
        by_lanes(mhi_hbm, mhi_ref, in_sems.at[1], rows, count),
        by_lanes(mlo_hbm, mlo_ref, in_sems.at[2], rows, count),
    ]
    going = [
        by_lanes(ohi_ref, ohi_hbm, out_sems.at[0], rows, count),
        by_lanes(olo_ref, olo_hbm, out_sems.at[1], rows, count),
    ]
    start_all(coming)
    acc_ref[...] = jnp.zeros_like(acc_ref)

    @pl.loop(0, count)
    def _(k):
        at = piece(k, rows)
        for flow in coming:
            flow.copy(k).wait()
        ohi, olo = split2(turned(o_ref[at]))
        ohi_ref[:, at] = ohi
        olo_ref[:, at] = olo
        mhi = mhi_ref[:, at]
        acc_ref[...] += dot(mhi, ohi, NT) + dot(mhi, olo, NT) + dot(mlo_ref[:, at], ohi, NT)
        for flow in going:
            flow.copy(k).start()

    for e in range(CHUNKS):
        for c in range(CHUNKS):
            put(out_ref, CHUNKS * e + c, acc_ref[e * LANES:(e + 1) * LANES, c * LANES:(c + 1) * LANES])
    for flow in going:
        flow.wait()


def local_units(other, mhi, mlo):
    depth = other.shape[0]
    rows = row_block(depth)
    count = depth // rows
    units = CHUNKS * CHUNKS
    wide = pltpu.VMEM((PB, depth), BF16)
    return pl.pallas_call(
        functools.partial(local_kernel, count, rows),
        in_specs=[ANY] * 3,
        out_specs=[ANY, ANY, pl.BlockSpec((GROUP, units, SUB, LANES))],
        out_shape=[pltpu.HBM((PB, depth), BF16)] * 2 + [pltpu.HBM((GROUP, units, SUB, LANES), F32)],
        scratch_shapes=[
            pltpu.VMEM((depth, PB), F32), wide, wide, wide, wide,
            pltpu.VMEM((PB, PB), F32),
            pltpu.SemaphoreType.DMA((3, count)),
            pltpu.SemaphoreType.DMA((2, count)),
        ],
        compiler_params=pltpu.CompilerParams(vmem_limit_bytes=WIDE),
        cost_estimate=pl.CostEstimate(flops=10 * depth * PB * PB, bytes_accessed=12 * depth * PB, transcendentals=0),
        name="local_units",
    )(in_hbm(other), in_hbm(mhi), in_hbm(mlo))


def put(out_ref, unit, block):
    out_ref[:, unit] = block.reshape(GROUP, SUB, LANES)


IN_VMEM = pl.BlockSpec(memory_space=pltpu.VMEM)
IN_SMEM = pl.BlockSpec(memory_space=pltpu.SMEM)
FLAG = {"c": 0, "am": 1, "ar": 1, "b": 2}
EARLY = 4


def step_units(c):
    units = [("am", e, c, 0) for e in range(CHUNKS)]
    units += [("ar", c, e, 2) for e in range(CHUNKS)]
    units += [("b", e, c, 1) for e in range(c, CHUNKS)]
    units += [("b", c, e, 2) for e in range(c + 1, CHUNKS)]
    return units


def step_kernel(c, count, rows, apart, *refs):
    if apart:
        place_ref, refs = refs[0], refs[1:]
    mhi_hbm, mlo_hbm, ohi_hbm, olo_hbm, r_hbm, refs = *refs[:5], refs[5:]
    outs = SIDE if apart else 1
    out_refs, (hi_ref, lo_ref, r_ref, wide_ref, slim_ref, units_ref, sems) = refs[:outs], refs[outs:]
    left = (CHUNKS - c) * LANES

    def lanes(src, dst, sem, at, base, n):
        return Flow(
            lambda k: src.at[pl.ds(at, n), piece(k, rows)],
            lambda k: dst.at[pl.ds(base, n), piece(k, rows)],
            sem,
            count,
        )

    coming = [
        by_rows(r_hbm, r_ref, sems.at[0], rows, count),
        lanes(mhi_hbm, hi_ref, sems.at[1], 0, 0, PB),
        lanes(ohi_hbm, hi_ref, sems.at[2], PB - left, PB, left),
        lanes(mlo_hbm, lo_ref, sems.at[3], 0, 0, PB),
        lanes(olo_hbm, lo_ref, sems.at[4], PB - left, PB, left),
    ]
    start_all(coming)
    wide_ref[...] = jnp.zeros_like(wide_ref)
    slim_ref[...] = jnp.zeros_like(slim_ref)

    @pl.loop(0, count)
    def _(k):
        at = piece(k, rows)
        for flow in coming:
            flow.copy(k).wait()
        rhi, rlo = split2(r_ref[at])
        wide_ref[...] += dot(hi_ref[:, at], jnp.concatenate([rhi, rlo], axis=1), NN)
        slim_ref[...] += dot(lo_ref[:, at], rhi, NN)

    def block(n):
        rows = slice(n * LANES, (n + 1) * LANES)
        return wide_ref[rows, :LANES] + (wide_ref[rows, LANES:] + slim_ref[rows])

    out_ref = units_ref if apart else out_refs[0]
    for e in range(CHUNKS):
        a = block(e)
        put(out_ref, e, a)
        put(out_ref, CHUNKS + e, a.T)
    for e in range(c, CHUNKS):
        b = block(CHUNKS + e - c)
        put(out_ref, 2 * CHUNKS + e - c, b)
        if e > c:
            put(out_ref, 3 * CHUNKS + e - 2 * c - 1, b.T)
    if apart:
        for d in range(SIDE):
            out_refs[d][...] = units_ref[pl.ds(lax.rem(place_ref[0] + d, SIDE) * SIDE, SIDE)]


def arrived_units(c, mhi, mlo, ohi, olo, r, place=None):
    depth = r.shape[0]
    rows = row_block(mhi.shape[1])
    count = depth // rows
    units = len(step_units(c))
    lines = PB + (CHUNKS - c) * LANES
    apart = place is not None
    whole_units = (GROUP, units, SUB, LANES)
    if apart:
        shapes = [jax.ShapeDtypeStruct((SIDE, units, SUB, LANES), F32)] * SIDE
    else:
        shapes = [pltpu.HBM(whole_units, F32)]
    got = pl.pallas_call(
        functools.partial(step_kernel, c, count, rows, apart),
        in_specs=[IN_SMEM] * apart + [ANY] * 5,
        out_specs=[pl.BlockSpec(shape.shape) for shape in shapes],
        out_shape=shapes,
        scratch_shapes=[
            pltpu.VMEM((lines, depth), BF16),
            pltpu.VMEM((lines, depth), BF16),
            pltpu.VMEM((depth, LANES), F32),
            pltpu.VMEM((lines, 2 * LANES), F32),
            pltpu.VMEM((lines, LANES), F32),
            pltpu.VMEM(whole_units, F32),
            pltpu.SemaphoreType.DMA((5, count)),
        ],
        compiler_params=pltpu.CompilerParams(vmem_limit_bytes=WIDE),
        cost_estimate=pl.CostEstimate(
            flops=6 * depth * lines * LANES, bytes_accessed=4 * depth * (lines + LANES), transcendentals=0
        ),
        name="arrived_units",
    )(*([place] if apart else []), *[in_hbm(x) for x in (mhi, mlo, ohi, olo, r)])
    return got if apart else got[0]


def squares(parts_ref, unit, flag):
    gram = parts_ref[0, unit]
    for n in range(1, GROUP):
        gram = gram + parts_ref[n, unit]
    return jnp.where(flag != 0, gram * gram, 0.0)


def early_kernel(names, kept, flags_ref, *refs):
    part_refs, out_ref = refs[:-1], refs[-1]
    n = 0
    if kept:
        n = part_refs[0].shape[0]
        out_ref[:n] = part_refs[0][...]
        part_refs = part_refs[1:]
    for part_ref, units in zip(part_refs, names):
        for u, name in enumerate(units):
            out_ref[n] = squares(part_ref, u, flags_ref[FLAG[name]])
            n += 1
    for pad in range(n, out_ref.shape[0]):
        out_ref[pad] = jnp.zeros((SUB, LANES), F32)


def early_tiles(names, flags, parts, count, kept=()):
    return pl.pallas_call(
        functools.partial(early_kernel, names, len(kept)),
        in_specs=[IN_SMEM] + [IN_VMEM] * (len(kept) + len(parts)),
        out_specs=IN_VMEM,
        out_shape=pltpu.HBM((count, SUB, LANES), F32),
        compiler_params=pltpu.CompilerParams(vmem_limit_bytes=VMEM),
        name="early_tiles",
    )(flags, *[whole(x) for x in (*kept, *parts)])


def send_kernel(slots, flags_ref, pick_ref, source_ref, spread_ref, *refs):
    term_refs, out_ref, held_ref = refs[:-2], refs[-2], refs[-1]
    size = held_ref.shape[1]
    per = out_ref.shape[1] - size
    for kind, units in enumerate(slots):
        for n, (u, name) in enumerate(units):
            gram = term_refs[0][u]
            for term_ref in term_refs[1:]:
                gram = gram + term_ref[u]
            held_ref[kind, n] = jnp.where(flags_ref[FLAG[name]] != 0, gram * gram, 0.0)
        for n in range(len(units), size):
            held_ref[kind, n] = jnp.zeros((SUB, LANES), F32)

    @pl.loop(0, PTS)
    def _(k):
        out_ref[k, :size] = held_ref[pick_ref[k]]
        for n in range(per):
            at = source_ref[k * per + n]
            out_ref[k, size + n] = jnp.where(at >= 0, spread_ref[jnp.maximum(at, 0)], 0.0)


def sendings(slots, flags, pick, source, spread, terms):
    size = max(len(units) for units in slots)
    per = spread.shape[0] // PTS
    return pl.pallas_call(
        functools.partial(send_kernel, slots),
        in_specs=[IN_SMEM] * 3 + [IN_VMEM] * (1 + len(terms)),
        out_specs=IN_VMEM,
        out_shape=jax.ShapeDtypeStruct((PTS, size + per, SUB, LANES), F32),
        scratch_shapes=[pltpu.VMEM((len(slots), size, SUB, LANES), F32)],
        compiler_params=pltpu.CompilerParams(vmem_limit_bytes=VMEM),
        name="sendings",
    )(flags, pick, source, whole(spread), *[whole(x) for x in terms])


def final_kernel(early_at, late_at, where_ref, got_ref, out_ref):
    def unit(name, e, c):
        if (name, e, c) in early_at:
            return got_ref[early_at[(name, e, c)]]
        kind, slot = late_at[(name, e, c)]
        got = got_ref[where_ref[1 + kind], slot]
        return jnp.where(where_ref[4] != 0, got, 0.0) if kind == 2 else got

    groups = ("c", "am", "b", "ar")
    sides = [jnp.concatenate([unit(g, e, c) for g in groups for e in range(CHUNKS)], axis=0).T for c in range(CHUNKS)]
    placed = turned_back(jnp.concatenate(sides, axis=0))
    for g in range(len(groups)):
        out_ref[lax.rem(g + 2 * where_ref[0], 4)] = placed[g * SHARE:(g + 1) * SHARE]


def final_tiles(early_at, late_at, where, got):
    return pl.pallas_call(
        functools.partial(final_kernel, early_at, late_at),
        in_specs=[IN_SMEM, IN_VMEM],
        out_specs=IN_VMEM,
        out_shape=jax.ShapeDtypeStruct((4, SHARE, PB), F32),
        compiler_params=pltpu.CompilerParams(vmem_limit_bytes=VMEM),
        name="final_tiles",
    )(where, whole(got))


def shared_out(parts, onto):
    return [parts[0]] + [
        lax.ppermute(parts[d], "bas", [(j, onto(j, d)) for j in range(GROUP)]) for d in range(1, SIDE)
    ]


def after(x, *others):
    return lax.optimization_barrier((x,) + others)[0]


def body(orbitals, owner_perm, pair_reach):
    me = lax.axis_index("pts")
    chips = PTS // 2
    swap = [(p, p ^ 1) for p in range(PTS)]
    onward = [(2 * z, (2 * z - 2) % PTS) for z in range(chips)] + [(2 * z + 1, (2 * z + 3) % PTS) for z in range(chips)]

    ids = jnp.arange(PTS, dtype=jnp.int32)
    three = jnp.arange(3, dtype=jnp.int32)[:, None]
    first_of = me + (three == 2) - (me % 2) * (three + 1)
    apart = (three == 1).astype(jnp.int32)
    live = (ids == first_of) & (apart < pair_reach[None, :]) & (ids + apart + 1 < PTS)
    flags = jnp.sum(live.astype(jnp.int32), axis=1)
    block = jnp.sum(jnp.where(owner_perm[:, None] == ids[None, :], ids[:, None], 0), axis=0)
    partner = block - 2 + 4 * (block % 2)
    there = (partner >= 0) & (partner < PTS)
    partner = jnp.clip(partner, 0, PTS - 1)
    mine = ids == me
    five = jnp.arange(5, dtype=jnp.int32)[:, None]
    facts = jnp.where(five == 0, block % 2, jnp.where(five == 1, block, jnp.where(five == 2, block ^ 1, partner)))
    facts = jnp.where(five == 4, there.astype(jnp.int32), facts)
    where = jnp.sum(jnp.where(mine, facts, 0), axis=1)
    pick = jnp.where(block == me, 0, jnp.where(block == (me ^ 1), 1, 2))

    other = lax.ppermute(orbitals, "pts", swap)
    (first,) = chunks(orbitals, 0, 1)
    *others, mhi, mlo = chunks(after(orbitals, first), 1, CHUNKS - 1, True)
    ohi, olo, local = local_units(after(other, others[0]), mhi, mlo)
    sent = [first, *others]
    arrived = []
    for c, x in enumerate(sent):
        arrived.append(lax.ppermute(x if c < 2 else after(x, arrived[0]), "pts", onward))

    to_sum = lambda x: lax.all_to_all(x, "bas", 0, 0)
    kinds = [[("c", e, c, 0) for e in range(CHUNKS) for c in range(CHUNKS)]] + [step_units(c) for c in range(CHUNKS)]
    names = [[u[0] for u in k] for k in kinds]
    flat = [u for k in kinds[:EARLY] for u in k]
    per = -(-len(flat) // PTS)
    kind = jnp.array([u[3] for u in flat] + [0] * (per * PTS - len(flat)), jnp.int32).reshape(PTS, per)
    kind = jnp.sum(jnp.where(mine[:, None], kind, 0), axis=0)[None, :]
    source = jnp.where(kind == 0, block[:, None], jnp.where(kind == 1, block[:, None] ^ 1, partner[:, None]))
    source = source * per + jnp.arange(per)[None, :]
    source = jnp.where((kind == 2) & ~there[:, None], -1, source).reshape(-1)

    units = [local]
    parts = [to_sum(units[0])]

    def multiply(c, *first):
        units.append(arrived_units(c, mhi, mlo, ohi, olo, after(arrived[c], units[-1], *first)))

    multiply(0, flags, where, pick, source)
    parts.append(to_sum(units[1]))
    multiply(1, parts[0])
    parts.append(to_sum(units[2]))
    multiply(2, parts[1])
    place = lax.axis_index("bas")
    early = early_tiles(names[:2], flags, [after(x, units[3]) for x in parts[:2]], sum(len(x) for x in names[:2]))
    parts.append(to_sum(after(units[3], early)))
    early = early_tiles(names[2:3], flags, parts[2:3], sum(len(x) for x in names[:3]), (early,))
    along = arrived_units(
        3, mhi, mlo, ohi, olo, after(arrived[3], units[3], early), place=(place // SIDE).astype(jnp.int32)[None]
    )
    early = early_tiles(
        names[3:EARLY], flags, [after(x, along[0]) for x in parts[3:EARLY]], per * PTS, (early,)
    )
    spread = lax.all_to_all(early.reshape(PTS, per, SUB, LANES), "pts", 0, 0).reshape(PTS * per, SUB, LANES)
    along = shared_out(along, lambda j, d: (j // SIDE + d) % SIDE * SIDE + j % SIDE)
    line = along[0] + along[1] + along[2] + along[3]
    onward_parts = [lax.dynamic_index_in_dim(line, (place % SIDE + d) % SIDE, 0, keepdims=False) for d in range(SIDE)]
    terms = shared_out(onward_parts, lambda j, d: j // SIDE * SIDE + (j % SIDE + d) % SIDE)
    slots = [[], [], []]
    late_at = {}
    for u, (name, e, c, owner) in enumerate(kinds[EARLY]):
        late_at[(name, e, c)] = (owner, len(slots[owner]))
        slots[owner].append((u, name))
    size = max(len(x) for x in slots)
    early_at = {u[:3]: (n // per, size + n % per) for n, u in enumerate(flat)}
    got = lax.all_to_all(sendings(slots, flags, pick, source, spread, terms), "pts", 0, 0)
    return final_tiles(early_at, late_at, where, got)[None]


def solution(mesh):
    return jax.shard_map(
        body,
        mesh=mesh,
        in_specs=(P("bas", "pts"), P(), P()),
        out_specs=P("pts", None, "bas", None),
        check_vma=False,
    )
```
